512 devices in a mesh: seq: 8 (over x, core), dp: 64 (over y, z).
Axes of the slice: x: 4, y: 8, z: 8, core: 2. Of those that a mesh axis runs over, the one named last changes fastest.
Arguments:
- hidden: bfloat16 [64, 1024, 4096], P('dp', 'seq'), may hold values from -16 to 16
- query: bfloat16 [64, 1024, 4096], P('dp', 'seq'), may hold values from -5 to 5
- key: bfloat16 [64, 1024, 1024], P('dp', 'seq'), may hold values from -5 to 5
- grad_out: bfloat16 [64, 1024, 4096], P('dp', 'seq'), may hold values from -6 to 6
- doc_lens: int32 [64, 8], P('dp'), may hold values from 1 to 384, 1024 in all within a row
- master: float32 [4096, 1024], P('dp', 'seq'), may hold values from -6 to 6
- m_code: bfloat16 [4096, 1024], P('dp', 'seq'), may hold values from -1 to 1
- m_scale: float32 [2048, 8], P('dp', 'seq'), may hold values from 0.02 to 0.2
- v_code: bfloat16 [4096, 1024], P('dp', 'seq'), may hold values from 0.049804688 to 1
- v_scale: float32 [2048, 8], P('dp', 'seq'), may hold values from 0.5 to 5
Outputs:
- grad_query: bfloat16 [64, 1024, 4096], P('dp', 'seq')
- grad_key: bfloat16 [64, 1024, 1024], P('dp', 'seq')
- new_master: float32 [4096, 1024], P('dp', 'seq')
- new_m_code: bfloat16 [4096, 1024], P('dp', 'seq')
- new_m_scale: float32 [2048, 8], P('dp', 'seq')
- new_v_code: bfloat16 [4096, 1024], P('dp', 'seq')
- new_v_scale: float32 [2048, 8], P('dp', 'seq')
The draws below stay inside these ranges and needn't reach their ends.
Inputs may be any that keep to these rules, and one draw needn't show every extreme that they name: `doc_lens`: row g lists the lengths of the documents packed in order into sequence g; they sum to 1024 and the largest is exactly 384.
All inputs are finite; a program needn't handle non-finite values. Where the reference program divides by a largest or mean magnitude, that divisor is 1e-20 or more.
Results may differ from the reference program's by a relative error of at most 0.027.
Values may be sent and summed in bfloat16 or wider, within the bound.
No kernel may reach another device: no remote copies, remote signals or barrier semaphores. Data moves between devices by JAX's collectives and lax.ppermute only.
A program may use at most 128 MiB of HBM per device.

```python
import math
import jax
import jax.numpy as jnp
import numpy as np
from jax import lax

D = 4096
QH = 32
KV = 8
HD = 128
DOCS = 8
STEP = 1000
SEQ = 1024
MOST_DOC = 384
N_DP = 64


def query_key_pair(key):
    shape_k = (N_DP, SEQ, KV * HD)
    shape_q = (N_DP, SEQ, QH * HD)
    keys_drawn = jnp.clip(jax.random.normal(jax.random.fold_in(key, 21), shape_k, jnp.float32), -5.0, 5.0)
    queries_drawn = jnp.clip(jax.random.normal(jax.random.fold_in(key, 22), shape_q, jnp.float32), -5.0, 5.0)
    return (queries_drawn, keys_drawn)


def draw_query(key, part):
    queries_drawn, keys_drawn = query_key_pair(key)
    return queries_drawn.astype(jnp.bfloat16)


def draw_key(key, part):
    queries_drawn, keys_drawn = query_key_pair(key)
    return keys_drawn.astype(jnp.bfloat16)


def with_spikes(drawn, key, source, target, parts, factor):
    owner, partner = [(jnp.arange(drawn.shape[dim]) // (drawn.shape[dim] // parts)).reshape([-1 if axis == dim else 1 for axis in range(drawn.ndim)]) for dim in (source, target)]
    chosen = jax.random.permutation(key, parts)[partner]
    strong = (owner == chosen) | (owner == (partner + parts // 2) % parts)
    return jnp.where(strong, factor * drawn, drawn)


def levels(own_key, dims, pieces, least, high):
    level, own = 1.0, jax.random.fold_in(own_key, 6)
    for dim, blocks in pieces:
        steps = jnp.exp(jax.random.uniform(jax.random.fold_in(own, dim), (blocks,), jnp.float32, least / len(pieces), high / len(pieces)))
        level = level * jnp.repeat(steps, dims[dim] // blocks).reshape([-1 if axis == dim else 1 for axis in range(len(dims))])
    return level


def profile(count, total, bound, slope):
    portions = [(1 << 20) // math.isqrt(grade ** slope) + 1 for grade in range(2, count + 1)]
    spare, given = total - bound - (count - 1), [1] * (count - 1)
    while spare > 0:
        candidates = [i for i in range(count - 1) if given[i] < bound]
        mass, budget = sum([portions[i] for i in candidates]), spare
        for i in candidates:
            addition = min(bound - given[i], max(1, budget * portions[i] // mass), spare)
            given[i] = given[i] + addition
            spare = spare - addition
    return np.array([bound] + given)


def ragged(rng, number_of, total, bound, slope):
    if number_of == 2:
        one = jax.random.randint(rng, (), max(1, total - bound), min(bound, total - 1) + 1)
        return jnp.stack([one, total - one])
    sizes = jnp.asarray(profile(number_of, total, bound, slope), jnp.int32)
    pairs = (number_of - 1) // 2
    giver, receiver = sizes[1:1 + 2 * pairs:2], sizes[2:2 + 2 * pairs:2]
    room = jnp.minimum(giver - 1, bound - receiver)
    moved = jax.random.randint(jax.random.fold_in(rng, 1), (pairs,), 0, 1 << 20) % (room + 1)
    sizes = sizes.at[1:1 + 2 * pairs:2].set(giver - moved).at[2:2 + 2 * pairs:2].set(receiver + moved)
    return sizes[jax.random.permutation(jax.random.fold_in(rng, 2), number_of)]


def centred(key, dims, scale, reach, pieces=(), dtype=jnp.bfloat16):
    drawn = scale * jax.random.normal(key, dims, jnp.float32)
    if pieces:
        drawn = drawn * levels(key, dims, pieces, -0.22, 0.18)
    return jnp.clip(drawn, -reach, reach).astype(dtype)


def noise_with(key, dims, scale, reach, shards, heavy, held_as=jnp.bfloat16):
    array = scale * jax.random.normal(key, dims, jnp.float32)
    if shards:
        array = array * levels(key, dims, shards, -0.22, 0.18)
    return jnp.clip(with_spikes(array, jax.random.fold_in(key, 3), *heavy), -reach, reach).astype(held_as)


def setup_inputs(seed: int = 0) -> dict:
    seeds = jax.random.split(jax.random.key(seed), 11)
    return {
        "hidden": noise_with(seeds[0], (N_DP, SEQ, D), 1.0, 16.0, ((0, 64), (1, 8)), (0, 2, 64, 4.0)),
        "query": draw_query(jax.random.fold_in(seeds[10], 71), 0),
        "key": draw_key(jax.random.fold_in(seeds[10], 71), 0),
        "grad_out": centred(seeds[3], (N_DP, SEQ, QH * HD), 1.0, 6.0, ((0, 64), (1, 8))),
        "doc_lens": jax.vmap(lambda own: ragged(own, DOCS, SEQ, MOST_DOC, 2))(jax.random.split(seeds[4], N_DP)).reshape((N_DP, DOCS)).astype(jnp.int32),
        "master": centred(seeds[5], (D, KV * HD), 1.0, 6.0, ((0, 64), (1, 8)), jnp.float32),
        "m_code": jnp.clip(jax.random.uniform(seeds[6], (D, KV * HD), jnp.float32, -1.0, 1.0) * levels(seeds[6], (D, KV * HD), ((0, 64), (1, 8)), -0.4, 0.0), -1.0, 1.0).astype(jnp.bfloat16),
        "m_scale": jnp.clip(jnp.exp(math.log(0.2) - 2.3025851 * jax.random.uniform(seeds[7], (D // 2, KV), jnp.float32) ** levels(seeds[7], (D // 2, KV), ((0, 64), (1, 8)), -0.2, 0.2)), 0.02, 0.2),
        "v_code": jnp.clip(0.049804688 + 0.9501953 * jax.random.uniform(seeds[8], (D, KV * HD), jnp.float32) ** levels(seeds[8], (D, KV * HD), ((0, 64), (1, 8)), -0.2, 0.2), 0.049804688, 1.0).astype(jnp.bfloat16),
        "v_scale": jnp.clip(jnp.exp(math.log(5.0) - 2.3025851 * jax.random.uniform(seeds[9], (D // 2, KV), jnp.float32) ** levels(seeds[9], (D // 2, KV), ((0, 64), (1, 8)), -0.2, 0.2)), 0.5, 5.0),
    }


def doc_tables(lengths):
    ends = jnp.cumsum(lengths)
    position = jnp.arange(SEQ)
    after = position[:, None] >= ends[None, :]
    return lax.optimization_barrier(jnp.sum(after.astype(jnp.int32), axis=1))

def group_terms(hidden_rows, query_rows, key_rows, cot_rows, lengths, weight):
    group_size = QH // KV
    scale = 1.0 / math.sqrt(HD)
    inv_width = 1.0 / math.sqrt(D)
    values = (jnp.dot(hidden_rows, weight, preferred_element_type=jnp.float32) * inv_width).astype(jnp.bfloat16)
    queries = query_rows.astype(jnp.float32).reshape(SEQ, KV, group_size, HD)
    keys_all = key_rows.astype(jnp.float32).reshape(SEQ, KV, HD)
    value_heads = values.astype(jnp.float32).reshape(SEQ, KV, HD)
    cotangent = cot_rows.astype(jnp.float32).reshape(SEQ, KV, group_size, HD)
    doc_ids = doc_tables(lengths)
    position = jnp.arange(SEQ)
    allowed = (position[None, :] <= position[:, None]) & (doc_ids[:, None] == doc_ids[None, :])
    scores = jnp.einsum('qhgd,khd->hgqk', queries, keys_all) * scale
    scores = jnp.where(allowed, scores, -jnp.inf)
    highest = lax.optimization_barrier(jnp.max(scores, axis=3, keepdims=True))
    weights = jnp.exp(scores - highest)
    probabilities = (weights / lax.optimization_barrier(jnp.sum(weights, axis=3, keepdims=True))).astype(jnp.bfloat16)
    prob_back = lax.optimization_barrier(probabilities).astype(jnp.float32)
    attended = jnp.einsum('hgqk,khd->qhgd', prob_back, value_heads).astype(jnp.bfloat16)
    delta = jnp.einsum('qhgd,qhgd->hgq', attended.astype(jnp.float32), cotangent)
    prob_grad = jnp.einsum('qhgd,khd->hgqk', cotangent, value_heads)
    score_grad = (prob_back * (prob_grad - delta[..., None])).astype(jnp.bfloat16).astype(jnp.float32)
    grad_query = (jnp.einsum('hgqk,khd->qhgd', score_grad, keys_all) * scale).astype(jnp.bfloat16)
    grad_key = (jnp.einsum('hgqk,qhgd->khd', score_grad, queries) * scale).astype(jnp.bfloat16)
    grad_values = jnp.einsum('hgqk,qhgd->khd', prob_back, cotangent).astype(jnp.bfloat16)
    grad_values = grad_values.reshape(SEQ, KV * HD)
    term = jnp.dot(hidden_rows.T, grad_values, preferred_element_type=jnp.float32) * inv_width
    return (grad_query.reshape(SEQ, QH * HD), grad_key.reshape(SEQ, KV * HD), term)

def adam_update(grad_w, master, m_code, m_scale, v_code, v_scale):
    shape4 = (grad_w.shape[0] // 2, 2, m_scale.shape[1], HD)
    grad4 = grad_w.reshape(shape4)
    m_old = m_code.astype(jnp.float32).reshape(shape4) * m_scale[:, None, :, None]
    v_old = v_code.astype(jnp.float32).reshape(shape4) * v_scale[:, None, :, None]
    m_new = 0.9 * m_old + 0.1 * grad4
    v_new = 0.999 * v_old + 0.001 * grad4 * grad4
    first_fix = 1.0 - 0.9 ** STEP
    second_fix = 1.0 - 0.999 ** STEP
    update = m_new / first_fix / (jnp.sqrt(v_new / second_fix) + 1e-08)
    new_master = master - 0.01 * update.reshape(master.shape)
    m_top = lax.optimization_barrier(jnp.max(jnp.abs(m_new), axis=(1, 3)))
    v_top = lax.optimization_barrier(jnp.max(jnp.abs(v_new), axis=(1, 3)))
    new_m_code = (m_new / (m_top[:, None, :, None] + 1e-06)).astype(jnp.bfloat16).reshape(master.shape)
    new_v_code = (v_new / (v_top[:, None, :, None] + 1e-06)).astype(jnp.bfloat16).reshape(master.shape)
    return (new_master, new_m_code, m_top, new_v_code, v_top)

def reference(hidden, query, key, grad_out, doc_lens, master, m_code, m_scale, v_code, v_scale):
    weight = master.astype(jnp.bfloat16)

    def add_group(total, items):
        hidden_rows, query_rows, key_rows, cot_rows, lengths = items
        grad_query, grad_key, term = group_terms(hidden_rows, query_rows, key_rows, cot_rows, lengths, weight)
        return (total + term, (grad_query, grad_key))
    start_sum = jnp.zeros((D, KV * HD), jnp.float32)
    grad_w, outputs = lax.scan(add_group, start_sum, (hidden, query, key, grad_out, doc_lens))
    grad_query, grad_key = outputs
    new_master, new_m_code, new_m_scale, new_v_code, new_v_scale = adam_update(grad_w, master, m_code, m_scale, v_code, v_scale)
    return (grad_query, grad_key, new_master, new_m_code, new_m_scale, new_v_code, new_v_scale)
```

```python
import functools
import math

import jax
import jax.numpy as jnp
from jax import lax
from jax.experimental import pallas as pl
from jax.experimental.pallas import tpu as pltpu
from jax.sharding import PartitionSpec as P

D = 4096
HD = 128
DOCS = 8
STEP = 1000
SEQ = 1024
GROUP = 4
QW = GROUP * HD
ROWS = 128
BLOCKS = SEQ // ROWS
MOST = 4
NEG = -1e30
INV_WIDTH = 1.0 / math.sqrt(D)
SCALE = 1.0 / math.sqrt(HD)
VMEM_LIMIT = 48 * 1024 * 1024
F32 = jnp.float32
BF16 = jnp.bfloat16


def dot(a, b):
    return jnp.dot(a, b, preferred_element_type=F32)


def stacked(block):
    return jnp.concatenate([block[:, a * HD : (a + 1) * HD] for a in range(GROUP)], axis=0)


def params():
    return pltpu.CompilerParams(vmem_limit_bytes=VMEM_LIMIT)


def pack_kernel(q_ref, c_ref, k_ref, out_ref):
    out_ref[0, :, 0:QW] = q_ref[...]
    out_ref[0, :, QW : 2 * QW] = c_ref[...]
    out_ref[0, :, 2 * QW :] = k_ref[...]


def pack(query, cot, key):
    tokens = query.shape[0]
    return pl.pallas_call(
        pack_kernel,
        grid=(8,),
        in_specs=[
            pl.BlockSpec((tokens, QW), lambda j: (0, j)),
            pl.BlockSpec((tokens, QW), lambda j: (0, j)),
            pl.BlockSpec((tokens, HD), lambda j: (0, j)),
        ],
        out_specs=pl.BlockSpec((1, tokens, 2 * QW + HD), lambda j: (j, 0, 0)),
        out_shape=jax.ShapeDtypeStruct((8, tokens, 2 * QW + HD), BF16),
        compiler_params=params(),
    )(query, cot, key)


def by_window(i, body):
    for count in range(1, MOST + 1):
        chosen = (i == count - 1) if count < MOST else (i >= MOST - 1)
        pl.when(chosen)(functools.partial(body, count))


def probs_kernel(lens_ref, r_ref, pt_ref, gv_ref, acc_ref):
    i = pl.program_id(0)

    @pl.when(i == 0)
    def _():
        acc_ref[...] = jnp.zeros_like(acc_ref)

    first = pl.multiple_of(i * ROWS, ROWS)

    def body(count):
        lower = pl.multiple_of((i + 1 - count) * ROWS, ROWS)
        queries = stacked(r_ref[pl.ds(first, ROWS), 0:QW])
        cot = stacked(r_ref[pl.ds(first, ROWS), QW : 2 * QW])
        lane = lax.broadcasted_iota(jnp.int32, (1, GROUP * ROWS), 1)
        position = first + jnp.bitwise_and(lane, ROWS - 1)
        start = jnp.zeros_like(position)
        end = jnp.int32(0)
        for k in range(DOCS):
            length = lens_ref[0, k]
            end = end + length
            start = start + jnp.where(position >= end, length, 0)
        row = lax.broadcasted_iota(jnp.int32, (ROWS, GROUP * ROWS), 0)
        first_row = start - lower
        last_row = position - lower
        scores = []
        highest = None
        for b in range(count):
            keys = r_ref[pl.ds(lower + b * ROWS, ROWS), 2 * QW :]
            tile = lax.dot_general(
                keys, queries, (((1,), (1,)), ((), ())), preferred_element_type=F32
            )
            allowed = row >= first_row - b * ROWS
            if b == count - 1:
                allowed = allowed & (row <= last_row - b * ROWS)
            tile = jnp.where(allowed, tile, NEG)
            top = jnp.max(tile, axis=0, keepdims=True)
            highest = top if highest is None else jnp.maximum(highest, top)
            scores.append(tile)
        total = None
        weights = []
        for tile in scores:
            weight = jnp.exp2((tile - highest) * (SCALE * math.log2(math.e)))
            part = jnp.sum(weight, axis=0, keepdims=True)
            total = part if total is None else total + part
            weights.append(weight)
        inverse = 1.0 / total
        for b in range(count):
            probs = (weights[b] * inverse).astype(BF16)
            pt_ref[0, b * ROWS : (b + 1) * ROWS, :] = probs
            rows = pl.ds(lower + b * ROWS, ROWS)
            acc_ref[rows, :] = acc_ref[rows, :] + dot(probs, cot)

    by_window(i, body)

    @pl.when(i == BLOCKS - 1)
    def _():
        gv_ref[...] = acc_ref[...].astype(BF16)


def probs_call(doc_lens, packed):
    width = 2 * QW + HD
    return pl.pallas_call(
        probs_kernel,
        grid=(BLOCKS,),
        in_specs=[
            pl.BlockSpec(memory_space=pltpu.SMEM),
            pl.BlockSpec((SEQ, width), lambda i: (0, 0)),
        ],
        out_specs=[
            pl.BlockSpec((1, MOST * ROWS, GROUP * ROWS), lambda i: (i, 0, 0)),
            pl.BlockSpec((SEQ, HD), lambda i: (0, 0)),
        ],
        out_shape=[
            jax.ShapeDtypeStruct((BLOCKS, MOST * ROWS, GROUP * ROWS), BF16),
            jax.ShapeDtypeStruct((SEQ, HD), BF16),
        ],
        scratch_shapes=[pltpu.VMEM((SEQ, HD), F32)],
        compiler_params=params(),
    )(doc_lens, packed)


def project_kernel(h_ref, w_ref, gv_ref, val_ref, term_ref, acc_ref, gvt_ref):
    j = pl.program_id(0)

    @pl.when(j == 0)
    def _():
        acc_ref[...] = jnp.zeros_like(acc_ref)
        gvt_ref[...] = gv_ref[...].T

    hidden = h_ref[...]
    term = dot(gvt_ref[...], hidden)
    term_ref[...] = (term.T * INV_WIDTH).astype(BF16)
    acc_ref[...] = acc_ref[...] + dot(hidden, w_ref[...])

    @pl.when(j == pl.num_programs(0) - 1)
    def _():
        val_ref[...] = (acc_ref[...] * INV_WIDTH).astype(BF16)


def project_call(whole, weight, grad_values):
    step = 512
    return pl.pallas_call(
        project_kernel,
        grid=(D // step,),
        in_specs=[
            pl.BlockSpec((SEQ, step), lambda j: (0, j)),
            pl.BlockSpec((step, HD), lambda j: (j, 0)),
            pl.BlockSpec((SEQ, HD), lambda j: (0, 0)),
        ],
        out_specs=[
            pl.BlockSpec((SEQ, HD), lambda j: (0, 0)),
            pl.BlockSpec((step, HD), lambda j: (j, 0)),
        ],
        out_shape=[
            jax.ShapeDtypeStruct((SEQ, HD), BF16),
            jax.ShapeDtypeStruct((D, HD), BF16),
        ],
        scratch_shapes=[pltpu.VMEM((SEQ, HD), F32), pltpu.VMEM((HD, SEQ), BF16)],
        compiler_params=params(),
    )(whole, weight, grad_values)


def grads_kernel(r_ref, pt_ref, val_ref, out_ref, acc_ref, kt_ref, vt_ref):
    i = pl.program_id(0)

    @pl.when(i == 0)
    def _():
        acc_ref[...] = jnp.zeros_like(acc_ref)
        kt_ref[...] = r_ref[:, 2 * QW :].T
        vt_ref[...] = val_ref[...].T

    first = pl.multiple_of(i * ROWS, ROWS)

    def body(count):
        lower = pl.multiple_of((i + 1 - count) * ROWS, ROWS)
        size = count * ROWS
        queries = stacked(r_ref[pl.ds(first, ROWS), 0:QW])
        cot_t = stacked(r_ref[pl.ds(first, ROWS), QW : 2 * QW]).T
        attn_t = dot(vt_ref[:, pl.ds(lower, size)], pt_ref[0, 0:size, :]).astype(BF16)
        delta = jnp.sum(attn_t.astype(F32) * cot_t.astype(F32), axis=0, keepdims=True)
        grads = []
        for b in range(count):
            rows = pl.ds(lower + b * ROWS, ROWS)
            prob_grad = dot(val_ref[rows, :], cot_t)
            probs = pt_ref[0, b * ROWS : (b + 1) * ROWS, :].astype(F32)
            score_grad = (probs * (prob_grad - delta)).astype(BF16)
            acc_ref[rows, :] = acc_ref[rows, :] + dot(score_grad, queries)
            grads.append(score_grad)
        grad_t = dot(kt_ref[:, pl.ds(lower, size)], jnp.concatenate(grads, axis=0)) * SCALE
        grad = grad_t.T.astype(BF16)
        for a in range(GROUP):
            out_ref[pl.ds(first, ROWS), a * HD : (a + 1) * HD] = grad[a * ROWS : (a + 1) * ROWS, :]

    by_window(i, body)

    @pl.when(i == BLOCKS - 1)
    def _():
        out_ref[:, QW:] = (acc_ref[...] * SCALE).astype(BF16)


def grads_call(packed, probs, values):
    width = 2 * QW + HD
    return pl.pallas_call(
        grads_kernel,
        grid=(BLOCKS,),
        in_specs=[
            pl.BlockSpec((SEQ, width), lambda i: (0, 0)),
            pl.BlockSpec((1, MOST * ROWS, GROUP * ROWS), lambda i: (i, 0, 0)),
            pl.BlockSpec((SEQ, HD), lambda i: (0, 0)),
        ],
        out_specs=pl.BlockSpec((SEQ, QW + HD), lambda i: (0, 0)),
        out_shape=jax.ShapeDtypeStruct((SEQ, QW + HD), BF16),
        scratch_shapes=[
            pltpu.VMEM((SEQ, HD), F32),
            pltpu.VMEM((HD, SEQ), BF16),
            pltpu.VMEM((HD, SEQ), BF16),
        ],
        compiler_params=params(),
    )(packed, probs, values)


def unpack_kernel(in_ref, q_ref, k_ref):
    q_ref[...] = in_ref[0, :, 0:QW]
    k_ref[...] = in_ref[0, :, QW:]


def unpack(back):
    tokens = back.shape[1]
    return pl.pallas_call(
        unpack_kernel,
        grid=(8,),
        in_specs=[pl.BlockSpec((1, tokens, QW + HD), lambda j: (j, 0, 0))],
        out_specs=[
            pl.BlockSpec((tokens, QW), lambda j: (0, j)),
            pl.BlockSpec((tokens, HD), lambda j: (0, j)),
        ],
        out_shape=[
            jax.ShapeDtypeStruct((tokens, 8 * QW), BF16),
            jax.ShapeDtypeStruct((tokens, 8 * HD), BF16),
        ],
        compiler_params=params(),
    )(back)


def adam_kernel(
    parts_ref,
    master_ref,
    mc_ref,
    ms_ref,
    vc_ref,
    vs_ref,
    master_out,
    mc_out,
    ms_out,
    vc_out,
    vs_out,
    grad_ref,
    mold_ref,
    vold_ref,
    step_ref,
    mcode_ref,
    vcode_ref,
):
    total = jnp.zeros(grad_ref.shape, F32)
    for g in range(parts_ref.shape[0]):
        total = total + parts_ref[g].astype(F32)
    grad_ref[...] = total
    mold_ref[...] = mc_ref[...].astype(F32)
    vold_ref[...] = vc_ref[...].astype(F32)
    half = grad_ref.shape[0] // 2
    first_fix = 1.0 - 0.9**STEP
    second_fix = 1.0 - 0.999**STEP
    news = []
    for odd in range(2):
        rows = pl.ds(odd, half, stride=2)
        grad = grad_ref[rows, :]
        m_new = 0.9 * (mold_ref[rows, :] * ms_ref[...]) + 0.1 * grad
        v_new = 0.999 * (vold_ref[rows, :] * vs_ref[...]) + 0.001 * grad * grad
        step_ref[rows, :] = m_new / first_fix / (jnp.sqrt(v_new / second_fix) + 1e-08)
        news.append((m_new, v_new))
    m_top = jnp.maximum(
        jnp.max(jnp.abs(news[0][0]), axis=1, keepdims=True),
        jnp.max(jnp.abs(news[1][0]), axis=1, keepdims=True),
    )
    v_top = jnp.maximum(
        jnp.max(jnp.abs(news[0][1]), axis=1, keepdims=True),
        jnp.max(jnp.abs(news[1][1]), axis=1, keepdims=True),
    )
    ms_out[...] = m_top
    vs_out[...] = v_top
    for odd in range(2):
        rows = pl.ds(odd, half, stride=2)
        mcode_ref[rows, :] = news[odd][0] / (m_top + 1e-06)
        vcode_ref[rows, :] = news[odd][1] / (v_top + 1e-06)
    mc_out[...] = mcode_ref[...].astype(BF16)
    vc_out[...] = vcode_ref[...].astype(BF16)
    master_out[...] = master_ref[...] - 0.01 * step_ref[...]


def adam_call(parts, master, m_code, m_scale, v_code, v_scale):
    shape = master.shape
    return pl.pallas_call(
        adam_kernel,
        out_shape=[
            jax.ShapeDtypeStruct(shape, F32),
            jax.ShapeDtypeStruct(shape, BF16),
            jax.ShapeDtypeStruct(m_scale.shape, F32),
            jax.ShapeDtypeStruct(shape, BF16),
            jax.ShapeDtypeStruct(v_scale.shape, F32),
        ],
        scratch_shapes=[pltpu.VMEM(shape, F32) for _ in range(6)],
        compiler_params=params(),
    )(parts, master, m_code, m_scale, v_code, v_scale)


def shards(hidden, query, key, grad_out, doc_lens, master, m_code, m_scale, v_code, v_scale):
    n_dp = lax.axis_size("dp")
    packed = pack(query[0], grad_out[0], key[0])
    packed = lax.all_to_all(packed, "seq", split_axis=0, concat_axis=0, tiled=True)
    packed = packed.reshape(SEQ, 2 * QW + HD)
    whole = lax.all_gather(hidden[0], "seq", axis=0, tiled=True)
    copies = jnp.broadcast_to(master.astype(BF16)[None], (n_dp,) + master.shape)
    weight = lax.all_to_all(copies, "dp", split_axis=0, concat_axis=0, tiled=True)
    weight = weight.reshape(D, HD)
    probs, grad_values = probs_call(doc_lens, packed)
    values, term = project_call(whole, weight, grad_values)
    parts = lax.all_to_all(
        term.reshape((n_dp,) + master.shape), "dp", split_axis=0, concat_axis=0, tiled=True
    )
    grads = grads_call(packed, probs, values)
    back = lax.all_to_all(
        grads.reshape(8, ROWS, QW + HD), "seq", split_axis=0, concat_axis=0, tiled=True
    )
    grad_query, grad_key = unpack(back)
    state = adam_call(parts, master, m_code, m_scale, v_code, v_scale)
    return (grad_query[None], grad_key[None]) + tuple(state)


def solution(mesh):
    return jax.shard_map(
        shards,
        mesh=mesh,
        in_specs=(
            P("dp", "seq", None),
            P("dp", "seq", None),
            P("dp", "seq", None),
            P("dp", "seq", None),
            P("dp", None),
            P("dp", "seq"),
            P("dp", "seq"),
            P("dp", "seq"),
            P("dp", "seq"),
            P("dp", "seq"),
        ),
        out_specs=(
            P("dp", "seq", None),
            P("dp", "seq", None),
            P("dp", "seq"),
            P("dp", "seq"),
            P("dp", "seq"),
            P("dp", "seq"),
            P("dp", "seq"),
        ),
        check_vma=False,
    )
```

```python
import functools
import math

import jax
import jax.numpy as jnp
from jax import lax
from jax.experimental import pallas as pl
from jax.experimental.pallas import tpu as pltpu
from jax.sharding import PartitionSpec as P

D = 4096
HD = 128
DOCS = 8
STEP = 1000
SEQ = 1024
GROUP = 4
QW = GROUP * HD
ROWS = 128
BLOCKS = SEQ // ROWS
MOST = 4
NEG = -1e30
INV_WIDTH = 1.0 / math.sqrt(D)
SCALE = 1.0 / math.sqrt(HD)
VMEM_LIMIT = 48 * 1024 * 1024
F32 = jnp.float32
BF16 = jnp.bfloat16


def dot(a, b):
    return jnp.dot(a, b, preferred_element_type=F32)


def stacked(block):
    return jnp.concatenate([block[:, a * HD : (a + 1) * HD] for a in range(GROUP)], axis=0)


def params():
    return pltpu.CompilerParams(vmem_limit_bytes=VMEM_LIMIT)


XS = 4
HOPS = [(0, 0), (0, 1), (1, 0), (3, 0), (1, 1), (3, 1), (2, 0), (2, 1)]


def hop(value, k):
    dx, dc = HOPS[k]
    return lax.rem(lax.div(value, 2) + dx, XS) * 2 + jnp.bitwise_xor(lax.rem(value, 2), dc)


def perm(k):
    dx, dc = HOPS[k]
    return [(s, ((s // 2 + dx) % XS) * 2 + ((s % 2) ^ dc)) for s in range(2 * XS)]


def send(array, k):
    return lax.ppermute(array, "seq", perm(k))


ANYWHERE = pl.BlockSpec(memory_space=pl.ANY)
SCALARS = pl.BlockSpec(memory_space=pltpu.SMEM)


def run_copies(copies):
    for copy in copies:
        copy.start()
    for copy in copies:
        copy.wait()


def pack_kernel(to_ref, q_ref, c_ref, k_ref, *refs):
    outs, sems = refs[:-1], refs[-1]
    copies = []
    for r, out in enumerate(outs):
        j = to_ref[r]
        wide = pl.ds(pl.multiple_of(j * QW, QW), QW)
        thin = pl.ds(pl.multiple_of(j * HD, HD), HD)
        for n, (src, lanes, place) in enumerate(
            [
                (q_ref, wide, pl.ds(0, QW)),
                (c_ref, wide, pl.ds(QW, QW)),
                (k_ref, thin, pl.ds(2 * QW, HD)),
            ]
        ):
            copies.append(
                pltpu.make_async_copy(src.at[:, lanes], out.at[:, place], sems.at[3 * r + n])
            )
    run_copies(copies)


def pack(to, query, cot, key):
    tokens = query.shape[0]
    return pl.pallas_call(
        pack_kernel,
        in_specs=[SCALARS, ANYWHERE, ANYWHERE, ANYWHERE],
        out_specs=[ANYWHERE] * 8,
        out_shape=[jax.ShapeDtypeStruct((tokens, 2 * QW + HD), BF16)] * 8,
        scratch_shapes=[pltpu.SemaphoreType.DMA((24,))],
        compiler_params=params(),
    )(to, query, cot, key)


def gather_pieces(from_ref, piece_refs, whole_ref, sems):
    run_copies(
        [
            pltpu.make_async_copy(
                piece,
                whole_ref.at[pl.ds(pl.multiple_of(from_ref[r] * ROWS, ROWS), ROWS), :],
                sems.at[r],
            )
            for r, piece in enumerate(piece_refs)
        ]
    )


def by_window(i, body):
    for count in range(1, MOST + 1):
        chosen = (i == count - 1) if count < MOST else (i >= MOST - 1)
        pl.when(chosen)(functools.partial(body, count))


def probs_kernel(lens_ref, from_ref, *refs):
    pieces, (pt_ref, gv_ref, r_ref, acc_ref, sems) = refs[:8], refs[8:]
    i = pl.program_id(0)

    @pl.when(i == 0)
    def _():
        gather_pieces(from_ref, pieces, r_ref, sems)
        acc_ref[...] = jnp.zeros_like(acc_ref)

    first = pl.multiple_of(i * ROWS, ROWS)

    def body(count):
        lower = pl.multiple_of((i + 1 - count) * ROWS, ROWS)
        queries = stacked(r_ref[pl.ds(first, ROWS), 0:QW])
        cot = stacked(r_ref[pl.ds(first, ROWS), QW : 2 * QW])
        lane = lax.broadcasted_iota(jnp.int32, (1, GROUP * ROWS), 1)
        position = first + jnp.bitwise_and(lane, ROWS - 1)
        start = jnp.zeros_like(position)
        end = jnp.int32(0)
        for k in range(DOCS):
            length = lens_ref[0, k]
            end = end + length
            start = start + jnp.where(position >= end, length, 0)
        row = lax.broadcasted_iota(jnp.int32, (ROWS, GROUP * ROWS), 0)
        first_row = start - lower
        last_row = position - lower
        scores = []
        highest = None
        for b in range(count):
            keys = r_ref[pl.ds(lower + b * ROWS, ROWS), 2 * QW :]
            tile = lax.dot_general(
                keys, queries, (((1,), (1,)), ((), ())), preferred_element_type=F32
            )
            allowed = row >= first_row - b * ROWS
            if b == count - 1:
                allowed = allowed & (row <= last_row - b * ROWS)
            tile = jnp.where(allowed, tile, NEG)
            top = jnp.max(tile, axis=0, keepdims=True)
            highest = top if highest is None else jnp.maximum(highest, top)
            scores.append(tile)
        total = None
        weights = []
        for tile in scores:
            weight = jnp.exp2((tile - highest) * (SCALE * math.log2(math.e)))
            part = jnp.sum(weight, axis=0, keepdims=True)
            total = part if total is None else total + part
            weights.append(weight)
        inverse = 1.0 / total
        for b in range(count):
            probs = (weights[b] * inverse).astype(BF16)
            pt_ref[0, b * ROWS : (b + 1) * ROWS, :] = probs
            rows = pl.ds(lower + b * ROWS, ROWS)
            acc_ref[rows, :] = acc_ref[rows, :] + dot(probs, cot)

    by_window(i, body)

    @pl.when(i == BLOCKS - 1)
    def _():
        gv_ref[...] = acc_ref[...].astype(BF16)


def probs_call(doc_lens, origin, pieces):
    width = 2 * QW + HD
    return pl.pallas_call(
        probs_kernel,
        grid=(BLOCKS,),
        in_specs=[SCALARS, SCALARS] + [ANYWHERE] * 8,
        out_specs=[
            pl.BlockSpec((1, MOST * ROWS, GROUP * ROWS), lambda i: (i, 0, 0)),
            pl.BlockSpec((SEQ, HD), lambda i: (0, 0)),
        ],
        out_shape=[
            jax.ShapeDtypeStruct((BLOCKS, MOST * ROWS, GROUP * ROWS), BF16),
            jax.ShapeDtypeStruct((SEQ, HD), BF16),
        ],
        scratch_shapes=[
            pltpu.VMEM((SEQ, width), BF16),
            pltpu.VMEM((SEQ, HD), F32),
            pltpu.SemaphoreType.DMA((8,)),
        ],
        compiler_params=params(),
    )(doc_lens, origin, *pieces)


def project_kernel(from_ref, *refs):
    hidden_refs, (w_ref, gv_ref, val_ref, term_ref, acc_ref, gvt_ref) = refs[:10], refs[10:]
    j = pl.program_id(0)

    @pl.when(j == 0)
    def _():
        acc_ref[...] = jnp.zeros_like(acc_ref)
        for r in range(8):
            rows = pl.ds(pl.multiple_of(from_ref[r] * ROWS, ROWS), ROWS)
            gvt_ref[:, r * ROWS : (r + 1) * ROWS] = gv_ref[rows, :].T

    hidden = jnp.concatenate([ref[...] for ref in hidden_refs], axis=0)
    term = dot(gvt_ref[...], hidden)
    term_ref[...] = (term.T * INV_WIDTH).astype(BF16)
    acc_ref[...] = acc_ref[...] + dot(hidden, w_ref[...])

    @pl.when(j == pl.num_programs(0) - 1)
    def _():
        for r in range(8):
            rows = pl.ds(pl.multiple_of(from_ref[r] * ROWS, ROWS), ROWS)
            part = acc_ref[r * ROWS : (r + 1) * ROWS, :]
            val_ref[rows, :] = (part * INV_WIDTH).astype(BF16)


def project_call(origin, pieces, weight, grad_values):
    step = 512
    return pl.pallas_call(
        project_kernel,
        grid=(D // step,),
        in_specs=[SCALARS]
        + [pl.BlockSpec((piece.shape[0], step), lambda j: (0, j)) for piece in pieces]
        + [
            pl.BlockSpec((step, HD), lambda j: (j, 0)),
            pl.BlockSpec((SEQ, HD), lambda j: (0, 0)),
        ],
        out_specs=[
            pl.BlockSpec((SEQ, HD), lambda j: (0, 0)),
            pl.BlockSpec((step, HD), lambda j: (j, 0)),
        ],
        out_shape=[
            jax.ShapeDtypeStruct((SEQ, HD), BF16),
            jax.ShapeDtypeStruct((D, HD), BF16),
        ],
        scratch_shapes=[pltpu.VMEM((SEQ, HD), F32), pltpu.VMEM((HD, SEQ), BF16)],
        compiler_params=params(),
    )(origin, *pieces, weight, grad_values)


def grads_kernel(from_ref, to_ref, *refs):
    pieces, (pt_ref, val_ref), outs = refs[:8], refs[8:10], refs[10:18]
    r_ref, out_ref, acc_ref, kt_ref, vt_ref, sems = refs[18:]
    i = pl.program_id(0)

    @pl.when(i == 0)
    def _():
        gather_pieces(from_ref, pieces, r_ref, sems)
        acc_ref[...] = jnp.zeros_like(acc_ref)
        kt_ref[...] = r_ref[:, 2 * QW :].T
        vt_ref[...] = val_ref[...].T

    first = pl.multiple_of(i * ROWS, ROWS)

    def body(count):
        lower = pl.multiple_of((i + 1 - count) * ROWS, ROWS)
        size = count * ROWS
        queries = stacked(r_ref[pl.ds(first, ROWS), 0:QW])
        cot_t = stacked(r_ref[pl.ds(first, ROWS), QW : 2 * QW]).T
        attn_t = dot(vt_ref[:, pl.ds(lower, size)], pt_ref[0, 0:size, :]).astype(BF16)
        delta = jnp.sum(attn_t.astype(F32) * cot_t.astype(F32), axis=0, keepdims=True)
        grads = []
        for b in range(count):
            rows = pl.ds(lower + b * ROWS, ROWS)
            prob_grad = dot(val_ref[rows, :], cot_t)
            probs = pt_ref[0, b * ROWS : (b + 1) * ROWS, :].astype(F32)
            score_grad = (probs * (prob_grad - delta)).astype(BF16)
            acc_ref[rows, :] = acc_ref[rows, :] + dot(score_grad, queries)
            grads.append(score_grad)
        grad_t = dot(kt_ref[:, pl.ds(lower, size)], jnp.concatenate(grads, axis=0)) * SCALE
        grad = grad_t.T.astype(BF16)
        for a in range(GROUP):
            out_ref[pl.ds(first, ROWS), a * HD : (a + 1) * HD] = grad[a * ROWS : (a + 1) * ROWS, :]

    by_window(i, body)

    @pl.when(i == BLOCKS - 1)
    def _():
        out_ref[:, QW:] = (acc_ref[...] * SCALE).astype(BF16)
        run_copies(
            [
                pltpu.make_async_copy(
                    out_ref.at[pl.ds(pl.multiple_of(to_ref[r] * ROWS, ROWS), ROWS), :],
                    out,
                    sems.at[r],
                )
                for r, out in enumerate(outs)
            ]
        )


def grads_call(origin, to, pieces, probs, values):
    width = 2 * QW + HD
    return pl.pallas_call(
        grads_kernel,
        grid=(BLOCKS,),
        in_specs=[SCALARS, SCALARS]
        + [ANYWHERE] * 8
        + [
            pl.BlockSpec((1, MOST * ROWS, GROUP * ROWS), lambda i: (i, 0, 0)),
            pl.BlockSpec((SEQ, HD), lambda i: (0, 0)),
        ],
        out_specs=[ANYWHERE] * 8,
        out_shape=[jax.ShapeDtypeStruct((ROWS, QW + HD), BF16)] * 8,
        scratch_shapes=[
            pltpu.VMEM((SEQ, width), BF16),
            pltpu.VMEM((SEQ, QW + HD), BF16),
            pltpu.VMEM((SEQ, HD), F32),
            pltpu.VMEM((HD, SEQ), BF16),
            pltpu.VMEM((HD, SEQ), BF16),
            pltpu.SemaphoreType.DMA((8,)),
        ],
        compiler_params=params(),
    )(origin, to, *pieces, probs, values)


def unpack_kernel(from_ref, *refs):
    pieces, (q_ref, k_ref, sems) = refs[:8], refs[8:]
    copies = []
    for r, piece in enumerate(pieces):
        j = from_ref[r]
        wide = pl.ds(pl.multiple_of(j * QW, QW), QW)
        thin = pl.ds(pl.multiple_of(j * HD, HD), HD)
        copies.append(
            pltpu.make_async_copy(piece.at[:, pl.ds(0, QW)], q_ref.at[:, wide], sems.at[2 * r])
        )
        copies.append(
            pltpu.make_async_copy(piece.at[:, pl.ds(QW, HD)], k_ref.at[:, thin], sems.at[2 * r + 1])
        )
    run_copies(copies)


def unpack(origin, pieces):
    return pl.pallas_call(
        unpack_kernel,
        in_specs=[SCALARS] + [ANYWHERE] * 8,
        out_specs=[ANYWHERE] * 2,
        out_shape=[
            jax.ShapeDtypeStruct((ROWS, 8 * QW), BF16),
            jax.ShapeDtypeStruct((ROWS, 8 * HD), BF16),
        ],
        scratch_shapes=[pltpu.SemaphoreType.DMA((16,))],
        compiler_params=params(),
    )(origin, *pieces)


def adam_kernel(
    parts_ref,
    master_ref,
    mc_ref,
    ms_ref,
    vc_ref,
    vs_ref,
    master_out,
    mc_out,
    ms_out,
    vc_out,
    vs_out,
    grad_ref,
    mold_ref,
    vold_ref,
    step_ref,
    mcode_ref,
    vcode_ref,
):
    total = jnp.zeros(grad_ref.shape, F32)
    for g in range(parts_ref.shape[0]):
        total = total + parts_ref[g].astype(F32)
    grad_ref[...] = total
    mold_ref[...] = mc_ref[...].astype(F32)
    vold_ref[...] = vc_ref[...].astype(F32)
    half = grad_ref.shape[0] // 2
    first_fix = 1.0 - 0.9**STEP
    second_fix = 1.0 - 0.999**STEP
    news = []
    for odd in range(2):
        rows = pl.ds(odd, half, stride=2)
        grad = grad_ref[rows, :]
        m_new = 0.9 * (mold_ref[rows, :] * ms_ref[...]) + 0.1 * grad
        v_new = 0.999 * (vold_ref[rows, :] * vs_ref[...]) + 0.001 * grad * grad
        step_ref[rows, :] = m_new / first_fix / (jnp.sqrt(v_new / second_fix) + 1e-08)
        news.append((m_new, v_new))
    m_top = jnp.maximum(
        jnp.max(jnp.abs(news[0][0]), axis=1, keepdims=True),
        jnp.max(jnp.abs(news[1][0]), axis=1, keepdims=True),
    )
    v_top = jnp.maximum(
        jnp.max(jnp.abs(news[0][1]), axis=1, keepdims=True),
        jnp.max(jnp.abs(news[1][1]), axis=1, keepdims=True),
    )
    ms_out[...] = m_top
    vs_out[...] = v_top
    for odd in range(2):
        rows = pl.ds(odd, half, stride=2)
        mcode_ref[rows, :] = news[odd][0] / (m_top + 1e-06)
        vcode_ref[rows, :] = news[odd][1] / (v_top + 1e-06)
    mc_out[...] = mcode_ref[...].astype(BF16)
    vc_out[...] = vcode_ref[...].astype(BF16)
    master_out[...] = master_ref[...] - 0.01 * step_ref[...]


def adam_call(parts, master, m_code, m_scale, v_code, v_scale):
    shape = master.shape
    return pl.pallas_call(
        adam_kernel,
        out_shape=[
            jax.ShapeDtypeStruct(shape, F32),
            jax.ShapeDtypeStruct(shape, BF16),
            jax.ShapeDtypeStruct(m_scale.shape, F32),
            jax.ShapeDtypeStruct(shape, BF16),
            jax.ShapeDtypeStruct(v_scale.shape, F32),
        ],
        scratch_shapes=[pltpu.VMEM(shape, F32) for _ in range(6)],
        compiler_params=params(),
    )(parts, master, m_code, m_scale, v_code, v_scale)


def exchange(pieces):
    return [pieces[0]] + [send(pieces[r], r) for r in range(1, 8)]


def spread(own):
    right, left, core = send(own, 2), send(own, 3), send(own, 1)
    half = own.shape[0] // 2
    far_lo, far_hi = send(right[:half], 2), send(left[half:], 3)
    return [
        own,
        core,
        right,
        left,
        send(right, 1),
        send(left, 1),
        far_lo,
        far_hi,
        send(far_lo, 1),
        send(far_hi, 1),
    ]


def shards(hidden, query, key, grad_out, doc_lens, master, m_code, m_scale, v_code, v_scale):
    n_dp = lax.axis_size("dp")
    me = lax.axis_index("seq")
    to = jnp.stack([hop(me, r) for r in range(8)])
    back = [0, 1, 3, 2, 5, 4, 6, 7]
    origin = jnp.stack([hop(me, back[r]) for r in range(8)])
    hiddens = spread(hidden[0])
    pieces = exchange(pack(to, query[0], grad_out[0], key[0]))
    copies = jnp.broadcast_to(master.astype(BF16)[None], (n_dp,) + master.shape)
    weight = lax.all_to_all(copies, "dp", split_axis=0, concat_axis=0, tiled=True)
    weight = weight.reshape(D, HD)
    probs, grad_values = probs_call(doc_lens, origin, pieces)
    values, term = project_call(origin, hiddens, weight, grad_values)
    parts = lax.all_to_all(
        term.reshape((n_dp,) + master.shape), "dp", split_axis=0, concat_axis=0, tiled=True
    )
    grads = grads_call(origin, to, pieces, probs, values)
    grad_query, grad_key = unpack(origin, exchange(grads))
    state = adam_call(parts, master, m_code, m_scale, v_code, v_scale)
    return (grad_query[None], grad_key[None]) + tuple(state)


def solution(mesh):
    return jax.shard_map(
        shards,
        mesh=mesh,
        in_specs=(
            P("dp", "seq", None),
            P("dp", "seq", None),
            P("dp", "seq", None),
            P("dp", "seq", None),
            P("dp", None),
            P("dp", "seq"),
            P("dp", "seq"),
            P("dp", "seq"),
            P("dp", "seq"),
            P("dp", "seq"),
        ),
        out_specs=(
            P("dp", "seq", None),
            P("dp", "seq", None),
            P("dp", "seq"),
            P("dp", "seq"),
            P("dp", "seq"),
            P("dp", "seq"),
            P("dp", "seq"),
        ),
        check_vma=False,
    )
```

```python
import functools
import math

import jax
import jax.numpy as jnp
from jax import lax
from jax.experimental import pallas as pl
from jax.experimental.pallas import tpu as pltpu
from jax.sharding import PartitionSpec as P

D = 4096
HD = 128
DOCS = 8
STEP = 1000
SEQ = 1024
GROUP = 4
QW = GROUP * HD
ROWS = 128
BLOCKS = SEQ // ROWS
MOST = 4
NEG = -1e30
INV_WIDTH = 1.0 / math.sqrt(D)
SCALE = 1.0 / math.sqrt(HD)
F32 = jnp.float32
BF16 = jnp.bfloat16


def dot(a, b):
    return jnp.dot(a, b, preferred_element_type=F32)


def stacked(block):
    return jnp.concatenate([block[:, a * HD : (a + 1) * HD] for a in range(GROUP)], axis=0)


def params(mebibytes=24):
    return pltpu.CompilerParams(vmem_limit_bytes=mebibytes * 1024 * 1024)


XS = 4


def place(value, dx, dc):
    chip = lax.rem(lax.div(value, 2) + dx, XS)
    return chip * 2 + jnp.bitwise_xor(lax.rem(value, 2), dc)


def send(array, dx, dc):
    pairs = [(s, ((s // 2 + dx) % XS) * 2 + ((s % 2) ^ dc)) for s in range(2 * XS)]
    return lax.ppermute(array, "seq", pairs)


ANYWHERE = pl.BlockSpec(memory_space=pl.ANY)
SCALARS = pl.BlockSpec(memory_space=pltpu.SMEM)


def run_copies(copies):
    for copy in copies:
        copy.start()
    for copy in copies:
        copy.wait()


def pack_kernel(to_ref, q_ref, c_ref, k_ref, *refs):
    outs, sems = refs[:-1], refs[-1]
    copies = []
    for r in range(8):
        out = outs[r // 2].at[r % 2]
        j = to_ref[r]
        wide = pl.ds(pl.multiple_of(j * QW, QW), QW)
        thin = pl.ds(pl.multiple_of(j * HD, HD), HD)
        for n, (src, lanes, into) in enumerate(
            [
                (q_ref, wide, pl.ds(0, QW)),
                (c_ref, wide, pl.ds(QW, QW)),
                (k_ref, thin, pl.ds(2 * QW, HD)),
            ]
        ):
            copies.append(
                pltpu.make_async_copy(src.at[:, lanes], out.at[:, into], sems.at[3 * r + n])
            )
    run_copies(copies)


def pack(to, query, cot, key):
    tokens = query.shape[0]
    return pl.pallas_call(
        pack_kernel,
        in_specs=[SCALARS, ANYWHERE, ANYWHERE, ANYWHERE],
        out_specs=[ANYWHERE] * XS,
        out_shape=[jax.ShapeDtypeStruct((2, tokens, 2 * QW + HD), BF16)] * XS,
        scratch_shapes=[pltpu.SemaphoreType.DMA((24,))],
        compiler_params=params(60),
    )(to, query, cot, key)


def merge_kernel(*refs):
    pairs, out, sems = refs[:XS], refs[XS], refs[XS + 1]
    run_copies(
        [pltpu.make_async_copy(pair.at[1], out.at[r], sems.at[r]) for r, pair in enumerate(pairs)]
    )


def merge(pairs):
    return pl.pallas_call(
        merge_kernel,
        in_specs=[ANYWHERE] * XS,
        out_specs=ANYWHERE,
        out_shape=jax.ShapeDtypeStruct((XS,) + pairs[0].shape[1:], BF16),
        scratch_shapes=[pltpu.SemaphoreType.DMA((XS,))],
        compiler_params=params(4),
    )(*pairs)


def exchange(pairs):
    got = [pairs[0]] + [send(pairs[dx], dx, 0) for dx in (1, 3, 2)]
    got = [got[0], got[1], got[3], got[2]]
    return got + [send(merge(got), 0, 1)]


def arrived(refs):
    return [refs[r // 2].at[0] if r % 2 == 0 else refs[XS].at[r // 2] for r in range(8)]


def gather_pieces(from_ref, piece_refs, whole_ref, sems):
    run_copies(
        [
            pltpu.make_async_copy(
                piece,
                whole_ref.at[pl.ds(pl.multiple_of(from_ref[r] * ROWS, ROWS), ROWS), :],
                sems.at[r],
            )
            for r, piece in enumerate(arrived(piece_refs))
        ]
    )


def by_step(i, body):
    for v in range(BLOCKS // 2):
        pl.when(i == v)(functools.partial(body, v))


def window(block):
    count = min(block + 1, MOST)
    return count, (block + 1 - count) * ROWS


def block_probs(block, lens_ref, r_ref, pt_ref):
    first = block * ROWS
    count, lower = window(block)
    queries = stacked(r_ref[first : first + ROWS, 0:QW])
    lane = lax.broadcasted_iota(jnp.int32, (1, GROUP * ROWS), 1)
    position = first + jnp.bitwise_and(lane, ROWS - 1)
    start = jnp.zeros_like(position)
    end = jnp.int32(0)
    for k in range(DOCS):
        length = lens_ref[0, k]
        end = end + length
        start = start + jnp.where(position >= end, length, 0)
    row = lax.broadcasted_iota(jnp.int32, (ROWS, GROUP * ROWS), 0)
    first_row = start - lower
    last_row = position - lower
    scores = []
    highest = None
    for b in range(count):
        keys = r_ref[lower + b * ROWS : lower + (b + 1) * ROWS, 2 * QW :]
        tile = lax.dot_general(keys, queries, (((1,), (1,)), ((), ())), preferred_element_type=F32)
        allowed = row >= first_row - b * ROWS
        if b == count - 1:
            allowed = allowed & (row <= last_row - b * ROWS)
        tile = jnp.where(allowed, tile, NEG)
        top = jnp.max(tile, axis=0, keepdims=True)
        highest = top if highest is None else jnp.maximum(highest, top)
        scores.append(tile)
    total = None
    weights = []
    for tile in scores:
        weight = jnp.exp2((tile - highest) * (SCALE * math.log2(math.e)))
        part = jnp.sum(weight, axis=0, keepdims=True)
        total = part if total is None else total + part
        weights.append(weight)
    inverse = 1.0 / total
    for b in range(count):
        pt_ref[b * ROWS : (b + 1) * ROWS, :] = (weights[b] * inverse).astype(BF16)


def probs_kernel(lens_ref, from_ref, *refs):
    pieces, (pt_ref, gv_ref, r_ref, acc_ref, sems) = refs[:5], refs[5:]
    i = pl.program_id(0)

    @pl.when(i == 0)
    def _():
        gather_pieces(from_ref, pieces, r_ref, sems)
        acc_ref[...] = jnp.zeros_like(acc_ref)

    def body(v):
        for n, block in enumerate((v, v + MOST)):
            block_probs(block, lens_ref, r_ref, pt_ref.at[0, n])
        for n, block in enumerate((v, v + MOST)):
            count, lower = window(block)
            cot = stacked(r_ref[block * ROWS : (block + 1) * ROWS, QW : 2 * QW])
            size = count * ROWS
            acc_ref[lower : lower + size, :] += dot(pt_ref[0, n, 0:size, :], cot)

    by_step(i, body)

    @pl.when(i == BLOCKS // 2 - 1)
    def _():
        gv_ref[...] = acc_ref[...].astype(BF16)


PROBS_SHAPE = (BLOCKS // 2, 2, MOST * ROWS, GROUP * ROWS)
PROBS_SPEC = pl.BlockSpec((1,) + PROBS_SHAPE[1:], lambda i: (i, 0, 0, 0))


def probs_call(doc_lens, origin, pieces):
    width = 2 * QW + HD
    return pl.pallas_call(
        probs_kernel,
        grid=(BLOCKS // 2,),
        in_specs=[SCALARS, SCALARS] + [ANYWHERE] * 5,
        out_specs=[PROBS_SPEC, pl.BlockSpec((SEQ, HD), lambda i: (0, 0))],
        out_shape=[
            jax.ShapeDtypeStruct(PROBS_SHAPE, BF16),
            jax.ShapeDtypeStruct((SEQ, HD), BF16),
        ],
        scratch_shapes=[
            pltpu.VMEM((SEQ, width), BF16),
            pltpu.VMEM((SEQ, HD), F32),
            pltpu.SemaphoreType.DMA((8,)),
        ],
        compiler_params=params(),
    )(doc_lens, origin, *pieces)


def join(refs):
    return jnp.concatenate([ref[...] for ref in refs], axis=0)


def term_kernel(from_ref, *refs):
    hidden_refs, (gv_ref, term_ref, gvt_ref) = refs[:10], refs[10:]

    @pl.when(pl.program_id(0) == 0)
    def _():
        for r in range(8):
            rows = pl.ds(pl.multiple_of(from_ref[r] * ROWS, ROWS), ROWS)
            gvt_ref[:, r * ROWS : (r + 1) * ROWS] = gv_ref[rows, :].T

    term = dot(gvt_ref[...], join(hidden_refs))
    term_ref[...] = (term.T * INV_WIDTH).astype(BF16)


def values_kernel(from_ref, *refs):
    hidden_refs, (w_ref, val_ref, acc_ref) = refs[:10], refs[10:]
    j = pl.program_id(0)

    @pl.when(j == 0)
    def _():
        acc_ref[...] = jnp.zeros_like(acc_ref)

    acc_ref[...] += dot(join(hidden_refs), w_ref[...])

    @pl.when(j == pl.num_programs(0) - 1)
    def _():
        for r in range(8):
            rows = pl.ds(pl.multiple_of(from_ref[r] * ROWS, ROWS), ROWS)
            part = acc_ref[r * ROWS : (r + 1) * ROWS, :]
            val_ref[rows, :] = (part * INV_WIDTH).astype(BF16)


STRIPE = 1024


def hidden_specs(pieces):
    return [pl.BlockSpec((piece.shape[0], STRIPE), lambda j: (0, j)) for piece in pieces]


def term_call(origin, pieces, grad_values):
    return pl.pallas_call(
        term_kernel,
        grid=(D // STRIPE,),
        in_specs=[SCALARS]
        + hidden_specs(pieces)
        + [pl.BlockSpec((SEQ, HD), lambda j: (0, 0))],
        out_specs=pl.BlockSpec((STRIPE, HD), lambda j: (j, 0)),
        out_shape=jax.ShapeDtypeStruct((D, HD), BF16),
        scratch_shapes=[pltpu.VMEM((HD, SEQ), BF16)],
        compiler_params=params(),
    )(origin, *pieces, grad_values)


def values_call(origin, pieces, weight):
    return pl.pallas_call(
        values_kernel,
        grid=(D // STRIPE,),
        in_specs=[SCALARS]
        + hidden_specs(pieces)
        + [pl.BlockSpec((STRIPE, HD), lambda j: (j, 0))],
        out_specs=pl.BlockSpec((SEQ, HD), lambda j: (0, 0)),
        out_shape=jax.ShapeDtypeStruct((SEQ, HD), BF16),
        scratch_shapes=[pltpu.VMEM((SEQ, HD), F32)],
        compiler_params=params(),
    )(origin, *pieces, weight)


def block_grads(block, r_ref, pt_ref, val_ref, out_ref, acc_ref, kt_ref, vt_ref):
    first = block * ROWS
    count, lower = window(block)
    size = count * ROWS
    queries = stacked(r_ref[first : first + ROWS, 0:QW])
    cot_t = stacked(r_ref[first : first + ROWS, QW : 2 * QW]).T
    attn_t = dot(vt_ref[:, lower : lower + size], pt_ref[0:size, :]).astype(BF16)
    delta = jnp.sum(attn_t.astype(F32) * cot_t.astype(F32), axis=0, keepdims=True)
    prob_grad = dot(val_ref[lower : lower + size, :], cot_t)
    probs = pt_ref[0:size, :].astype(F32)
    score_grad = (probs * (prob_grad - delta)).astype(BF16)
    acc_ref[lower : lower + size, :] += dot(score_grad, queries)
    grad_t = dot(kt_ref[:, lower : lower + size], score_grad) * SCALE
    grad = grad_t.T.astype(BF16)
    for a in range(GROUP):
        out_ref[first : first + ROWS, a * HD : (a + 1) * HD] = grad[a * ROWS : (a + 1) * ROWS, :]


def grads_kernel(from_ref, to_ref, *refs):
    pieces, (pt_ref, val_ref), outs = refs[:5], refs[5:7], refs[7 : 7 + XS]
    r_ref, out_ref, acc_ref, kt_ref, vt_ref, sems = refs[7 + XS :]
    i = pl.program_id(0)

    @pl.when(i == 0)
    def _():
        gather_pieces(from_ref, pieces, r_ref, sems)
        acc_ref[...] = jnp.zeros_like(acc_ref)
        kt_ref[...] = r_ref[:, 2 * QW :].T
        vt_ref[...] = val_ref[...].T

    def body(v):
        for n, block in enumerate((v, v + MOST)):
            block_grads(block, r_ref, pt_ref.at[0, n], val_ref, out_ref, acc_ref, kt_ref, vt_ref)

    by_step(i, body)

    @pl.when(i == BLOCKS // 2 - 1)
    def _():
        out_ref[:, QW:] = (acc_ref[...] * SCALE).astype(BF16)
        run_copies(
            [
                pltpu.make_async_copy(
                    out_ref.at[pl.ds(pl.multiple_of(to_ref[r] * ROWS, ROWS), ROWS), :],
                    outs[r // 2].at[r % 2],
                    sems.at[r],
                )
                for r in range(8)
            ]
        )


def grads_call(origin, to, pieces, probs, values):
    width = 2 * QW + HD
    return pl.pallas_call(
        grads_kernel,
        grid=(BLOCKS // 2,),
        in_specs=[SCALARS, SCALARS]
        + [ANYWHERE] * 5
        + [PROBS_SPEC, pl.BlockSpec((SEQ, HD), lambda i: (0, 0))],
        out_specs=[ANYWHERE] * XS,
        out_shape=[jax.ShapeDtypeStruct((2, ROWS, QW + HD), BF16)] * XS,
        scratch_shapes=[
            pltpu.VMEM((SEQ, width), BF16),
            pltpu.VMEM((SEQ, QW + HD), BF16),
            pltpu.VMEM((SEQ, HD), F32),
            pltpu.VMEM((HD, SEQ), BF16),
            pltpu.VMEM((HD, SEQ), BF16),
            pltpu.SemaphoreType.DMA((8,)),
        ],
        compiler_params=params(),
    )(origin, to, *pieces, probs, values)


def unpack_kernel(from_ref, *refs):
    pieces, (q_ref, k_ref, sems) = refs[:5], refs[5:]
    copies = []
    for r, piece in enumerate(arrived(pieces)):
        j = from_ref[r]
        wide = pl.ds(pl.multiple_of(j * QW, QW), QW)
        thin = pl.ds(pl.multiple_of(j * HD, HD), HD)
        copies.append(
            pltpu.make_async_copy(piece.at[:, pl.ds(0, QW)], q_ref.at[:, wide], sems.at[2 * r])
        )
        copies.append(
            pltpu.make_async_copy(piece.at[:, pl.ds(QW, HD)], k_ref.at[:, thin], sems.at[2 * r + 1])
        )
    run_copies(copies)


def unpack(origin, pieces):
    return pl.pallas_call(
        unpack_kernel,
        in_specs=[SCALARS] + [ANYWHERE] * 5,
        out_specs=[ANYWHERE] * 2,
        out_shape=[
            jax.ShapeDtypeStruct((ROWS, 8 * QW), BF16),
            jax.ShapeDtypeStruct((ROWS, 8 * HD), BF16),
        ],
        scratch_shapes=[pltpu.SemaphoreType.DMA((16,))],
        compiler_params=params(4),
    )(origin, *pieces)


def adam_kernel(
    parts_ref,
    master_ref,
    mc_ref,
    ms_ref,
    vc_ref,
    vs_ref,
    master_out,
    mc_out,
    ms_out,
    vc_out,
    vs_out,
    grad_ref,
    mold_ref,
    vold_ref,
    step_ref,
    mcode_ref,
    vcode_ref,
):
    total = jnp.zeros(grad_ref.shape, F32)
    for g in range(parts_ref.shape[0]):
        total = total + parts_ref[g].astype(F32)
    grad_ref[...] = total
    mold_ref[...] = mc_ref[...].astype(F32)
    vold_ref[...] = vc_ref[...].astype(F32)
    half = grad_ref.shape[0] // 2
    first_fix = 1.0 - 0.9**STEP
    second_fix = 1.0 - 0.999**STEP
    news = []
    for odd in range(2):
        rows = pl.ds(odd, half, stride=2)
        grad = grad_ref[rows, :]
        m_new = 0.9 * (mold_ref[rows, :] * ms_ref[...]) + 0.1 * grad
        v_new = 0.999 * (vold_ref[rows, :] * vs_ref[...]) + 0.001 * grad * grad
        step_ref[rows, :] = m_new / first_fix / (jnp.sqrt(v_new / second_fix) + 1e-08)
        news.append((m_new, v_new))
    m_top = jnp.maximum(
        jnp.max(jnp.abs(news[0][0]), axis=1, keepdims=True),
        jnp.max(jnp.abs(news[1][0]), axis=1, keepdims=True),
    )
    v_top = jnp.maximum(
        jnp.max(jnp.abs(news[0][1]), axis=1, keepdims=True),
        jnp.max(jnp.abs(news[1][1]), axis=1, keepdims=True),
    )
    ms_out[...] = m_top
    vs_out[...] = v_top
    for odd in range(2):
        rows = pl.ds(odd, half, stride=2)
        mcode_ref[rows, :] = news[odd][0] / (m_top + 1e-06)
        vcode_ref[rows, :] = news[odd][1] / (v_top + 1e-06)
    mc_out[...] = mcode_ref[...].astype(BF16)
    vc_out[...] = vcode_ref[...].astype(BF16)
    master_out[...] = master_ref[...] - 0.01 * step_ref[...]


def adam_call(parts, master, m_code, m_scale, v_code, v_scale):
    shape = master.shape
    return pl.pallas_call(
        adam_kernel,
        out_shape=[
            jax.ShapeDtypeStruct(shape, F32),
            jax.ShapeDtypeStruct(shape, BF16),
            jax.ShapeDtypeStruct(m_scale.shape, F32),
            jax.ShapeDtypeStruct(shape, BF16),
            jax.ShapeDtypeStruct(v_scale.shape, F32),
        ],
        scratch_shapes=[pltpu.VMEM(shape, F32) for _ in range(6)],
        compiler_params=params(16),
    )(parts, master, m_code, m_scale, v_code, v_scale)


def shards(hidden, query, key, grad_out, doc_lens, master, m_code, m_scale, v_code, v_scale):
    n_dp = lax.axis_size("dp")
    me = lax.axis_index("seq")
    to = jnp.stack([place(me, r // 2, r % 2) for r in range(8)])
    origin = jnp.stack([place(me, (XS - r // 2) % XS, r % 2) for r in range(8)])
    around = jnp.stack([place(me, dx, dc) for dx in (0, 3, 1, 2) for dc in (0, 1)])
    own = hidden[0]
    half = own.shape[0] // 2
    left, right = send(own, 1, 0), send(own, 3, 0)
    pairs = pack(to, query[0], grad_out[0], key[0])
    pieces = exchange(pairs)
    master_bf, _ = lax.optimization_barrier((master.astype(BF16), pairs[0]))
    copies = jnp.broadcast_to(master_bf[None], (n_dp,) + master.shape)
    weight = lax.all_to_all(copies, "dp", split_axis=0, concat_axis=0, tiled=True)
    weight = weight.reshape(D, HD)
    far_lo, far_hi = send(left[:half], 1, 0), send(right[half:], 3, 0)
    own_core, left_core, right_core = send(own, 0, 1), send(left, 0, 1), send(right, 0, 1)
    probs, grad_values = probs_call(doc_lens, origin, pieces)
    far_lo, far_hi, grad_values = lax.optimization_barrier((far_lo, far_hi, grad_values))
    far_core = [send(far_lo, 0, 1), send(far_hi, 0, 1)]
    hiddens = [own, own_core, left, left_core, right, right_core, far_lo, far_hi] + far_core
    term = term_call(around, hiddens, grad_values)
    parts = lax.all_to_all(
        term.reshape((n_dp,) + master.shape), "dp", split_axis=0, concat_axis=0, tiled=True
    )
    values = values_call(around, hiddens, weight)
    grads = grads_call(origin, to, pieces, probs, values)
    grad_query, grad_key = unpack(origin, exchange(grads))
    state = adam_call(parts, master, m_code, m_scale, v_code, v_scale)
    return (grad_query[None], grad_key[None]) + tuple(state)


def solution(mesh):
    return jax.shard_map(
        shards,
        mesh=mesh,
        in_specs=(
            P("dp", "seq", None),
            P("dp", "seq", None),
            P("dp", "seq", None),
            P("dp", "seq", None),
            P("dp", None),
            P("dp", "seq"),
            P("dp", "seq"),
            P("dp", "seq"),
            P("dp", "seq"),
            P("dp", "seq"),
        ),
        out_specs=(
            P("dp", "seq", None),
            P("dp", "seq", None),
            P("dp", "seq"),
            P("dp", "seq"),
            P("dp", "seq"),
            P("dp", "seq"),
            P("dp", "seq"),
        ),
        check_vma=False,
    )
```

```python
import functools
import math

import jax
import jax.numpy as jnp
from jax import lax
from jax.experimental import pallas as pl
from jax.experimental.pallas import tpu as pltpu
from jax.sharding import PartitionSpec as P

D = 4096
HD = 128
DOCS = 8
STEP = 1000
SEQ = 1024
GROUP = 4
QW = GROUP * HD
ROWS = 128
BLOCKS = SEQ // ROWS
MOST = 4
NEG = -1e30
INV_WIDTH = 1.0 / math.sqrt(D)
SCALE = 1.0 / math.sqrt(HD)
F32 = jnp.float32
BF16 = jnp.bfloat16


def dot(a, b):
    return jnp.dot(a, b, preferred_element_type=F32)


def stacked(block):
    return jnp.concatenate([block[:, a * HD : (a + 1) * HD] for a in range(GROUP)], axis=0)


def params(mebibytes=24):
    return pltpu.CompilerParams(vmem_limit_bytes=mebibytes * 1024 * 1024)


XS = 4


def place(value, dx, dc):
    chip = lax.rem(lax.div(value, 2) + dx, XS)
    return chip * 2 + jnp.bitwise_xor(lax.rem(value, 2), dc)


def send(array, dx, dc):
    pairs = [(s, ((s // 2 + dx) % XS) * 2 + ((s % 2) ^ dc)) for s in range(2 * XS)]
    return lax.ppermute(array, "seq", pairs)


ANYWHERE = pl.BlockSpec(memory_space=pl.ANY)
SCALARS = pl.BlockSpec(memory_space=pltpu.SMEM)


def run_copies(copies):
    for copy in copies:
        copy.start()
    for copy in copies:
        copy.wait()


def pack_kernel(to_ref, q_ref, c_ref, k_ref, *refs):
    outs, sems = refs[:-1], refs[-1]
    copies = []
    for r in range(8):
        out = outs[r // 2].at[r % 2]
        j = to_ref[r]
        wide = pl.ds(pl.multiple_of(j * QW, QW), QW)
        thin = pl.ds(pl.multiple_of(j * HD, HD), HD)
        for n, (src, lanes, into) in enumerate(
            [
                (q_ref, wide, pl.ds(0, QW)),
                (c_ref, wide, pl.ds(QW, QW)),
                (k_ref, thin, pl.ds(2 * QW, HD)),
            ]
        ):
            copies.append(
                pltpu.make_async_copy(src.at[:, lanes], out.at[:, into], sems.at[3 * r + n])
            )
    run_copies(copies)


def pack(to, query, cot, key):
    tokens = query.shape[0]
    return pl.pallas_call(
        pack_kernel,
        in_specs=[SCALARS] + [pl.BlockSpec(memory_space=pltpu.VMEM)] * 3,
        out_specs=[ANYWHERE] * XS,
        out_shape=[jax.ShapeDtypeStruct((2, tokens, 2 * QW + HD), BF16)] * XS,
        scratch_shapes=[pltpu.SemaphoreType.DMA((24,))],
        compiler_params=params(60),
    )(to, query, cot, key)


def merge_kernel(*refs):
    pairs, out, sems = refs[:XS], refs[XS], refs[XS + 1]
    run_copies(
        [pltpu.make_async_copy(pair.at[1], out.at[r], sems.at[r]) for r, pair in enumerate(pairs)]
    )


def merge(pairs):
    return pl.pallas_call(
        merge_kernel,
        in_specs=[ANYWHERE] * XS,
        out_specs=ANYWHERE,
        out_shape=jax.ShapeDtypeStruct((XS,) + pairs[0].shape[1:], BF16),
        scratch_shapes=[pltpu.SemaphoreType.DMA((XS,))],
        compiler_params=params(4),
    )(*pairs)


def exchange(pairs):
    got = [pairs[0]] + [send(pairs[dx], dx, 0) for dx in (1, 3, 2)]
    got = [got[0], got[1], got[3], got[2]]
    return got + [send(merge(got), 0, 1)]


def arrived(refs):
    return [refs[r // 2].at[0] if r % 2 == 0 else refs[XS].at[r // 2] for r in range(8)]


def gather_pieces(from_ref, piece_refs, whole_ref, sems):
    run_copies(
        [
            pltpu.make_async_copy(
                piece,
                whole_ref.at[pl.ds(pl.multiple_of(from_ref[r] * ROWS, ROWS), ROWS), :],
                sems.at[r],
            )
            for r, piece in enumerate(arrived(piece_refs))
        ]
    )


def by_step(i, body):
    for v in range(BLOCKS // 2):
        pl.when(i == v)(functools.partial(body, v))


def window(block):
    count = min(block + 1, MOST)
    return count, (block + 1 - count) * ROWS


def block_probs(block, lens_ref, r_ref, pt_ref):
    first = block * ROWS
    count, lower = window(block)
    queries = stacked(r_ref[first : first + ROWS, 0:QW])
    lane = lax.broadcasted_iota(jnp.int32, (1, GROUP * ROWS), 1)
    position = first + jnp.bitwise_and(lane, ROWS - 1)
    start = jnp.zeros_like(position)
    end = jnp.int32(0)
    for k in range(DOCS):
        length = lens_ref[0, k]
        end = end + length
        start = start + jnp.where(position >= end, length, 0)
    row = lax.broadcasted_iota(jnp.int32, (ROWS, GROUP * ROWS), 0)
    first_row = start - lower
    last_row = position - lower
    scores = []
    highest = None
    for b in range(count):
        keys = r_ref[lower + b * ROWS : lower + (b + 1) * ROWS, 2 * QW :]
        tile = lax.dot_general(keys, queries, (((1,), (1,)), ((), ())), preferred_element_type=F32)
        allowed = row >= first_row - b * ROWS
        if b == count - 1:
            allowed = allowed & (row <= last_row - b * ROWS)
        tile = jnp.where(allowed, tile, NEG)
        top = jnp.max(tile, axis=0, keepdims=True)
        highest = top if highest is None else jnp.maximum(highest, top)
        scores.append(tile)
    total = None
    weights = []
    for tile in scores:
        weight = jnp.exp2((tile - highest) * (SCALE * math.log2(math.e)))
        part = jnp.sum(weight, axis=0, keepdims=True)
        total = part if total is None else total + part
        weights.append(weight)
    inverse = 1.0 / total
    for b in range(count):
        pt_ref[b * ROWS : (b + 1) * ROWS, :] = (weights[b] * inverse).astype(BF16)


def probs_kernel(lens_ref, from_ref, *refs):
    pieces, (pt_ref, gv_ref, r_ref, acc_ref, sems) = refs[:5], refs[5:]
    i = pl.program_id(0)

    @pl.when(i == 0)
    def _():
        gather_pieces(from_ref, pieces, r_ref, sems)
        acc_ref[...] = jnp.zeros_like(acc_ref)

    def body(v):
        for n, block in enumerate((v, v + MOST)):
            block_probs(block, lens_ref, r_ref, pt_ref.at[0, n])
        for n, block in enumerate((v, v + MOST)):
            count, lower = window(block)
            cot = stacked(r_ref[block * ROWS : (block + 1) * ROWS, QW : 2 * QW])
            size = count * ROWS
            acc_ref[lower : lower + size, :] += dot(pt_ref[0, n, 0:size, :], cot)

    by_step(i, body)

    @pl.when(i == BLOCKS // 2 - 1)
    def _():
        gv_ref[...] = acc_ref[...].astype(BF16)


PROBS_SHAPE = (BLOCKS // 2, 2, MOST * ROWS, GROUP * ROWS)
PROBS_SPEC = pl.BlockSpec((1,) + PROBS_SHAPE[1:], lambda i: (i, 0, 0, 0))


def probs_call(doc_lens, origin, pieces):
    width = 2 * QW + HD
    return pl.pallas_call(
        probs_kernel,
        grid=(BLOCKS // 2,),
        in_specs=[SCALARS, SCALARS] + [ANYWHERE] * 5,
        out_specs=[PROBS_SPEC, pl.BlockSpec((SEQ, HD), lambda i: (0, 0))],
        out_shape=[
            jax.ShapeDtypeStruct(PROBS_SHAPE, BF16),
            jax.ShapeDtypeStruct((SEQ, HD), BF16),
        ],
        scratch_shapes=[
            pltpu.VMEM((SEQ, width), BF16),
            pltpu.VMEM((SEQ, HD), F32),
            pltpu.SemaphoreType.DMA((8,)),
        ],
        compiler_params=params(),
    )(doc_lens, origin, *pieces)


def join(refs):
    return jnp.concatenate([ref[...] for ref in refs], axis=0)


def term_kernel(from_ref, *refs):
    hidden_refs, (gv_ref, term_ref, gvt_ref) = refs[:10], refs[10:]

    @pl.when(pl.program_id(0) == 0)
    def _():
        for r in range(8):
            rows = pl.ds(pl.multiple_of(from_ref[r] * ROWS, ROWS), ROWS)
            gvt_ref[:, r * ROWS : (r + 1) * ROWS] = gv_ref[rows, :].T

    term = dot(gvt_ref[...], join(hidden_refs))
    term_ref[...] = (term.T * INV_WIDTH).astype(BF16)


def values_kernel(from_ref, *refs):
    hidden_refs, (w_ref, val_ref, acc_ref) = refs[:10], refs[10:]
    j = pl.program_id(0)

    @pl.when(j == 0)
    def _():
        acc_ref[...] = jnp.zeros_like(acc_ref)

    acc_ref[...] += dot(join(hidden_refs), w_ref[...])

    @pl.when(j == pl.num_programs(0) - 1)
    def _():
        for r in range(8):
            rows = pl.ds(pl.multiple_of(from_ref[r] * ROWS, ROWS), ROWS)
            part = acc_ref[r * ROWS : (r + 1) * ROWS, :]
            val_ref[rows, :] = (part * INV_WIDTH).astype(BF16)


STRIPE = 1024


def hidden_specs(pieces):
    return [pl.BlockSpec((piece.shape[0], STRIPE), lambda j: (0, j)) for piece in pieces]


def term_call(origin, pieces, grad_values):
    return pl.pallas_call(
        term_kernel,
        grid=(D // STRIPE,),
        in_specs=[SCALARS]
        + hidden_specs(pieces)
        + [pl.BlockSpec((SEQ, HD), lambda j: (0, 0))],
        out_specs=pl.BlockSpec((STRIPE, HD), lambda j: (j, 0)),
        out_shape=jax.ShapeDtypeStruct((D, HD), BF16),
        scratch_shapes=[pltpu.VMEM((HD, SEQ), BF16)],
        compiler_params=params(),
    )(origin, *pieces, grad_values)


def values_call(origin, pieces, weight):
    return pl.pallas_call(
        values_kernel,
        grid=(D // STRIPE,),
        in_specs=[SCALARS]
        + hidden_specs(pieces)
        + [pl.BlockSpec((STRIPE, HD), lambda j: (j, 0))],
        out_specs=pl.BlockSpec((SEQ, HD), lambda j: (0, 0)),
        out_shape=jax.ShapeDtypeStruct((SEQ, HD), BF16),
        scratch_shapes=[pltpu.VMEM((SEQ, HD), F32)],
        compiler_params=params(),
    )(origin, *pieces, weight)


def block_grads(block, r_ref, pt_ref, val_ref, out_ref, acc_ref, kt_ref, vt_ref):
    first = block * ROWS
    count, lower = window(block)
    size = count * ROWS
    queries = stacked(r_ref[first : first + ROWS, 0:QW])
    cot_t = stacked(r_ref[first : first + ROWS, QW : 2 * QW]).T
    attn_t = dot(vt_ref[:, lower : lower + size], pt_ref[0:size, :]).astype(BF16)
    delta = jnp.sum(attn_t.astype(F32) * cot_t.astype(F32), axis=0, keepdims=True)
    prob_grad = dot(val_ref[lower : lower + size, :], cot_t)
    probs = pt_ref[0:size, :].astype(F32)
    score_grad = (probs * (prob_grad - delta)).astype(BF16)
    acc_ref[lower : lower + size, :] += dot(score_grad, queries)
    grad_t = dot(kt_ref[:, lower : lower + size], score_grad) * SCALE
    grad = grad_t.T.astype(BF16)
    for a in range(GROUP):
        out_ref[first : first + ROWS, a * HD : (a + 1) * HD] = grad[a * ROWS : (a + 1) * ROWS, :]


def grads_kernel(from_ref, to_ref, *refs):
    pieces, (pt_ref, val_ref), outs = refs[:5], refs[5:7], refs[7 : 7 + XS]
    r_ref, out_ref, acc_ref, kt_ref, vt_ref, sems = refs[7 + XS :]
    i = pl.program_id(0)

    @pl.when(i == 0)
    def _():
        gather_pieces(from_ref, pieces, r_ref, sems)
        acc_ref[...] = jnp.zeros_like(acc_ref)
        kt_ref[...] = r_ref[:, 2 * QW :].T
        vt_ref[...] = val_ref[...].T

    def body(v):
        for n, block in enumerate((v, v + MOST)):
            block_grads(block, r_ref, pt_ref.at[0, n], val_ref, out_ref, acc_ref, kt_ref, vt_ref)

    by_step(i, body)

    @pl.when(i == BLOCKS // 2 - 1)
    def _():
        out_ref[:, QW:] = (acc_ref[...] * SCALE).astype(BF16)
        run_copies(
            [
                pltpu.make_async_copy(
                    out_ref.at[pl.ds(pl.multiple_of(to_ref[r] * ROWS, ROWS), ROWS), :],
                    outs[r // 2].at[r % 2],
                    sems.at[r],
                )
                for r in range(8)
            ]
        )


def grads_call(origin, to, pieces, probs, values):
    width = 2 * QW + HD
    return pl.pallas_call(
        grads_kernel,
        grid=(BLOCKS // 2,),
        in_specs=[SCALARS, SCALARS]
        + [ANYWHERE] * 5
        + [PROBS_SPEC, pl.BlockSpec((SEQ, HD), lambda i: (0, 0))],
        out_specs=[ANYWHERE] * XS,
        out_shape=[jax.ShapeDtypeStruct((2, ROWS, QW + HD), BF16)] * XS,
        scratch_shapes=[
            pltpu.VMEM((SEQ, width), BF16),
            pltpu.VMEM((SEQ, QW + HD), BF16),
            pltpu.VMEM((SEQ, HD), F32),
            pltpu.VMEM((HD, SEQ), BF16),
            pltpu.VMEM((HD, SEQ), BF16),
            pltpu.SemaphoreType.DMA((8,)),
        ],
        compiler_params=params(),
    )(origin, to, *pieces, probs, values)


def unpack_kernel(from_ref, *refs):
    pieces, (q_ref, k_ref, sems) = refs[:5], refs[5:]
    copies = []
    for r, piece in enumerate(arrived(pieces)):
        j = from_ref[r]
        wide = pl.ds(pl.multiple_of(j * QW, QW), QW)
        thin = pl.ds(pl.multiple_of(j * HD, HD), HD)
        copies.append(
            pltpu.make_async_copy(piece.at[:, pl.ds(0, QW)], q_ref.at[:, wide], sems.at[2 * r])
        )
        copies.append(
            pltpu.make_async_copy(piece.at[:, pl.ds(QW, HD)], k_ref.at[:, thin], sems.at[2 * r + 1])
        )
    run_copies(copies)


def unpack(origin, pieces):
    return pl.pallas_call(
        unpack_kernel,
        in_specs=[SCALARS] + [ANYWHERE] * 5,
        out_specs=[ANYWHERE] * 2,
        out_shape=[
            jax.ShapeDtypeStruct((ROWS, 8 * QW), BF16),
            jax.ShapeDtypeStruct((ROWS, 8 * HD), BF16),
        ],
        scratch_shapes=[pltpu.SemaphoreType.DMA((16,))],
        compiler_params=params(4),
    )(origin, *pieces)


def adam_kernel(
    parts_ref,
    master_ref,
    mc_ref,
    ms_ref,
    vc_ref,
    vs_ref,
    master_out,
    mc_out,
    ms_out,
    vc_out,
    vs_out,
    grad_ref,
    mold_ref,
    vold_ref,
    step_ref,
    mcode_ref,
    vcode_ref,
):
    total = jnp.zeros(grad_ref.shape, F32)
    for g in range(parts_ref.shape[0]):
        total = total + parts_ref[g].astype(F32)
    grad_ref[...] = total
    mold_ref[...] = mc_ref[...].astype(F32)
    vold_ref[...] = vc_ref[...].astype(F32)
    half = grad_ref.shape[0] // 2
    first_fix = 1.0 - 0.9**STEP
    second_fix = 1.0 - 0.999**STEP
    news = []
    for odd in range(2):
        rows = pl.ds(odd, half, stride=2)
        grad = grad_ref[rows, :]
        m_new = 0.9 * (mold_ref[rows, :] * ms_ref[...]) + 0.1 * grad
        v_new = 0.999 * (vold_ref[rows, :] * vs_ref[...]) + 0.001 * grad * grad
        step_ref[rows, :] = m_new / first_fix / (jnp.sqrt(v_new / second_fix) + 1e-08)
        news.append((m_new, v_new))
    m_top = jnp.maximum(
        jnp.max(jnp.abs(news[0][0]), axis=1, keepdims=True),
        jnp.max(jnp.abs(news[1][0]), axis=1, keepdims=True),
    )
    v_top = jnp.maximum(
        jnp.max(jnp.abs(news[0][1]), axis=1, keepdims=True),
        jnp.max(jnp.abs(news[1][1]), axis=1, keepdims=True),
    )
    ms_out[...] = m_top
    vs_out[...] = v_top
    for odd in range(2):
        rows = pl.ds(odd, half, stride=2)
        mcode_ref[rows, :] = news[odd][0] / (m_top + 1e-06)
        vcode_ref[rows, :] = news[odd][1] / (v_top + 1e-06)
    mc_out[...] = mcode_ref[...].astype(BF16)
    vc_out[...] = vcode_ref[...].astype(BF16)
    master_out[...] = master_ref[...] - 0.01 * step_ref[...]


def adam_call(parts, master, m_code, m_scale, v_code, v_scale):
    shape = master.shape
    return pl.pallas_call(
        adam_kernel,
        out_shape=[
            jax.ShapeDtypeStruct(shape, F32),
            jax.ShapeDtypeStruct(shape, BF16),
            jax.ShapeDtypeStruct(m_scale.shape, F32),
            jax.ShapeDtypeStruct(shape, BF16),
            jax.ShapeDtypeStruct(v_scale.shape, F32),
        ],
        scratch_shapes=[pltpu.VMEM(shape, F32) for _ in range(6)],
        compiler_params=params(16),
    )(parts, master, m_code, m_scale, v_code, v_scale)


def shards(hidden, query, key, grad_out, doc_lens, master, m_code, m_scale, v_code, v_scale):
    n_dp = lax.axis_size("dp")
    me = lax.axis_index("seq")
    to = jnp.stack([place(me, r // 2, r % 2) for r in range(8)])
    origin = jnp.stack([place(me, (XS - r // 2) % XS, r % 2) for r in range(8)])
    around = jnp.stack([place(me, dx, dc) for dx in (0, 3, 1, 2) for dc in (0, 1)])
    own = hidden[0]
    half = own.shape[0] // 2
    left, right = send(own, 1, 0), send(own, 3, 0)
    pairs = pack(to, query[0], grad_out[0], key[0])
    pieces = exchange(pairs)
    master_bf, _ = lax.optimization_barrier((master.astype(BF16), pairs[0]))
    copies = jnp.broadcast_to(master_bf[None], (n_dp,) + master.shape)
    weight = lax.all_to_all(copies, "dp", split_axis=0, concat_axis=0, tiled=True)
    weight = weight.reshape(D, HD)
    far_lo, far_hi = send(left[:half], 1, 0), send(right[half:], 3, 0)
    own_core, left_core, right_core = send(own, 0, 1), send(left, 0, 1), send(right, 0, 1)
    probs, grad_values = probs_call(doc_lens, origin, pieces)

    far_core = [send(far_lo, 0, 1), send(far_hi, 0, 1)]
    hiddens = [own, own_core, left, left_core, right, right_core, far_lo, far_hi] + far_core
    term = term_call(around, hiddens, grad_values)
    parts = lax.all_to_all(
        term.reshape((n_dp,) + master.shape), "dp", split_axis=0, concat_axis=0, tiled=True
    )
    values = values_call(around, hiddens, weight)
    grads = grads_call(origin, to, pieces, probs, values)
    grad_query, grad_key = unpack(origin, exchange(grads))
    state = adam_call(parts, master, m_code, m_scale, v_code, v_scale)
    return (grad_query[None], grad_key[None]) + tuple(state)


def solution(mesh):
    return jax.shard_map(
        shards,
        mesh=mesh,
        in_specs=(
            P("dp", "seq", None),
            P("dp", "seq", None),
            P("dp", "seq", None),
            P("dp", "seq", None),
            P("dp", None),
            P("dp", "seq"),
            P("dp", "seq"),
            P("dp", "seq"),
            P("dp", "seq"),
            P("dp", "seq"),
        ),
        out_specs=(
            P("dp", "seq", None),
            P("dp", "seq", None),
            P("dp", "seq"),
            P("dp", "seq"),
            P("dp", "seq"),
            P("dp", "seq"),
            P("dp", "seq"),
        ),
        check_vma=False,
    )
```

```python
import functools
import math

import jax
import jax.numpy as jnp
from jax import lax
from jax.experimental import pallas as pl
from jax.experimental.pallas import tpu as pltpu
from jax.sharding import Mesh
from jax.sharding import PartitionSpec as P

D = 4096
HD = 128
DOCS = 8
STEP = 1000
SEQ = 1024
GROUP = 4
QW = GROUP * HD
ROWS = 128
BLOCKS = SEQ // ROWS
MOST = 4
NEG = -1e30
INV_WIDTH = 1.0 / math.sqrt(D)
SCALE = 1.0 / math.sqrt(HD)
F32 = jnp.float32
BF16 = jnp.bfloat16


def dot(a, b):
    return jnp.dot(a, b, preferred_element_type=F32)


def stacked(block):
    return jnp.concatenate([block[:, a * HD : (a + 1) * HD] for a in range(GROUP)], axis=0)


def params(mebibytes=24):
    return pltpu.CompilerParams(vmem_limit_bytes=mebibytes * 1024 * 1024)


def cost(microseconds):
    return pl.CostEstimate(
        flops=int(microseconds * 1e9), bytes_accessed=int(microseconds * 1e6), transcendentals=0
    )


XS = 4


def place(value, dx, dc):
    chip = lax.rem(lax.div(value, 2) + dx, XS)
    return chip * 2 + jnp.bitwise_xor(lax.rem(value, 2), dc)


def send(array, dx, dc):
    pairs = [(s, ((s // 2 + dx) % XS) * 2 + ((s % 2) ^ dc)) for s in range(2 * XS)]
    return lax.ppermute(array, "seq", pairs)


ANYWHERE = pl.BlockSpec(memory_space=pl.ANY)
SCALARS = pl.BlockSpec(memory_space=pltpu.SMEM)


def run_copies(copies):
    for copy in copies:
        copy.start()
    for copy in copies:
        copy.wait()


def pack_kernel(to_ref, q_ref, c_ref, k_ref, *refs):
    outs, sems = refs[:-1], refs[-1]
    copies = []
    for r in range(8):
        out = outs[r // 2].at[r % 2]
        j = to_ref[r]
        wide = pl.ds(pl.multiple_of(j * QW, QW), QW)
        thin = pl.ds(pl.multiple_of(j * HD, HD), HD)
        for n, (src, lanes, into) in enumerate(
            [
                (q_ref, wide, pl.ds(0, QW)),
                (c_ref, wide, pl.ds(QW, QW)),
                (k_ref, thin, pl.ds(2 * QW, HD)),
            ]
        ):
            copies.append(
                pltpu.make_async_copy(src.at[:, lanes], out.at[:, into], sems.at[3 * r + n])
            )
    run_copies(copies)


def pack(to, query, cot, key):
    tokens = query.shape[0]
    return pl.pallas_call(
        pack_kernel,
        in_specs=[SCALARS] + [pl.BlockSpec(memory_space=pltpu.VMEM)] * 3,
        out_specs=[ANYWHERE] * XS,
        out_shape=[jax.ShapeDtypeStruct((2, tokens, 2 * QW + HD), BF16)] * XS,
        scratch_shapes=[pltpu.SemaphoreType.DMA((24,))],
        cost_estimate=cost(3),
        compiler_params=params(60),
    )(to, query, cot, key)


def merge_kernel(*refs):
    pairs, out, sems = refs[:XS], refs[XS], refs[XS + 1]
    run_copies(
        [pltpu.make_async_copy(pair.at[1], out.at[r], sems.at[r]) for r, pair in enumerate(pairs)]
    )


def merge(pairs):
    return pl.pallas_call(
        merge_kernel,
        in_specs=[ANYWHERE] * XS,
        out_specs=ANYWHERE,
        out_shape=jax.ShapeDtypeStruct((XS,) + pairs[0].shape[1:], BF16),
        scratch_shapes=[pltpu.SemaphoreType.DMA((XS,))],
        cost_estimate=cost(1),
        compiler_params=params(4),
    )(*pairs)


def exchange(pairs):
    got = [pairs[0]] + [send(pairs[dx], dx, 0) for dx in (1, 3, 2)]
    got = [got[0], got[1], got[3], got[2]]
    return got + [send(merge(got), 0, 1)]


def arrived(refs):
    return [refs[r // 2].at[0] if r % 2 == 0 else refs[XS].at[r // 2] for r in range(8)]


def gather_pieces(from_ref, piece_refs, whole_ref, sems):
    run_copies(
        [
            pltpu.make_async_copy(
                piece,
                whole_ref.at[pl.ds(pl.multiple_of(from_ref[r] * ROWS, ROWS), ROWS), :],
                sems.at[r],
            )
            for r, piece in enumerate(arrived(piece_refs))
        ]
    )


def by_step(i, body):
    for v in range(BLOCKS // 2):
        pl.when(i == v)(functools.partial(body, v))


def window(block):
    count = min(block + 1, MOST)
    return count, (block + 1 - count) * ROWS


def block_probs(block, lens_ref, r_ref, pt_ref):
    first = block * ROWS
    count, lower = window(block)
    queries = stacked(r_ref[first : first + ROWS, 0:QW])
    lane = lax.broadcasted_iota(jnp.int32, (1, GROUP * ROWS), 1)
    position = first + jnp.bitwise_and(lane, ROWS - 1)
    start = jnp.zeros_like(position)
    end = jnp.int32(0)
    for k in range(DOCS):
        length = lens_ref[0, k]
        end = end + length
        start = start + jnp.where(position >= end, length, 0)
    row = lax.broadcasted_iota(jnp.int32, (ROWS, GROUP * ROWS), 0)
    first_row = start - lower
    last_row = position - lower
    scores = []
    highest = None
    for b in range(count):
        keys = r_ref[lower + b * ROWS : lower + (b + 1) * ROWS, 2 * QW :]
        tile = lax.dot_general(keys, queries, (((1,), (1,)), ((), ())), preferred_element_type=F32)
        allowed = row >= first_row - b * ROWS
        if b == count - 1:
            allowed = allowed & (row <= last_row - b * ROWS)
        tile = jnp.where(allowed, tile, NEG)
        top = jnp.max(tile, axis=0, keepdims=True)
        highest = top if highest is None else jnp.maximum(highest, top)
        scores.append(tile)
    total = None
    weights = []
    for tile in scores:
        weight = jnp.exp2((tile - highest) * (SCALE * math.log2(math.e)))
        part = jnp.sum(weight, axis=0, keepdims=True)
        total = part if total is None else total + part
        weights.append(weight)
    inverse = 1.0 / total
    for b in range(count):
        pt_ref[b * ROWS : (b + 1) * ROWS, :] = (weights[b] * inverse).astype(BF16)


def probs_kernel(lens_ref, from_ref, *refs):
    pieces, (pt_ref, gv_ref, r_ref, acc_ref, sems) = refs[:5], refs[5:]
    i = pl.program_id(0)

    @pl.when(i == 0)
    def _():
        gather_pieces(from_ref, pieces, r_ref, sems)
        acc_ref[...] = jnp.zeros_like(acc_ref)

    def body(v):
        for n, block in enumerate((v, v + MOST)):
            block_probs(block, lens_ref, r_ref, pt_ref.at[0, n])
        for n, block in enumerate((v, v + MOST)):
            count, lower = window(block)
            cot = stacked(r_ref[block * ROWS : (block + 1) * ROWS, QW : 2 * QW])
            size = count * ROWS
            acc_ref[lower : lower + size, :] += dot(pt_ref[0, n, 0:size, :], cot)

    by_step(i, body)

    @pl.when(i == BLOCKS // 2 - 1)
    def _():
        gv_ref[...] = acc_ref[...].astype(BF16)


PROBS_SHAPE = (BLOCKS // 2, 2, MOST * ROWS, GROUP * ROWS)
PROBS_SPEC = pl.BlockSpec((1,) + PROBS_SHAPE[1:], lambda i: (i, 0, 0, 0))


def probs_call(doc_lens, origin, pieces):
    width = 2 * QW + HD
    return pl.pallas_call(
        probs_kernel,
        grid=(BLOCKS // 2,),
        in_specs=[SCALARS, SCALARS] + [ANYWHERE] * 5,
        out_specs=[PROBS_SPEC, pl.BlockSpec((SEQ, HD), lambda i: (0, 0))],
        out_shape=[
            pltpu.HBM(PROBS_SHAPE, BF16),
            jax.ShapeDtypeStruct((SEQ, HD), BF16),
        ],
        scratch_shapes=[
            pltpu.VMEM((SEQ, width), BF16),
            pltpu.VMEM((SEQ, HD), F32),
            pltpu.SemaphoreType.DMA((8,)),
        ],
        cost_estimate=cost(8),
        compiler_params=params(),
    )(doc_lens, origin, *pieces)


def join(refs):
    return jnp.concatenate([ref[...] for ref in refs], axis=0)


def term_kernel(from_ref, *refs):
    hidden_refs, (gv_ref, term_ref, gvt_ref) = refs[:10], refs[10:]

    @pl.when(pl.program_id(0) == 0)
    def _():
        for r in range(8):
            rows = pl.ds(pl.multiple_of(from_ref[r] * ROWS, ROWS), ROWS)
            gvt_ref[:, r * ROWS : (r + 1) * ROWS] = gv_ref[rows, :].T

    term = dot(gvt_ref[...], join(hidden_refs))
    term_ref[...] = (term.T * INV_WIDTH).astype(BF16)


def values_kernel(*refs):
    hidden_refs, (w_ref, val_ref, acc_ref) = refs[:-3], refs[-3:]
    j = pl.program_id(0)

    @pl.when(j == 0)
    def _():
        acc_ref[...] = jnp.zeros_like(acc_ref)

    acc_ref[...] += dot(join(hidden_refs), w_ref[...])

    @pl.when(j == pl.num_programs(0) - 1)
    def _():
        val_ref[...] = (acc_ref[...] * INV_WIDTH).astype(BF16)


STRIPE = 1024


def hidden_specs(pieces):
    return [pl.BlockSpec((piece.shape[0], STRIPE), lambda j: (0, j)) for piece in pieces]


def term_call(origin, pieces, grad_values):
    return pl.pallas_call(
        term_kernel,
        grid=(D // STRIPE,),
        in_specs=[SCALARS]
        + hidden_specs(pieces)
        + [pl.BlockSpec((SEQ, HD), lambda j: (0, 0))],
        out_specs=pl.BlockSpec((STRIPE, HD), lambda j: (j, 0)),
        out_shape=jax.ShapeDtypeStruct((D, HD), BF16),
        scratch_shapes=[pltpu.VMEM((HD, SEQ), BF16)],
        cost_estimate=cost(5),
        compiler_params=params(),
    )(origin, *pieces, grad_values)


def values_call(pieces, weight):
    rows = sum(piece.shape[0] for piece in pieces)
    return pl.pallas_call(
        values_kernel,
        grid=(D // STRIPE,),
        in_specs=hidden_specs(pieces) + [pl.BlockSpec((STRIPE, HD), lambda j: (j, 0))],
        out_specs=pl.BlockSpec((rows, HD), lambda j: (0, 0)),
        out_shape=jax.ShapeDtypeStruct((rows, HD), BF16),
        scratch_shapes=[pltpu.VMEM((rows, HD), F32)],
        cost_estimate=cost(rows * 6 // SEQ),
        compiler_params=params(),
    )(*pieces, weight)


def block_grads(block, r_ref, pt_ref, val_ref, out_ref, acc_ref, kt_ref, vt_ref):
    first = block * ROWS
    count, lower = window(block)
    size = count * ROWS
    queries = stacked(r_ref[first : first + ROWS, 0:QW])
    cot_t = stacked(r_ref[first : first + ROWS, QW : 2 * QW]).T
    attn_t = dot(vt_ref[:, lower : lower + size], pt_ref[0:size, :]).astype(BF16)
    delta = jnp.sum(attn_t.astype(F32) * cot_t.astype(F32), axis=0, keepdims=True)
    prob_grad = dot(val_ref[lower : lower + size, :], cot_t)
    probs = pt_ref[0:size, :].astype(F32)
    score_grad = (probs * (prob_grad - delta)).astype(BF16)
    acc_ref[lower : lower + size, :] += dot(score_grad, queries)
    grad_t = dot(kt_ref[:, lower : lower + size], score_grad) * SCALE
    grad = grad_t.T.astype(BF16)
    for a in range(GROUP):
        out_ref[first : first + ROWS, a * HD : (a + 1) * HD] = grad[a * ROWS : (a + 1) * ROWS, :]


def grads_kernel(from_ref, to_ref, around_ref, *refs):
    pieces, (pt_ref, near_ref, far_ref), outs = refs[:5], refs[5:8], refs[8 : 8 + XS]
    r_ref, val_ref, out_ref, acc_ref, kt_ref, vt_ref, sems = refs[8 + XS :]
    i = pl.program_id(0)

    @pl.when(i == 0)
    def _():
        gather_pieces(from_ref, pieces, r_ref, sems)
        acc_ref[...] = jnp.zeros_like(acc_ref)
        kt_ref[...] = r_ref[:, 2 * QW :].T
        for r in range(8):
            rows = pl.ds(pl.multiple_of(around_ref[r] * ROWS, ROWS), ROWS)
            held, at = (near_ref, r) if r < 6 else (far_ref, r - 6)
            val_ref[rows, :] = held[at * ROWS : (at + 1) * ROWS, :]
        vt_ref[...] = val_ref[...].T

    def body(v):
        for n, block in enumerate((v, v + MOST)):
            block_grads(block, r_ref, pt_ref.at[0, n], val_ref, out_ref, acc_ref, kt_ref, vt_ref)

    by_step(i, body)

    @pl.when(i == BLOCKS // 2 - 1)
    def _():
        out_ref[:, QW:] = (acc_ref[...] * SCALE).astype(BF16)
        run_copies(
            [
                pltpu.make_async_copy(
                    out_ref.at[pl.ds(pl.multiple_of(to_ref[r] * ROWS, ROWS), ROWS), :],
                    outs[r // 2].at[r % 2],
                    sems.at[r],
                )
                for r in range(8)
            ]
        )


def grads_call(origin, to, around, pieces, probs, near, far):
    width = 2 * QW + HD
    return pl.pallas_call(
        grads_kernel,
        grid=(BLOCKS // 2,),
        in_specs=[SCALARS, SCALARS, SCALARS]
        + [ANYWHERE] * 5
        + [
            PROBS_SPEC,
            pl.BlockSpec(near.shape, lambda i: (0, 0)),
            pl.BlockSpec(far.shape, lambda i: (0, 0)),
        ],
        out_specs=[ANYWHERE] * XS,
        out_shape=[jax.ShapeDtypeStruct((2, ROWS, QW + HD), BF16)] * XS,
        scratch_shapes=[
            pltpu.VMEM((SEQ, width), BF16),
            pltpu.VMEM((SEQ, HD), BF16),
            pltpu.VMEM((SEQ, QW + HD), BF16),
            pltpu.VMEM((SEQ, HD), F32),
            pltpu.VMEM((HD, SEQ), BF16),
            pltpu.VMEM((HD, SEQ), BF16),
            pltpu.SemaphoreType.DMA((8,)),
        ],
        cost_estimate=cost(9),
        compiler_params=params(),
    )(origin, to, around, *pieces, probs, near, far)


def unpack_kernel(from_ref, *refs):
    pieces, (q_ref, k_ref, sems) = refs[:5], refs[5:]
    copies = []
    for r, piece in enumerate(arrived(pieces)):
        j = from_ref[r]
        wide = pl.ds(pl.multiple_of(j * QW, QW), QW)
        thin = pl.ds(pl.multiple_of(j * HD, HD), HD)
        copies.append(
            pltpu.make_async_copy(piece.at[:, pl.ds(0, QW)], q_ref.at[:, wide], sems.at[2 * r])
        )
        copies.append(
            pltpu.make_async_copy(piece.at[:, pl.ds(QW, HD)], k_ref.at[:, thin], sems.at[2 * r + 1])
        )
    run_copies(copies)


def unpack(origin, pieces):
    return pl.pallas_call(
        unpack_kernel,
        in_specs=[SCALARS] + [ANYWHERE] * 5,
        out_specs=[ANYWHERE] * 2,
        out_shape=[
            jax.ShapeDtypeStruct((ROWS, 8 * QW), BF16),
            jax.ShapeDtypeStruct((ROWS, 8 * HD), BF16),
        ],
        scratch_shapes=[pltpu.SemaphoreType.DMA((16,))],
        cost_estimate=cost(2),
        compiler_params=params(4),
    )(origin, *pieces)


def add_kernel(parts_ref, out_ref):
    total = parts_ref[0].astype(F32)
    for g in range(1, parts_ref.shape[0]):
        total = total + parts_ref[g].astype(F32)
    out_ref[...] = total.astype(BF16)


def add_parts(parts):
    return pl.pallas_call(
        add_kernel,
        out_shape=jax.ShapeDtypeStruct(parts.shape[1:], BF16),
        cost_estimate=cost(1),
        compiler_params=params(8),
    )(parts)


def adam_kernel(
    parts_ref,
    master_ref,
    mc_ref,
    ms_ref,
    vc_ref,
    vs_ref,
    master_out,
    mc_out,
    ms_out,
    vc_out,
    vs_out,
    grad_ref,
    mold_ref,
    vold_ref,
    step_ref,
    mcode_ref,
    vcode_ref,
):
    total = jnp.zeros(grad_ref.shape, F32)
    for g in range(parts_ref.shape[0]):
        total = total + parts_ref[g].astype(F32)
    grad_ref[...] = total
    mold_ref[...] = mc_ref[...].astype(F32)
    vold_ref[...] = vc_ref[...].astype(F32)
    half = grad_ref.shape[0] // 2
    first_fix = 1.0 - 0.9**STEP
    second_fix = 1.0 - 0.999**STEP
    news = []
    for odd in range(2):
        rows = pl.ds(odd, half, stride=2)
        grad = grad_ref[rows, :]
        m_new = 0.9 * (mold_ref[rows, :] * ms_ref[...]) + 0.1 * grad
        v_new = 0.999 * (vold_ref[rows, :] * vs_ref[...]) + 0.001 * grad * grad
        step_ref[rows, :] = m_new / first_fix / (jnp.sqrt(v_new / second_fix) + 1e-08)
        news.append((m_new, v_new))
    m_top = jnp.maximum(
        jnp.max(jnp.abs(news[0][0]), axis=1, keepdims=True),
        jnp.max(jnp.abs(news[1][0]), axis=1, keepdims=True),
    )
    v_top = jnp.maximum(
        jnp.max(jnp.abs(news[0][1]), axis=1, keepdims=True),
        jnp.max(jnp.abs(news[1][1]), axis=1, keepdims=True),
    )
    ms_out[...] = m_top
    vs_out[...] = v_top
    for odd in range(2):
        rows = pl.ds(odd, half, stride=2)
        mcode_ref[rows, :] = news[odd][0] / (m_top + 1e-06)
        vcode_ref[rows, :] = news[odd][1] / (v_top + 1e-06)
    mc_out[...] = mcode_ref[...].astype(BF16)
    vc_out[...] = vcode_ref[...].astype(BF16)
    master_out[...] = master_ref[...] - 0.01 * step_ref[...]


def adam_call(parts, master, m_code, m_scale, v_code, v_scale):
    shape = master.shape
    return pl.pallas_call(
        adam_kernel,
        out_shape=[
            jax.ShapeDtypeStruct(shape, F32),
            jax.ShapeDtypeStruct(shape, BF16),
            jax.ShapeDtypeStruct(m_scale.shape, F32),
            jax.ShapeDtypeStruct(shape, BF16),
            jax.ShapeDtypeStruct(v_scale.shape, F32),
        ],
        scratch_shapes=[pltpu.VMEM(shape, F32) for _ in range(6)],
        cost_estimate=cost(2),
        compiler_params=params(16),
    )(parts, master, m_code, m_scale, v_code, v_scale)


def shards(hidden, query, key, grad_out, doc_lens, master, m_code, m_scale, v_code, v_scale):
    n_y, n_z = lax.axis_size("y"), lax.axis_size("z")
    me = lax.axis_index("seq")
    to = jnp.stack([place(me, r // 2, r % 2) for r in range(8)])
    origin = jnp.stack([place(me, (XS - r // 2) % XS, r % 2) for r in range(8)])
    around = jnp.stack([place(me, dx, dc) for dx in (0, 3, 1, 2) for dc in (0, 1)])
    own = hidden[0]
    half = own.shape[0] // 2
    left, right = send(own, 1, 0), send(own, 3, 0)
    pairs = pack(to, query[0], grad_out[0], key[0])
    pieces = exchange(pairs)
    master_bf, _ = lax.optimization_barrier((master.astype(BF16), pairs[0]))
    copies = jnp.broadcast_to(master_bf[None], (n_y * n_z,) + master.shape)
    weight = lax.all_to_all(copies, ("y", "z"), split_axis=0, concat_axis=0, tiled=True)
    weight = weight.reshape(n_y * n_z * master.shape[0], HD)
    far_lo, far_hi = send(left[:half], 1, 0), send(right[half:], 3, 0)
    own_core, left_core, right_core = send(own, 0, 1), send(left, 0, 1), send(right, 0, 1)
    probs, grad_values = probs_call(doc_lens, origin, pieces)
    near = [own, own_core, left, left_core, right, right_core]
    near_values = values_call(near, weight)
    far_lo, far_hi, grad_values, near_values = lax.optimization_barrier(
        (far_lo, far_hi, grad_values, near_values)
    )
    far = [far_lo, far_hi, send(far_lo, 0, 1), send(far_hi, 0, 1)]
    term = term_call(around, near + far, grad_values)
    parts = lax.all_to_all(
        term.reshape((n_y, n_z) + master.shape), "y", split_axis=0, concat_axis=0, tiled=True
    )
    parts = lax.all_to_all(add_parts(parts), "z", split_axis=0, concat_axis=0, tiled=True)
    far_values = values_call(far, weight)
    grads = grads_call(origin, to, around, pieces, probs, near_values, far_values)
    grad_query, grad_key = unpack(origin, exchange(grads))
    state = adam_call(parts, master, m_code, m_scale, v_code, v_scale)
    return (grad_query[None], grad_key[None]) + tuple(state)


def solution(mesh):
    tokens, state = P(("y", "z"), "seq", None), P(("y", "z"), "seq")
    rows = math.gcd(8, mesh.shape["dp"])
    cut = mesh.devices.reshape(mesh.shape["seq"], rows, mesh.shape["dp"] // rows)
    return jax.shard_map(
        shards,
        mesh=Mesh(cut, ("seq", "y", "z")),
        in_specs=(tokens,) * 4 + (P(("y", "z"), None),) + (state,) * 5,
        out_specs=(tokens,) * 2 + (state,) * 5,
        check_vma=False,
    )
```

```python
import functools
import math

import jax
import jax.numpy as jnp
from jax import lax
from jax.experimental import pallas as pl
from jax.experimental.pallas import tpu as pltpu
from jax.sharding import Mesh
from jax.sharding import PartitionSpec as P

D = 4096
HD = 128
DOCS = 8
STEP = 1000
SEQ = 1024
GROUP = 4
QW = GROUP * HD
ROWS = 128
BLOCKS = SEQ // ROWS
MOST = 4
NEG = -1e30
INV_WIDTH = 1.0 / math.sqrt(D)
SCALE = 1.0 / math.sqrt(HD)
F32 = jnp.float32
BF16 = jnp.bfloat16


def dot(a, b):
    return jnp.dot(a, b, preferred_element_type=F32)


def stacked(block):
    return jnp.concatenate([block[:, a * HD : (a + 1) * HD] for a in range(GROUP)], axis=0)


def params(mebibytes=24):
    return pltpu.CompilerParams(vmem_limit_bytes=mebibytes * 1024 * 1024)


def cost(microseconds):
    return pl.CostEstimate(
        flops=int(microseconds * 1e9), bytes_accessed=int(microseconds * 1e6), transcendentals=0
    )


XS = 4


def place(value, dx, dc):
    chip = lax.rem(lax.div(value, 2) + dx, XS)
    return chip * 2 + jnp.bitwise_xor(lax.rem(value, 2), dc)


def send(array, dx, dc):
    pairs = [(s, ((s // 2 + dx) % XS) * 2 + ((s % 2) ^ dc)) for s in range(2 * XS)]
    return lax.ppermute(array, "seq", pairs)


def turn(array, dx):
    pairs = [(s, ((s // 2 + (dx if s % 2 == 0 else -dx)) % XS) * 2 + s % 2) for s in range(2 * XS)]
    return lax.ppermute(array, "seq", pairs)


ANYWHERE = pl.BlockSpec(memory_space=pl.ANY)
SCALARS = pl.BlockSpec(memory_space=pltpu.SMEM)


def run_copies(copies):
    for copy in copies:
        copy.start()
    for copy in copies:
        copy.wait()


def pack_kernel(to_ref, q_ref, c_ref, k_ref, *refs):
    outs, sems = refs[:-1], refs[-1]
    copies = []
    for r in range(8):
        out = outs[r // 2].at[r % 2]
        j = to_ref[r]
        wide = pl.ds(pl.multiple_of(j * QW, QW), QW)
        thin = pl.ds(pl.multiple_of(j * HD, HD), HD)
        for n, (src, lanes, into) in enumerate(
            [
                (q_ref, wide, pl.ds(0, QW)),
                (c_ref, wide, pl.ds(QW, QW)),
                (k_ref, thin, pl.ds(2 * QW, HD)),
            ]
        ):
            copies.append(
                pltpu.make_async_copy(src.at[:, lanes], out.at[:, into], sems.at[3 * r + n])
            )
    run_copies(copies)


def pack(to, query, cot, key):
    tokens = query.shape[0]
    return pl.pallas_call(
        pack_kernel,
        in_specs=[SCALARS] + [pl.BlockSpec(memory_space=pltpu.VMEM)] * 3,
        out_specs=[ANYWHERE] * XS,
        out_shape=[jax.ShapeDtypeStruct((2, tokens, 2 * QW + HD), BF16)] * XS,
        scratch_shapes=[pltpu.SemaphoreType.DMA((24,))],
        cost_estimate=cost(3),
        compiler_params=params(60),
    )(to, query, cot, key)


def merge_kernel(*refs):
    pairs, out, sems = refs[:XS], refs[XS], refs[XS + 1]
    run_copies(
        [pltpu.make_async_copy(pair.at[1], out.at[r], sems.at[r]) for r, pair in enumerate(pairs)]
    )


def merge(pairs):
    return pl.pallas_call(
        merge_kernel,
        in_specs=[ANYWHERE] * XS,
        out_specs=pl.BlockSpec(memory_space=pltpu.VMEM),
        out_shape=jax.ShapeDtypeStruct((XS,) + pairs[0].shape[1:], BF16),
        scratch_shapes=[pltpu.SemaphoreType.DMA((XS,))],
        cost_estimate=cost(1),
        compiler_params=params(8),
    )(*pairs)


def along(pairs):
    return [pairs[0]] + [send(pairs[dx], dx, 0) for dx in range(1, XS)]


def across(got):
    return got + [send(merge(got), 0, 1)]


def arrived(refs):
    return [refs[r // 2].at[0] if r % 2 == 0 else refs[XS].at[r // 2] for r in range(8)]


def gather_pieces(from_ref, piece_refs, whole_ref, sems):
    run_copies(
        [
            pltpu.make_async_copy(
                piece,
                whole_ref.at[pl.ds(pl.multiple_of(from_ref[r] * ROWS, ROWS), ROWS), :],
                sems.at[r],
            )
            for r, piece in enumerate(arrived(piece_refs))
        ]
    )


def by_step(i, body):
    for v in range(BLOCKS // 2):
        pl.when(i == v)(functools.partial(body, v))


def window(block):
    count = min(block + 1, MOST)
    return count, (block + 1 - count) * ROWS


def block_probs(block, lens_ref, r_ref, pt_ref):
    first = block * ROWS
    count, lower = window(block)
    queries = stacked(r_ref[first : first + ROWS, 0:QW])
    lane = lax.broadcasted_iota(jnp.int32, (1, GROUP * ROWS), 1)
    position = first + jnp.bitwise_and(lane, ROWS - 1)
    start = jnp.zeros_like(position)
    end = jnp.int32(0)
    for k in range(DOCS):
        length = lens_ref[0, k]
        end = end + length
        start = start + jnp.where(position >= end, length, 0)
    row = lax.broadcasted_iota(jnp.int32, (ROWS, GROUP * ROWS), 0)
    first_row = start - lower
    last_row = position - lower
    scores = []
    highest = None
    for b in range(count):
        keys = r_ref[lower + b * ROWS : lower + (b + 1) * ROWS, 2 * QW :]
        tile = lax.dot_general(keys, queries, (((1,), (1,)), ((), ())), preferred_element_type=F32)
        allowed = row >= first_row - b * ROWS
        if b == count - 1:
            allowed = allowed & (row <= last_row - b * ROWS)
        tile = jnp.where(allowed, tile, NEG)
        top = jnp.max(tile, axis=0, keepdims=True)
        highest = top if highest is None else jnp.maximum(highest, top)
        scores.append(tile)
    total = None
    weights = []
    for tile in scores:
        weight = jnp.exp2((tile - highest) * (SCALE * math.log2(math.e)))
        part = jnp.sum(weight, axis=0, keepdims=True)
        total = part if total is None else total + part
        weights.append(weight)
    inverse = 1.0 / total
    for b in range(count):
        pt_ref[b * ROWS : (b + 1) * ROWS, :] = (weights[b] * inverse).astype(BF16)


def probs_kernel(lens_ref, from_ref, *refs):
    pieces, (pt_ref, gv_ref, r_ref, acc_ref, sems) = refs[:5], refs[5:]
    i = pl.program_id(0)

    @pl.when(i == 0)
    def _():
        gather_pieces(from_ref, pieces, r_ref, sems)
        acc_ref[...] = jnp.zeros_like(acc_ref)

    def body(v):
        for n, block in enumerate((v, v + MOST)):
            block_probs(block, lens_ref, r_ref, pt_ref.at[0, n])
        for n, block in enumerate((v, v + MOST)):
            count, lower = window(block)
            cot = stacked(r_ref[block * ROWS : (block + 1) * ROWS, QW : 2 * QW])
            size = count * ROWS
            acc_ref[lower : lower + size, :] += dot(pt_ref[0, n, 0:size, :], cot)

    by_step(i, body)

    @pl.when(i == BLOCKS // 2 - 1)
    def _():
        gv_ref[...] = acc_ref[...].astype(BF16)


PROBS_SHAPE = (BLOCKS // 2, 2, MOST * ROWS, GROUP * ROWS)
PROBS_SPEC = pl.BlockSpec((1,) + PROBS_SHAPE[1:], lambda i: (i, 0, 0, 0))


def probs_call(doc_lens, origin, pieces):
    width = 2 * QW + HD
    return pl.pallas_call(
        probs_kernel,
        grid=(BLOCKS // 2,),
        in_specs=[SCALARS, SCALARS] + [ANYWHERE] * 5,
        out_specs=[PROBS_SPEC, pl.BlockSpec((SEQ, HD), lambda i: (0, 0))],
        out_shape=[
            pltpu.HBM(PROBS_SHAPE, BF16),
            jax.ShapeDtypeStruct((SEQ, HD), BF16),
        ],
        scratch_shapes=[
            pltpu.VMEM((SEQ, width), BF16),
            pltpu.VMEM((SEQ, HD), F32),
            pltpu.SemaphoreType.DMA((8,)),
        ],
        cost_estimate=cost(8),
        compiler_params=params(),
    )(doc_lens, origin, *pieces)


def join(refs):
    return jnp.concatenate([ref[...] for ref in refs], axis=0)


def term_kernel(from_ref, *refs):
    hidden_refs, (gv_ref, term_ref, gvt_ref) = refs[:8], refs[8:]

    @pl.when(pl.program_id(0) == 0)
    def _():
        for r in range(8):
            rows = pl.ds(pl.multiple_of(from_ref[r] * ROWS, ROWS), ROWS)
            gvt_ref[:, r * ROWS : (r + 1) * ROWS] = gv_ref[rows, :].T

    term = dot(gvt_ref[...], join(hidden_refs))
    term_ref[...] = (term.T * INV_WIDTH).astype(BF16)


def values_kernel(*refs):
    hidden_refs, (w_ref, val_ref, acc_ref) = refs[:-3], refs[-3:]
    j = pl.program_id(0)

    @pl.when(j == 0)
    def _():
        acc_ref[...] = jnp.zeros_like(acc_ref)

    acc_ref[...] += dot(join(hidden_refs), w_ref[...])

    @pl.when(j == pl.num_programs(0) - 1)
    def _():
        val_ref[...] = (acc_ref[...] * INV_WIDTH).astype(BF16)


STRIPE = 1024


def hidden_specs(pieces):
    return [pl.BlockSpec((piece.shape[0], STRIPE), lambda j: (0, j)) for piece in pieces]


def term_call(origin, pieces, grad_values):
    return pl.pallas_call(
        term_kernel,
        grid=(D // STRIPE,),
        in_specs=[SCALARS]
        + hidden_specs(pieces)
        + [pl.BlockSpec((SEQ, HD), lambda j: (0, 0))],
        out_specs=pl.BlockSpec((STRIPE, HD), lambda j: (j, 0)),
        out_shape=jax.ShapeDtypeStruct((D, HD), BF16),
        scratch_shapes=[pltpu.VMEM((HD, SEQ), BF16)],
        cost_estimate=cost(5),
        compiler_params=params(),
    )(origin, *pieces, grad_values)


def values_call(pieces, weight):
    rows = sum(piece.shape[0] for piece in pieces)
    return pl.pallas_call(
        values_kernel,
        grid=(D // STRIPE,),
        in_specs=hidden_specs(pieces) + [pl.BlockSpec((STRIPE, HD), lambda j: (j, 0))],
        out_specs=pl.BlockSpec((rows, HD), lambda j: (0, 0)),
        out_shape=jax.ShapeDtypeStruct((rows, HD), BF16),
        scratch_shapes=[pltpu.VMEM((rows, HD), F32)],
        cost_estimate=cost(rows * 6 // SEQ),
        compiler_params=params(),
    )(*pieces, weight)


def block_grads(block, r_ref, pt_ref, val_ref, out_ref, acc_ref, kt_ref, vt_ref):
    first = block * ROWS
    count, lower = window(block)
    size = count * ROWS
    queries = stacked(r_ref[first : first + ROWS, 0:QW])
    cot_t = stacked(r_ref[first : first + ROWS, QW : 2 * QW]).T
    attn_t = dot(vt_ref[:, lower : lower + size], pt_ref[0:size, :]).astype(BF16)
    delta = jnp.sum(attn_t.astype(F32) * cot_t.astype(F32), axis=0, keepdims=True)
    prob_grad = dot(val_ref[lower : lower + size, :], cot_t)
    probs = pt_ref[0:size, :].astype(F32)
    score_grad = (probs * (prob_grad - delta)).astype(BF16)
    acc_ref[lower : lower + size, :] += dot(score_grad, queries)
    grad_t = dot(kt_ref[:, lower : lower + size], score_grad) * SCALE
    grad = grad_t.T.astype(BF16)
    for a in range(GROUP):
        out_ref[first : first + ROWS, a * HD : (a + 1) * HD] = grad[a * ROWS : (a + 1) * ROWS, :]


def grads_kernel(from_ref, to_ref, around_ref, *refs):
    pieces, (pt_ref, held_ref), outs = refs[:5], refs[5:7], refs[7 : 7 + XS]
    r_ref, val_ref, out_ref, acc_ref, kt_ref, vt_ref, sems = refs[7 + XS :]
    i = pl.program_id(0)

    @pl.when(i == 0)
    def _():
        gather_pieces(from_ref, pieces, r_ref, sems)
        acc_ref[...] = jnp.zeros_like(acc_ref)
        kt_ref[...] = r_ref[:, 2 * QW :].T
        for r in range(8):
            rows = pl.ds(pl.multiple_of(around_ref[r] * ROWS, ROWS), ROWS)
            val_ref[rows, :] = held_ref[r * ROWS : (r + 1) * ROWS, :]
        vt_ref[...] = val_ref[...].T

    def body(v):
        for n, block in enumerate((v, v + MOST)):
            block_grads(block, r_ref, pt_ref.at[0, n], val_ref, out_ref, acc_ref, kt_ref, vt_ref)

    by_step(i, body)

    @pl.when(i == BLOCKS // 2 - 1)
    def _():
        out_ref[:, QW:] = (acc_ref[...] * SCALE).astype(BF16)
        run_copies(
            [
                pltpu.make_async_copy(
                    out_ref.at[pl.ds(pl.multiple_of(to_ref[r] * ROWS, ROWS), ROWS), :],
                    outs[r // 2].at[r % 2],
                    sems.at[r],
                )
                for r in range(8)
            ]
        )


def grads_call(origin, to, around, pieces, probs, values):
    width = 2 * QW + HD
    return pl.pallas_call(
        grads_kernel,
        grid=(BLOCKS // 2,),
        in_specs=[SCALARS, SCALARS, SCALARS]
        + [ANYWHERE] * 5
        + [
            PROBS_SPEC,
            pl.BlockSpec((SEQ, HD), lambda i: (0, 0)),
        ],
        out_specs=[ANYWHERE] * XS,
        out_shape=[jax.ShapeDtypeStruct((2, ROWS, QW + HD), BF16)] * XS,
        scratch_shapes=[
            pltpu.VMEM((SEQ, width), BF16),
            pltpu.VMEM((SEQ, HD), BF16),
            pltpu.VMEM((SEQ, QW + HD), BF16),
            pltpu.VMEM((SEQ, HD), F32),
            pltpu.VMEM((HD, SEQ), BF16),
            pltpu.VMEM((HD, SEQ), BF16),
            pltpu.SemaphoreType.DMA((8,)),
        ],
        cost_estimate=cost(9),
        compiler_params=params(),
    )(origin, to, around, *pieces, probs, values)


def unpack_kernel(from_ref, *refs):
    pieces, (q_ref, k_ref, sems) = refs[:5], refs[5:]
    copies = []
    for r, piece in enumerate(arrived(pieces)):
        j = from_ref[r]
        wide = pl.ds(pl.multiple_of(j * QW, QW), QW)
        thin = pl.ds(pl.multiple_of(j * HD, HD), HD)
        copies.append(
            pltpu.make_async_copy(piece.at[:, pl.ds(0, QW)], q_ref.at[:, wide], sems.at[2 * r])
        )
        copies.append(
            pltpu.make_async_copy(piece.at[:, pl.ds(QW, HD)], k_ref.at[:, thin], sems.at[2 * r + 1])
        )
    run_copies(copies)


def unpack(origin, pieces):
    return pl.pallas_call(
        unpack_kernel,
        in_specs=[SCALARS] + [pl.BlockSpec(memory_space=pltpu.VMEM)] * 5,
        out_specs=[ANYWHERE] * 2,
        out_shape=[
            jax.ShapeDtypeStruct((ROWS, 8 * QW), BF16),
            jax.ShapeDtypeStruct((ROWS, 8 * HD), BF16),
        ],
        scratch_shapes=[pltpu.SemaphoreType.DMA((16,))],
        cost_estimate=cost(2),
        compiler_params=params(8),
    )(origin, *pieces)


def add_kernel(parts_ref, out_ref):
    total = parts_ref[0].astype(F32)
    for g in range(1, parts_ref.shape[0]):
        total = total + parts_ref[g].astype(F32)
    out_ref[...] = total.astype(BF16)


def add_parts(parts):
    return pl.pallas_call(
        add_kernel,
        out_shape=jax.ShapeDtypeStruct(parts.shape[1:], BF16),
        cost_estimate=cost(1),
        compiler_params=params(8),
    )(parts)


def adam_kernel(
    parts_ref,
    master_ref,
    mc_ref,
    ms_ref,
    vc_ref,
    vs_ref,
    master_out,
    mc_out,
    ms_out,
    vc_out,
    vs_out,
    grad_ref,
    mold_ref,
    vold_ref,
    step_ref,
    mcode_ref,
    vcode_ref,
):
    total = jnp.zeros(grad_ref.shape, F32)
    for g in range(parts_ref.shape[0]):
        total = total + parts_ref[g].astype(F32)
    grad_ref[...] = total
    mold_ref[...] = mc_ref[...].astype(F32)
    vold_ref[...] = vc_ref[...].astype(F32)
    half = grad_ref.shape[0] // 2
    first_fix = 1.0 - 0.9**STEP
    second_fix = 1.0 - 0.999**STEP
    news = []
    for odd in range(2):
        rows = pl.ds(odd, half, stride=2)
        grad = grad_ref[rows, :]
        m_new = 0.9 * (mold_ref[rows, :] * ms_ref[...]) + 0.1 * grad
        v_new = 0.999 * (vold_ref[rows, :] * vs_ref[...]) + 0.001 * grad * grad
        step_ref[rows, :] = m_new / first_fix / (jnp.sqrt(v_new / second_fix) + 1e-08)
        news.append((m_new, v_new))
    m_top = jnp.maximum(
        jnp.max(jnp.abs(news[0][0]), axis=1, keepdims=True),
        jnp.max(jnp.abs(news[1][0]), axis=1, keepdims=True),
    )
    v_top = jnp.maximum(
        jnp.max(jnp.abs(news[0][1]), axis=1, keepdims=True),
        jnp.max(jnp.abs(news[1][1]), axis=1, keepdims=True),
    )
    ms_out[...] = jnp.broadcast_to(m_top, (half, HD)).T[0:1, :]
    vs_out[...] = jnp.broadcast_to(v_top, (half, HD)).T[0:1, :]
    for odd in range(2):
        rows = pl.ds(odd, half, stride=2)
        mcode_ref[rows, :] = news[odd][0] / (m_top + 1e-06)
        vcode_ref[rows, :] = news[odd][1] / (v_top + 1e-06)
    mc_out[...] = mcode_ref[...].astype(BF16)
    vc_out[...] = vcode_ref[...].astype(BF16)
    master_out[...] = master_ref[...] - 0.01 * step_ref[...]


def adam_call(parts, master, m_code, m_scale, v_code, v_scale):
    shape = master.shape
    return pl.pallas_call(
        adam_kernel,
        out_shape=[
            jax.ShapeDtypeStruct(shape, F32),
            jax.ShapeDtypeStruct(shape, BF16),
            jax.ShapeDtypeStruct(m_scale.shape[::-1], F32),
            jax.ShapeDtypeStruct(shape, BF16),
            jax.ShapeDtypeStruct(v_scale.shape[::-1], F32),
        ],
        scratch_shapes=[pltpu.VMEM(shape, F32) for _ in range(6)],
        cost_estimate=cost(2),
        compiler_params=params(16),
    )(parts, master, m_code, m_scale, v_code, v_scale)


def shards(hidden, query, key, grad_out, doc_lens, master, m_code, m_scale, v_code, v_scale):
    n_y, n_z = lax.axis_size("y"), lax.axis_size("z")
    me = lax.axis_index("seq")
    to = jnp.stack([place(me, r // 2, r % 2) for r in range(8)])
    origin = jnp.stack([place(me, (XS - r // 2) % XS, r % 2) for r in range(8)])
    around = jnp.stack([place(me, dx, dc) for dx in (0, 3, 1, 2) for dc in (0, 1)])
    core = lax.rem(me, 2)
    ahead = jnp.where(core == 0, XS - 1, 1)
    own = hidden[0]
    first, second = turn(own, 1), turn(own, -1)
    around = jnp.stack(
        [
            me,
            place(me, 0, 1),
            place(me, ahead, 0),
            place(me, XS - ahead, 1),
            place(me, XS - ahead, 0),
            place(me, ahead, 1),
            place(me, 2, 0),
            place(me, 2, 1),
        ]
    )
    pairs = pack(to, query[0], grad_out[0], key[0])
    pieces = across(along(pairs))
    master_bf, _ = lax.optimization_barrier((master.astype(BF16), pairs[0]))
    copies = jnp.broadcast_to(master_bf[None], (n_y * n_z,) + master.shape)
    weight = lax.all_to_all(copies, ("y", "z"), split_axis=0, concat_axis=0, tiled=True)
    weight = weight.reshape(n_y * n_z * master.shape[0], HD)
    far = turn(first, 1)
    near = [own, send(own, 0, 1), first, send(first, 0, 1), second, send(second, 0, 1)]
    probs, grad_values = probs_call(doc_lens, origin, pieces)
    far, grad_values, weight, near[1], near[3], near[5] = lax.optimization_barrier(
        (far, grad_values, weight, near[1], near[3], near[5])
    )
    hiddens = near + [far, send(far, 0, 1)]
    term = term_call(around, hiddens, grad_values)
    parts = lax.all_to_all(
        term.reshape((n_y, n_z) + master.shape), "y", split_axis=0, concat_axis=0, tiled=True
    )
    summed = add_parts(parts)
    parts = lax.all_to_all(summed, "z", split_axis=0, concat_axis=0, tiled=True)
    values = values_call(hiddens, weight)
    probs = pltpu.with_memory_space_constraint(probs, pltpu.HBM)
    grads = along(grads_call(origin, to, around, pieces, probs, values))
    grads[1], parts = lax.optimization_barrier((grads[1], parts))
    grad_query, grad_key = unpack(origin, across(grads))
    master, m_code, m_scale, v_code, v_scale = adam_call(
        parts, master, m_code, m_scale, v_code, v_scale
    )
    state = (master, m_code, m_scale.T, v_code, v_scale.T)
    return (grad_query[None], grad_key[None]) + state


def solution(mesh):
    tokens, state = P(("y", "z"), "seq", None), P(("y", "z"), "seq")
    rows = math.gcd(8, mesh.shape["dp"])
    cut = mesh.devices.reshape(mesh.shape["seq"], rows, mesh.shape["dp"] // rows)
    return jax.shard_map(
        shards,
        mesh=Mesh(cut, ("seq", "y", "z")),
        in_specs=(tokens,) * 4 + (P(("y", "z"), None),) + (state,) * 5,
        out_specs=(tokens,) * 2 + (state,) * 5,
        check_vma=False,
    )
```

```python
import functools
import math

import jax
import jax.numpy as jnp
from jax import lax
from jax.experimental import pallas as pl
from jax.experimental.pallas import tpu as pltpu
from jax.sharding import Mesh
from jax.sharding import PartitionSpec as P

D = 4096
HD = 128
DOCS = 8
STEP = 1000
SEQ = 1024
GROUP = 4
QW = GROUP * HD
ROWS = 128
BLOCKS = SEQ // ROWS
MOST = 4
NEG = -1e30
INV_WIDTH = 1.0 / math.sqrt(D)
SCALE = 1.0 / math.sqrt(HD)
F32 = jnp.float32
BF16 = jnp.bfloat16


def dot(a, b):
    return jnp.dot(a, b, preferred_element_type=F32)


def stacked(block):
    return jnp.concatenate([block[:, a * HD : (a + 1) * HD] for a in range(GROUP)], axis=0)


def params(mebibytes=24):
    return pltpu.CompilerParams(vmem_limit_bytes=mebibytes * 1024 * 1024)


def cost(microseconds):
    return pl.CostEstimate(
        flops=int(microseconds * 1e9), bytes_accessed=int(microseconds * 1e6), transcendentals=0
    )


XS = 4


def place(value, dx, dc):
    chip = lax.rem(lax.div(value, 2) + dx, XS)
    return chip * 2 + jnp.bitwise_xor(lax.rem(value, 2), dc)


def send(array, dx, dc):
    pairs = [(s, ((s // 2 + dx) % XS) * 2 + ((s % 2) ^ dc)) for s in range(2 * XS)]
    return lax.ppermute(array, "seq", pairs)


def turn(array, dx):
    pairs = [(s, ((s // 2 + (dx if s % 2 == 0 else -dx)) % XS) * 2 + s % 2) for s in range(2 * XS)]
    return lax.ppermute(array, "seq", pairs)


def in_hbm(array):
    return pltpu.with_memory_space_constraint(array, pltpu.HBM)


ANYWHERE = pl.BlockSpec(memory_space=pl.ANY)
SCALARS = pl.BlockSpec(memory_space=pltpu.SMEM)


def run_copies(copies):
    for copy in copies:
        copy.start()
    for copy in copies:
        copy.wait()


def pack_kernel(to_ref, q_ref, c_ref, k_ref, *refs):
    outs, sems = refs[:-1], refs[-1]
    copies = []
    for r in range(8):
        out = outs[r // 2].at[r % 2]
        j = to_ref[r]
        wide = pl.ds(pl.multiple_of(j * QW, QW), QW)
        thin = pl.ds(pl.multiple_of(j * HD, HD), HD)
        for n, (src, lanes, into) in enumerate(
            [
                (q_ref, wide, pl.ds(0, QW)),
                (c_ref, wide, pl.ds(QW, QW)),
                (k_ref, thin, pl.ds(2 * QW, HD)),
            ]
        ):
            copies.append(
                pltpu.make_async_copy(src.at[:, lanes], out.at[:, into], sems.at[3 * r + n])
            )
    run_copies(copies)


def pack(to, query, cot, key):
    tokens = query.shape[0]
    return pl.pallas_call(
        pack_kernel,
        in_specs=[SCALARS] + [pl.BlockSpec(memory_space=pltpu.VMEM)] * 3,
        out_specs=[ANYWHERE] * XS,
        out_shape=[pltpu.HBM((2, tokens, 2 * QW + HD), BF16)] * XS,
        scratch_shapes=[pltpu.SemaphoreType.DMA((24,))],
        cost_estimate=cost(3),
        compiler_params=params(60),
    )(to, query, cot, key)


def merge_kernel(*refs):
    pairs, out, sems = refs[:XS], refs[XS], refs[XS + 1]
    run_copies(
        [pltpu.make_async_copy(pair.at[1], out.at[r], sems.at[r]) for r, pair in enumerate(pairs)]
    )


def merge(pairs):
    return pl.pallas_call(
        merge_kernel,
        in_specs=[ANYWHERE] * XS,
        out_specs=pl.BlockSpec(memory_space=pltpu.VMEM),
        out_shape=jax.ShapeDtypeStruct((XS,) + pairs[0].shape[1:], BF16),
        scratch_shapes=[pltpu.SemaphoreType.DMA((XS,))],
        cost_estimate=cost(1),
        compiler_params=params(8),
    )(*pairs)


def along(pairs):
    return [pairs[0]] + [send(pairs[dx], dx, 0) for dx in range(1, XS)]


def across(got):
    return got + [send(merge(got), 0, 1)]


def arrived(refs):
    return [refs[r // 2].at[0] if r % 2 == 0 else refs[XS].at[r // 2] for r in range(8)]


def gather_pieces(from_ref, piece_refs, whole_ref, sems):
    run_copies(
        [
            pltpu.make_async_copy(
                piece,
                whole_ref.at[pl.ds(pl.multiple_of(from_ref[r] * ROWS, ROWS), ROWS), :],
                sems.at[r],
            )
            for r, piece in enumerate(arrived(piece_refs))
        ]
    )


def by_step(i, body):
    for v in range(BLOCKS // 2):
        pl.when(i == v)(functools.partial(body, v))


def window(block):
    count = min(block + 1, MOST)
    return count, (block + 1 - count) * ROWS


def block_probs(block, lens_ref, r_ref, pt_ref):
    first = block * ROWS
    count, lower = window(block)
    queries = stacked(r_ref[first : first + ROWS, 0:QW])
    lane = lax.broadcasted_iota(jnp.int32, (1, GROUP * ROWS), 1)
    position = first + jnp.bitwise_and(lane, ROWS - 1)
    start = jnp.zeros_like(position)
    end = jnp.int32(0)
    for k in range(DOCS):
        length = lens_ref[0, k]
        end = end + length
        start = start + jnp.where(position >= end, length, 0)
    row = lax.broadcasted_iota(jnp.int32, (ROWS, GROUP * ROWS), 0)
    first_row = start - lower
    last_row = position - lower
    scores = []
    highest = None
    for b in range(count):
        keys = r_ref[lower + b * ROWS : lower + (b + 1) * ROWS, 2 * QW :]
        tile = lax.dot_general(keys, queries, (((1,), (1,)), ((), ())), preferred_element_type=F32)
        allowed = row >= first_row - b * ROWS
        if b == count - 1:
            allowed = allowed & (row <= last_row - b * ROWS)
        tile = jnp.where(allowed, tile, NEG)
        top = jnp.max(tile, axis=0, keepdims=True)
        highest = top if highest is None else jnp.maximum(highest, top)
        scores.append(tile)
    total = None
    weights = []
    for tile in scores:
        weight = jnp.exp2((tile - highest) * (SCALE * math.log2(math.e)))
        part = jnp.sum(weight, axis=0, keepdims=True)
        total = part if total is None else total + part
        weights.append(weight)
    inverse = 1.0 / total
    for b in range(count):
        pt_ref[b * ROWS : (b + 1) * ROWS, :] = (weights[b] * inverse).astype(BF16)


def probs_kernel(lens_ref, from_ref, *refs):
    pieces, (pt_ref, gv_ref, r_ref, acc_ref, sems) = refs[:5], refs[5:]
    i = pl.program_id(0)

    @pl.when(i == 0)
    def _():
        gather_pieces(from_ref, pieces, r_ref, sems)
        acc_ref[...] = jnp.zeros_like(acc_ref)

    def body(v):
        for n, block in enumerate((v, v + MOST)):
            block_probs(block, lens_ref, r_ref, pt_ref.at[0, n])
        for n, block in enumerate((v, v + MOST)):
            count, lower = window(block)
            cot = stacked(r_ref[block * ROWS : (block + 1) * ROWS, QW : 2 * QW])
            size = count * ROWS
            acc_ref[lower : lower + size, :] += dot(pt_ref[0, n, 0:size, :], cot)

    by_step(i, body)

    @pl.when(i == BLOCKS // 2 - 1)
    def _():
        gv_ref[...] = acc_ref[...].astype(BF16)


PROBS_SHAPE = (BLOCKS // 2, 2, MOST * ROWS, GROUP * ROWS)
PROBS_SPEC = pl.BlockSpec((1,) + PROBS_SHAPE[1:], lambda i: (i, 0, 0, 0))


def probs_call(doc_lens, origin, pieces):
    width = 2 * QW + HD
    return pl.pallas_call(
        probs_kernel,
        grid=(BLOCKS // 2,),
        in_specs=[SCALARS, SCALARS] + [ANYWHERE] * 5,
        out_specs=[PROBS_SPEC, pl.BlockSpec((SEQ, HD), lambda i: (0, 0))],
        out_shape=[
            pltpu.HBM(PROBS_SHAPE, BF16),
            pltpu.HBM((SEQ, HD), BF16),
        ],
        scratch_shapes=[
            pltpu.VMEM((SEQ, width), BF16),
            pltpu.VMEM((SEQ, HD), F32),
            pltpu.SemaphoreType.DMA((8,)),
        ],
        cost_estimate=cost(8),
        compiler_params=params(),
    )(doc_lens, origin, *pieces)


def join(refs):
    return jnp.concatenate([ref[...] for ref in refs], axis=0)


def term_kernel(from_ref, low_ref, *refs):
    hidden_refs, (gv_ref, keep_ref, give_ref, gvt_ref) = refs[:8], refs[8:]

    @pl.when(pl.program_id(0) == 0)
    def _():
        for r in range(8):
            rows = pl.ds(pl.multiple_of(from_ref[r] * ROWS, ROWS), ROWS)
            gvt_ref[:, r * ROWS : (r + 1) * ROWS] = gv_ref[rows, :].T

    term = dot(gvt_ref[...], join(hidden_refs))
    term = (term.T * INV_WIDTH).astype(BF16)
    term = term.reshape(keep_ref.shape[0], -1, keep_ref.shape[1], HD)
    even, odd = term[:, 0], term[:, -1]
    keep_ref[...] = jnp.where(low_ref[0] == 0, even, odd)
    give_ref[...] = jnp.where(low_ref[0] == 0, odd, even)


def values_kernel(*refs):
    hidden_refs, (w_ref, val_ref, acc_ref) = refs[:-3], refs[-3:]
    j = pl.program_id(0)

    @pl.when(j == 0)
    def _():
        acc_ref[...] = jnp.zeros_like(acc_ref)

    acc_ref[...] += dot(join(hidden_refs), w_ref[...])

    @pl.when(j == pl.num_programs(0) - 1)
    def _():
        val_ref[...] = (acc_ref[...] * INV_WIDTH).astype(BF16)


STRIPE = 1024


def hidden_specs(pieces):
    return [pl.BlockSpec((piece.shape[0], STRIPE), lambda j: (0, j)) for piece in pieces]


def term_call(origin, low, pieces, grad_values, rows, pairing):
    count = D // rows // pairing
    step = count * STRIPE // D
    block = pl.BlockSpec((step, rows, HD), lambda j: (j, 0, 0))
    return pl.pallas_call(
        term_kernel,
        grid=(D // STRIPE,),
        in_specs=[SCALARS, SCALARS]
        + hidden_specs(pieces)
        + [pl.BlockSpec((SEQ, HD), lambda j: (0, 0))],
        out_specs=[block, block],
        out_shape=[pltpu.HBM((count, rows, HD), BF16)] * 2,
        scratch_shapes=[pltpu.VMEM((HD, SEQ), BF16)],
        cost_estimate=cost(5),
        compiler_params=params(),
    )(origin, low, *pieces, grad_values)


def values_call(pieces, weight):
    rows = sum(piece.shape[0] for piece in pieces)
    return pl.pallas_call(
        values_kernel,
        grid=(D // STRIPE,),
        in_specs=hidden_specs(pieces) + [pl.BlockSpec((STRIPE, HD), lambda j: (j, 0))],
        out_specs=pl.BlockSpec((rows, HD), lambda j: (0, 0)),
        out_shape=jax.ShapeDtypeStruct((rows, HD), BF16),
        scratch_shapes=[pltpu.VMEM((rows, HD), F32)],
        cost_estimate=cost(rows * 6 // SEQ),
        compiler_params=params(),
    )(*pieces, weight)


def block_grads(block, r_ref, pt_ref, val_ref, out_ref, acc_ref, kt_ref, vt_ref):
    first = block * ROWS
    count, lower = window(block)
    size = count * ROWS
    queries = stacked(r_ref[first : first + ROWS, 0:QW])
    cot_t = stacked(r_ref[first : first + ROWS, QW : 2 * QW]).T
    attn_t = dot(vt_ref[:, lower : lower + size], pt_ref[0:size, :]).astype(BF16)
    delta = jnp.sum(attn_t.astype(F32) * cot_t.astype(F32), axis=0, keepdims=True)
    prob_grad = dot(val_ref[lower : lower + size, :], cot_t)
    probs = pt_ref[0:size, :].astype(F32)
    score_grad = (probs * (prob_grad - delta)).astype(BF16)
    acc_ref[lower : lower + size, :] += dot(score_grad, queries)
    grad_t = dot(kt_ref[:, lower : lower + size], score_grad) * SCALE
    grad = grad_t.T.astype(BF16)
    for a in range(GROUP):
        out_ref[first : first + ROWS, a * HD : (a + 1) * HD] = grad[a * ROWS : (a + 1) * ROWS, :]


def grads_kernel(from_ref, to_ref, around_ref, *refs):
    pieces, (pt_ref, held_ref), outs = refs[:5], refs[5:7], refs[7 : 7 + XS]
    r_ref, val_ref, out_ref, acc_ref, kt_ref, vt_ref, sems = refs[7 + XS :]
    i = pl.program_id(0)

    @pl.when(i == 0)
    def _():
        gather_pieces(from_ref, pieces, r_ref, sems)
        acc_ref[...] = jnp.zeros_like(acc_ref)
        kt_ref[...] = r_ref[:, 2 * QW :].T
        for r in range(8):
            rows = pl.ds(pl.multiple_of(around_ref[r] * ROWS, ROWS), ROWS)
            val_ref[rows, :] = held_ref[r * ROWS : (r + 1) * ROWS, :]
        vt_ref[...] = val_ref[...].T

    def body(v):
        for n, block in enumerate((v, v + MOST)):
            block_grads(block, r_ref, pt_ref.at[0, n], val_ref, out_ref, acc_ref, kt_ref, vt_ref)

    by_step(i, body)

    @pl.when(i == BLOCKS // 2 - 1)
    def _():
        out_ref[:, QW:] = (acc_ref[...] * SCALE).astype(BF16)
        run_copies(
            [
                pltpu.make_async_copy(
                    out_ref.at[pl.ds(pl.multiple_of(to_ref[r] * ROWS, ROWS), ROWS), :],
                    outs[r // 2].at[r % 2],
                    sems.at[r],
                )
                for r in range(8)
            ]
        )


def grads_call(origin, to, around, pieces, probs, values):
    width = 2 * QW + HD
    return pl.pallas_call(
        grads_kernel,
        grid=(BLOCKS // 2,),
        in_specs=[SCALARS, SCALARS, SCALARS]
        + [ANYWHERE] * 5
        + [
            PROBS_SPEC,
            pl.BlockSpec((SEQ, HD), lambda i: (0, 0)),
        ],
        out_specs=[ANYWHERE] * XS,
        out_shape=[pltpu.HBM((2, ROWS, QW + HD), BF16)] * XS,
        scratch_shapes=[
            pltpu.VMEM((SEQ, width), BF16),
            pltpu.VMEM((SEQ, HD), BF16),
            pltpu.VMEM((SEQ, QW + HD), BF16),
            pltpu.VMEM((SEQ, HD), F32),
            pltpu.VMEM((HD, SEQ), BF16),
            pltpu.VMEM((HD, SEQ), BF16),
            pltpu.SemaphoreType.DMA((8,)),
        ],
        cost_estimate=cost(9),
        compiler_params=params(),
    )(origin, to, around, *pieces, probs, values)


def unpack_kernel(from_ref, *refs):
    pieces, (q_ref, k_ref, sems) = refs[:5], refs[5:]
    copies = []
    for r, piece in enumerate(arrived(pieces)):
        j = from_ref[r]
        wide = pl.ds(pl.multiple_of(j * QW, QW), QW)
        thin = pl.ds(pl.multiple_of(j * HD, HD), HD)
        copies.append(
            pltpu.make_async_copy(piece.at[:, pl.ds(0, QW)], q_ref.at[:, wide], sems.at[2 * r])
        )
        copies.append(
            pltpu.make_async_copy(piece.at[:, pl.ds(QW, HD)], k_ref.at[:, thin], sems.at[2 * r + 1])
        )
    run_copies(copies)


def unpack(origin, pieces):
    return pl.pallas_call(
        unpack_kernel,
        in_specs=[SCALARS] + [pl.BlockSpec(memory_space=pltpu.VMEM)] * 5,
        out_specs=[ANYWHERE] * 2,
        out_shape=[
            jax.ShapeDtypeStruct((ROWS, 8 * QW), BF16),
            jax.ShapeDtypeStruct((ROWS, 8 * HD), BF16),
        ],
        scratch_shapes=[pltpu.SemaphoreType.DMA((16,))],
        cost_estimate=cost(2),
        compiler_params=params(8),
    )(origin, *pieces)


def add_kernel(one_ref, two_ref, out_ref):
    out_ref[...] = (one_ref[...].astype(F32) + two_ref[...].astype(F32)).astype(BF16)


def add_pair(one, two):
    return pl.pallas_call(
        add_kernel,
        out_shape=jax.ShapeDtypeStruct(one.shape, BF16),
        cost_estimate=cost(1),
        compiler_params=params(8),
    )(one, two)


def swap_low(array):
    return lax.ppermute(array, "zl", [(0, 1), (1, 0)])


def adam_kernel(
    parts_ref,
    master_ref,
    mc_ref,
    ms_ref,
    vc_ref,
    vs_ref,
    master_out,
    mc_out,
    ms_out,
    vc_out,
    vs_out,
    grad_ref,
    mold_ref,
    vold_ref,
    step_ref,
    mcode_ref,
    vcode_ref,
):
    total = jnp.zeros(grad_ref.shape, F32)
    for g in range(parts_ref.shape[0]):
        total = total + parts_ref[g].astype(F32)
    grad_ref[...] = total
    mold_ref[...] = mc_ref[...].astype(F32)
    vold_ref[...] = vc_ref[...].astype(F32)
    half = grad_ref.shape[0] // 2
    first_fix = 1.0 - 0.9**STEP
    second_fix = 1.0 - 0.999**STEP
    news = []
    for odd in range(2):
        rows = pl.ds(odd, half, stride=2)
        grad = grad_ref[rows, :]
        m_new = 0.9 * (mold_ref[rows, :] * ms_ref[...]) + 0.1 * grad
        v_new = 0.999 * (vold_ref[rows, :] * vs_ref[...]) + 0.001 * grad * grad
        step_ref[rows, :] = m_new / first_fix / (jnp.sqrt(v_new / second_fix) + 1e-08)
        news.append((m_new, v_new))
    m_top = jnp.maximum(
        jnp.max(jnp.abs(news[0][0]), axis=1, keepdims=True),
        jnp.max(jnp.abs(news[1][0]), axis=1, keepdims=True),
    )
    v_top = jnp.maximum(
        jnp.max(jnp.abs(news[0][1]), axis=1, keepdims=True),
        jnp.max(jnp.abs(news[1][1]), axis=1, keepdims=True),
    )
    ms_out[...] = jnp.broadcast_to(m_top, (half, HD)).T[0:1, :]
    vs_out[...] = jnp.broadcast_to(v_top, (half, HD)).T[0:1, :]
    for odd in range(2):
        rows = pl.ds(odd, half, stride=2)
        mcode_ref[rows, :] = news[odd][0] / (m_top + 1e-06)
        vcode_ref[rows, :] = news[odd][1] / (v_top + 1e-06)
    mc_out[...] = mcode_ref[...].astype(BF16)
    vc_out[...] = vcode_ref[...].astype(BF16)
    master_out[...] = master_ref[...] - 0.01 * step_ref[...]


def adam_call(parts, master, m_code, m_scale, v_code, v_scale):
    shape = master.shape
    return pl.pallas_call(
        adam_kernel,
        out_shape=[
            jax.ShapeDtypeStruct(shape, F32),
            jax.ShapeDtypeStruct(shape, BF16),
            jax.ShapeDtypeStruct(m_scale.shape[::-1], F32),
            jax.ShapeDtypeStruct(shape, BF16),
            jax.ShapeDtypeStruct(v_scale.shape[::-1], F32),
        ],
        scratch_shapes=[pltpu.VMEM(shape, F32) for _ in range(6)],
        cost_estimate=cost(2),
        compiler_params=params(16),
    )(parts, master, m_code, m_scale, v_code, v_scale)


def shards(hidden, query, key, grad_out, doc_lens, master, m_code, m_scale, v_code, v_scale):
    n_far = lax.axis_size("y") * lax.axis_size("zh")
    low = lax.axis_index("zl")
    rows = master.shape[0]
    me = lax.axis_index("seq")
    to = jnp.stack([place(me, r // 2, r % 2) for r in range(8)])
    origin = jnp.stack([place(me, (XS - r // 2) % XS, r % 2) for r in range(8)])
    around = jnp.stack([place(me, dx, dc) for dx in (0, 3, 1, 2) for dc in (0, 1)])
    core = lax.rem(me, 2)
    ahead = jnp.where(core == 0, XS - 1, 1)
    own = in_hbm(hidden[0])
    first, second = turn(own, 1), turn(own, -1)
    around = jnp.stack(
        [
            me,
            place(me, 0, 1),
            place(me, ahead, 0),
            place(me, XS - ahead, 1),
            place(me, XS - ahead, 0),
            place(me, ahead, 1),
            place(me, 2, 0),
            place(me, 2, 1),
        ]
    )
    pairs = pack(to, query[0], grad_out[0], key[0])
    pieces = across(along(pairs))
    mine = master.astype(BF16)
    theirs = swap_low(mine)
    both = jnp.where(low == 0, jnp.stack([mine, theirs]), jnp.stack([theirs, mine]))
    both, _ = lax.optimization_barrier((both, pairs[0]))
    copies = jnp.broadcast_to(both[None], (n_far,) + both.shape)
    weight = lax.all_to_all(copies, ("y", "zh"), split_axis=0, concat_axis=0, tiled=True)
    weight = weight.reshape(D, HD)
    far = turn(first, 1)
    near = [own, send(own, 0, 1), first, send(first, 0, 1), second, send(second, 0, 1)]
    pieces = [in_hbm(piece) for piece in pieces[:XS]] + pieces[XS:]
    probs, grad_values = probs_call(doc_lens, origin, pieces)
    far, grad_values, weight, near[1], near[3], near[5] = lax.optimization_barrier(
        (far, grad_values, weight, near[1], near[3], near[5])
    )
    hiddens = near + [far, send(far, 0, 1)]
    keep, give = term_call(around, low[None], hiddens, in_hbm(grad_values), rows, 2)
    other = swap_low(give)
    values = values_call(hiddens, weight)
    probs = in_hbm(probs)
    grads = list(grads_call(origin, to, around, pieces, probs, values))
    other, keep, grads[1] = lax.optimization_barrier((other, keep, grads[1]))
    grads = along(grads)
    parts = lax.all_to_all(
        add_pair(keep, other), ("y", "zh"), split_axis=0, concat_axis=0, tiled=True
    )
    grad_query, grad_key = unpack(origin, across(grads))
    master, m_code, m_scale, v_code, v_scale = adam_call(
        parts, master, m_code, m_scale, v_code, v_scale
    )
    state = (master, m_code, m_scale.T, v_code, v_scale.T)
    return (grad_query[None], grad_key[None]) + state


def solution(mesh):
    tokens, state = P(("y", "zh", "zl"), "seq", None), P(("y", "zh", "zl"), "seq")
    cut = mesh.devices.reshape(mesh.shape["seq"], 8, mesh.shape["dp"] // 16, 2)
    return jax.shard_map(
        shards,
        mesh=Mesh(cut, ("seq", "y", "zh", "zl")),
        in_specs=(tokens,) * 4 + (P(("y", "zh", "zl"), None),) + (state,) * 5,
        out_specs=(tokens,) * 2 + (state,) * 5,
        check_vma=False,
    )
```

```python
import functools
import math

import jax
import jax.numpy as jnp
from jax import lax
from jax.experimental import pallas as pl
from jax.experimental.pallas import tpu as pltpu
from jax.sharding import Mesh
from jax.sharding import PartitionSpec as P

D = 4096
HD = 128
DOCS = 8
STEP = 1000
SEQ = 1024
GROUP = 4
QW = GROUP * HD
ROWS = 128
BLOCKS = SEQ // ROWS
MOST = 4
NEG = -1e30
INV_WIDTH = 1.0 / math.sqrt(D)
SCALE = 1.0 / math.sqrt(HD)
F32 = jnp.float32
BF16 = jnp.bfloat16


def dot(a, b):
    return jnp.dot(a, b, preferred_element_type=F32)


def stacked(block):
    return jnp.concatenate([block[:, a * HD : (a + 1) * HD] for a in range(GROUP)], axis=0)


def params(mebibytes=24):
    return pltpu.CompilerParams(vmem_limit_bytes=mebibytes * 1024 * 1024)


def cost(microseconds):
    return pl.CostEstimate(
        flops=int(microseconds * 1e9), bytes_accessed=int(microseconds * 1e6), transcendentals=0
    )


XS = 4


def place(value, dx, dc):
    chip = lax.rem(lax.div(value, 2) + dx, XS)
    return chip * 2 + jnp.bitwise_xor(lax.rem(value, 2), dc)


def send(array, dx, dc):
    pairs = [(s, ((s // 2 + dx) % XS) * 2 + ((s % 2) ^ dc)) for s in range(2 * XS)]
    return lax.ppermute(array, "seq", pairs)


def turn(array, dx):
    pairs = [(s, ((s // 2 + (dx if s % 2 == 0 else -dx)) % XS) * 2 + s % 2) for s in range(2 * XS)]
    return lax.ppermute(array, "seq", pairs)


def in_hbm(array):
    return pltpu.with_memory_space_constraint(array, pltpu.HBM)


ANYWHERE = pl.BlockSpec(memory_space=pl.ANY)
SCALARS = pl.BlockSpec(memory_space=pltpu.SMEM)


def run_copies(copies):
    for copy in copies:
        copy.start()
    for copy in copies:
        copy.wait()


def pack_kernel(to_ref, q_ref, c_ref, k_ref, *refs):
    outs, sems = refs[:-1], refs[-1]
    copies = []
    for r in range(8):
        out = outs[r // 2].at[r % 2]
        j = to_ref[r]
        wide = pl.ds(pl.multiple_of(j * QW, QW), QW)
        thin = pl.ds(pl.multiple_of(j * HD, HD), HD)
        for n, (src, lanes, into) in enumerate(
            [
                (q_ref, wide, pl.ds(0, QW)),
                (c_ref, wide, pl.ds(QW, QW)),
                (k_ref, thin, pl.ds(2 * QW, HD)),
            ]
        ):
            copies.append(
                pltpu.make_async_copy(src.at[:, lanes], out.at[:, into], sems.at[3 * r + n])
            )
    run_copies(copies)


def pack(to, query, cot, key):
    tokens = query.shape[0]
    return pl.pallas_call(
        pack_kernel,
        in_specs=[SCALARS] + [pl.BlockSpec(memory_space=pltpu.VMEM)] * 3,
        out_specs=[ANYWHERE] * XS,
        out_shape=[pltpu.HBM((2, tokens, 2 * QW + HD), BF16)] * XS,
        scratch_shapes=[pltpu.SemaphoreType.DMA((24,))],
        cost_estimate=cost(3),
        compiler_params=params(60),
    )(to, query, cot, key)


def merge_kernel(*refs):
    pairs, out, sems = refs[:XS], refs[XS], refs[XS + 1]
    run_copies(
        [pltpu.make_async_copy(pair.at[1], out.at[r], sems.at[r]) for r, pair in enumerate(pairs)]
    )


def merge(pairs):
    return pl.pallas_call(
        merge_kernel,
        in_specs=[ANYWHERE] * XS,
        out_specs=pl.BlockSpec(memory_space=pltpu.VMEM),
        out_shape=jax.ShapeDtypeStruct((XS,) + pairs[0].shape[1:], BF16),
        scratch_shapes=[pltpu.SemaphoreType.DMA((XS,))],
        cost_estimate=cost(1),
        compiler_params=params(8),
    )(*pairs)


def along(pairs):
    return [pairs[0]] + [send(pairs[dx], dx, 0) for dx in range(1, XS)]


def across(got):
    return got + [send(merge(got), 0, 1)]


def arrived(refs):
    return [refs[r // 2].at[0] if r % 2 == 0 else refs[XS].at[r // 2] for r in range(8)]


def gather_pieces(from_ref, piece_refs, whole_ref, sems):
    run_copies(
        [
            pltpu.make_async_copy(
                piece,
                whole_ref.at[pl.ds(pl.multiple_of(from_ref[r] * ROWS, ROWS), ROWS), :],
                sems.at[r],
            )
            for r, piece in enumerate(arrived(piece_refs))
        ]
    )


def by_step(i, body):
    for v in range(BLOCKS // 2):
        pl.when(i == v)(functools.partial(body, v))


def window(block):
    count = min(block + 1, MOST)
    return count, (block + 1 - count) * ROWS


def block_probs(block, lens_ref, r_ref, pt_ref):
    first = block * ROWS
    count, lower = window(block)
    queries = stacked(r_ref[first : first + ROWS, 0:QW])
    lane = lax.broadcasted_iota(jnp.int32, (1, GROUP * ROWS), 1)
    position = first + jnp.bitwise_and(lane, ROWS - 1)
    start = jnp.zeros_like(position)
    end = jnp.int32(0)
    for k in range(DOCS):
        length = lens_ref[0, k]
        end = end + length
        start = start + jnp.where(position >= end, length, 0)
    row = lax.broadcasted_iota(jnp.int32, (ROWS, GROUP * ROWS), 0)
    first_row = start - lower
    last_row = position - lower
    scores = []
    highest = None
    for b in range(count):
        keys = r_ref[lower + b * ROWS : lower + (b + 1) * ROWS, 2 * QW :]
        tile = lax.dot_general(keys, queries, (((1,), (1,)), ((), ())), preferred_element_type=F32)
        allowed = row >= first_row - b * ROWS
        if b == count - 1:
            allowed = allowed & (row <= last_row - b * ROWS)
        tile = jnp.where(allowed, tile, NEG)
        top = jnp.max(tile, axis=0, keepdims=True)
        highest = top if highest is None else jnp.maximum(highest, top)
        scores.append(tile)
    total = None
    weights = []
    for tile in scores:
        weight = jnp.exp2((tile - highest) * (SCALE * math.log2(math.e)))
        part = jnp.sum(weight, axis=0, keepdims=True)
        total = part if total is None else total + part
        weights.append(weight)
    inverse = 1.0 / total
    for b in range(count):
        pt_ref[b * ROWS : (b + 1) * ROWS, :] = (weights[b] * inverse).astype(BF16)


def probs_kernel(lens_ref, from_ref, *refs):
    pieces, (pt_ref, gv_ref, r_ref, acc_ref, sems) = refs[:5], refs[5:]
    i = pl.program_id(0)

    @pl.when(i == 0)
    def _():
        gather_pieces(from_ref, pieces, r_ref, sems)
        acc_ref[...] = jnp.zeros_like(acc_ref)

    def body(v):
        for n, block in enumerate((v, v + MOST)):
            block_probs(block, lens_ref, r_ref, pt_ref.at[0, n])
        for n, block in enumerate((v, v + MOST)):
            count, lower = window(block)
            cot = stacked(r_ref[block * ROWS : (block + 1) * ROWS, QW : 2 * QW])
            size = count * ROWS
            acc_ref[lower : lower + size, :] += dot(pt_ref[0, n, 0:size, :], cot)

    by_step(i, body)

    @pl.when(i == BLOCKS // 2 - 1)
    def _():
        gv_ref[...] = acc_ref[...].astype(BF16)


PROBS_SHAPE = (BLOCKS // 2, 2, MOST * ROWS, GROUP * ROWS)
PROBS_SPEC = pl.BlockSpec((1,) + PROBS_SHAPE[1:], lambda i: (i, 0, 0, 0))


def probs_call(doc_lens, origin, pieces):
    width = 2 * QW + HD
    return pl.pallas_call(
        probs_kernel,
        grid=(BLOCKS // 2,),
        in_specs=[SCALARS, SCALARS] + [ANYWHERE] * 5,
        out_specs=[PROBS_SPEC, pl.BlockSpec((SEQ, HD), lambda i: (0, 0))],
        out_shape=[
            pltpu.HBM(PROBS_SHAPE, BF16),
            pltpu.HBM((SEQ, HD), BF16),
        ],
        scratch_shapes=[
            pltpu.VMEM((SEQ, width), BF16),
            pltpu.VMEM((SEQ, HD), F32),
            pltpu.SemaphoreType.DMA((8,)),
        ],
        cost_estimate=cost(8),
        compiler_params=params(),
    )(doc_lens, origin, *pieces)


def join(refs):
    return jnp.concatenate([ref[...] for ref in refs], axis=0)


def term_kernel(from_ref, low_ref, *refs):
    hidden_refs, (gv_ref, keep_ref, give_ref, gvt_ref) = refs[:8], refs[8:]

    @pl.when(pl.program_id(0) == 0)
    def _():
        for r in range(8):
            rows = pl.ds(pl.multiple_of(from_ref[r] * ROWS, ROWS), ROWS)
            gvt_ref[:, r * ROWS : (r + 1) * ROWS] = gv_ref[rows, :].T

    term = dot(gvt_ref[...], join(hidden_refs))
    term = (term.T * INV_WIDTH).astype(BF16)
    term = term.reshape(keep_ref.shape[0], -1, keep_ref.shape[1], HD)
    even, odd = term[:, 0], term[:, -1]
    keep_ref[...] = jnp.where(low_ref[0] == 0, even, odd)
    give_ref[...] = jnp.where(low_ref[0] == 0, odd, even)


def values_kernel(*refs):
    hidden_refs, (w_ref, val_ref, acc_ref) = refs[:-3], refs[-3:]
    j = pl.program_id(0)

    @pl.when(j == 0)
    def _():
        acc_ref[...] = jnp.zeros_like(acc_ref)

    acc_ref[...] += dot(join(hidden_refs), w_ref[...])

    @pl.when(j == pl.num_programs(0) - 1)
    def _():
        val_ref[...] = (acc_ref[...] * INV_WIDTH).astype(BF16)


STRIPE = 1024


def hidden_specs(pieces):
    return [pl.BlockSpec((piece.shape[0], STRIPE), lambda j: (0, j)) for piece in pieces]


def term_call(origin, low, pieces, grad_values, rows, pairing):
    count = D // rows // pairing
    step = count * STRIPE // D
    block = pl.BlockSpec((step, rows, HD), lambda j: (j, 0, 0))
    return pl.pallas_call(
        term_kernel,
        grid=(D // STRIPE,),
        in_specs=[SCALARS, SCALARS]
        + hidden_specs(pieces)
        + [pl.BlockSpec((SEQ, HD), lambda j: (0, 0))],
        out_specs=[block, block],
        out_shape=[pltpu.HBM((count, rows, HD), BF16)] * 2,
        scratch_shapes=[pltpu.VMEM((HD, SEQ), BF16)],
        cost_estimate=cost(5),
        compiler_params=params(),
    )(origin, low, *pieces, grad_values)


def values_call(pieces, weight):
    rows = sum(piece.shape[0] for piece in pieces)
    return pl.pallas_call(
        values_kernel,
        grid=(D // STRIPE,),
        in_specs=hidden_specs(pieces) + [pl.BlockSpec((STRIPE, HD), lambda j: (j, 0))],
        out_specs=pl.BlockSpec((rows, HD), lambda j: (0, 0)),
        out_shape=jax.ShapeDtypeStruct((rows, HD), BF16),
        scratch_shapes=[pltpu.VMEM((rows, HD), F32)],
        cost_estimate=cost(rows * 6 // SEQ),
        compiler_params=params(),
    )(*pieces, weight)


def block_grads(block, r_ref, pt_ref, val_ref, out_ref, acc_ref, kt_ref, vt_ref):
    first = block * ROWS
    count, lower = window(block)
    size = count * ROWS
    queries = stacked(r_ref[first : first + ROWS, 0:QW])
    cot_t = stacked(r_ref[first : first + ROWS, QW : 2 * QW]).T
    attn_t = dot(vt_ref[:, lower : lower + size], pt_ref[0:size, :]).astype(BF16)
    delta = jnp.sum(attn_t.astype(F32) * cot_t.astype(F32), axis=0, keepdims=True)
    prob_grad = dot(val_ref[lower : lower + size, :], cot_t)
    probs = pt_ref[0:size, :].astype(F32)
    score_grad = (probs * (prob_grad - delta)).astype(BF16)
    acc_ref[lower : lower + size, :] += dot(score_grad, queries)
    grad_t = dot(kt_ref[:, lower : lower + size], score_grad) * SCALE
    grad = grad_t.T.astype(BF16)
    for a in range(GROUP):
        out_ref[first : first + ROWS, a * HD : (a + 1) * HD] = grad[a * ROWS : (a + 1) * ROWS, :]


def grads_kernel(from_ref, to_ref, around_ref, *refs):
    pieces, (pt_ref, held_ref), outs = refs[:5], refs[5:7], refs[7 : 7 + XS]
    r_ref, val_ref, out_ref, acc_ref, kt_ref, vt_ref, sems = refs[7 + XS :]
    i = pl.program_id(0)

    @pl.when(i == 0)
    def _():
        gather_pieces(from_ref, pieces, r_ref, sems)
        acc_ref[...] = jnp.zeros_like(acc_ref)
        kt_ref[...] = r_ref[:, 2 * QW :].T
        for r in range(8):
            rows = pl.ds(pl.multiple_of(around_ref[r] * ROWS, ROWS), ROWS)
            val_ref[rows, :] = held_ref[r * ROWS : (r + 1) * ROWS, :]
        vt_ref[...] = val_ref[...].T

    def body(v):
        for n, block in enumerate((v, v + MOST)):
            block_grads(block, r_ref, pt_ref.at[0, n], val_ref, out_ref, acc_ref, kt_ref, vt_ref)

    by_step(i, body)

    @pl.when(i == BLOCKS // 2 - 1)
    def _():
        out_ref[:, QW:] = (acc_ref[...] * SCALE).astype(BF16)
        run_copies(
            [
                pltpu.make_async_copy(
                    out_ref.at[pl.ds(pl.multiple_of(to_ref[r] * ROWS, ROWS), ROWS), :],
                    outs[r // 2].at[r % 2],
                    sems.at[r],
                )
                for r in range(8)
            ]
        )


def grads_call(origin, to, around, pieces, probs, values):
    width = 2 * QW + HD
    return pl.pallas_call(
        grads_kernel,
        grid=(BLOCKS // 2,),
        in_specs=[SCALARS, SCALARS, SCALARS]
        + [ANYWHERE] * 5
        + [
            PROBS_SPEC,
            pl.BlockSpec((SEQ, HD), lambda i: (0, 0)),
        ],
        out_specs=[ANYWHERE] * XS,
        out_shape=[pltpu.HBM((2, ROWS, QW + HD), BF16)] * XS,
        scratch_shapes=[
            pltpu.VMEM((SEQ, width), BF16),
            pltpu.VMEM((SEQ, HD), BF16),
            pltpu.VMEM((SEQ, QW + HD), BF16),
            pltpu.VMEM((SEQ, HD), F32),
            pltpu.VMEM((HD, SEQ), BF16),
            pltpu.VMEM((HD, SEQ), BF16),
            pltpu.SemaphoreType.DMA((8,)),
        ],
        cost_estimate=cost(9),
        compiler_params=params(),
    )(origin, to, around, *pieces, probs, values)


def unpack_kernel(from_ref, *refs):
    pieces, (q_ref, k_ref, sems) = refs[:5], refs[5:]
    copies = []
    for r, piece in enumerate(arrived(pieces)):
        j = from_ref[r]
        wide = pl.ds(pl.multiple_of(j * QW, QW), QW)
        thin = pl.ds(pl.multiple_of(j * HD, HD), HD)
        copies.append(
            pltpu.make_async_copy(piece.at[:, pl.ds(0, QW)], q_ref.at[:, wide], sems.at[2 * r])
        )
        copies.append(
            pltpu.make_async_copy(piece.at[:, pl.ds(QW, HD)], k_ref.at[:, thin], sems.at[2 * r + 1])
        )
    run_copies(copies)


def unpack(origin, pieces):
    return pl.pallas_call(
        unpack_kernel,
        in_specs=[SCALARS] + [pl.BlockSpec(memory_space=pltpu.VMEM)] * 5,
        out_specs=[ANYWHERE] * 2,
        out_shape=[
            jax.ShapeDtypeStruct((ROWS, 8 * QW), BF16),
            jax.ShapeDtypeStruct((ROWS, 8 * HD), BF16),
        ],
        scratch_shapes=[pltpu.SemaphoreType.DMA((16,))],
        cost_estimate=cost(2),
        compiler_params=params(8),
    )(origin, *pieces)


def split_kernel(low_ref, one_ref, two_ref, keep_ref, give_ref):
    total = one_ref[...].astype(F32) + two_ref[...].astype(F32)
    total = total.astype(BF16).reshape((keep_ref.shape[0], -1) + keep_ref.shape[1:])
    even, odd = total[:, 0], total[:, -1]
    keep_ref[...] = jnp.where(low_ref[0] == 0, even, odd)
    give_ref[...] = jnp.where(low_ref[0] == 0, odd, even)


def split_pair(low, one, two, outer):
    shape = (outer, one.shape[0] // outer // 2 * one.shape[1], HD)
    whole = pl.BlockSpec(memory_space=pltpu.VMEM)
    return pl.pallas_call(
        split_kernel,
        in_specs=[SCALARS, whole, whole],
        out_shape=[jax.ShapeDtypeStruct(shape, BF16)] * 2,
        cost_estimate=cost(1),
        compiler_params=params(8),
    )(low, one, two)


def add_kernel(one_ref, two_ref, out_ref):
    out_ref[...] = (one_ref[...].astype(F32) + two_ref[...].astype(F32)).astype(BF16)


def add_pair(one, two):
    return pl.pallas_call(
        add_kernel,
        out_shape=jax.ShapeDtypeStruct(one.shape, BF16),
        cost_estimate=cost(1),
        compiler_params=params(8),
    )(one, two)


def swap_low(array, axis):
    return lax.ppermute(array, axis, [(0, 1), (1, 0)])


def adam_kernel(
    parts_ref,
    master_ref,
    mc_ref,
    ms_ref,
    vc_ref,
    vs_ref,
    master_out,
    mc_out,
    ms_out,
    vc_out,
    vs_out,
    grad_ref,
    mold_ref,
    vold_ref,
    step_ref,
    mcode_ref,
    vcode_ref,
):
    total = jnp.zeros(grad_ref.shape, F32)
    for g in range(parts_ref.shape[0]):
        total = total + parts_ref[g].astype(F32)
    grad_ref[...] = total
    mold_ref[...] = mc_ref[...].astype(F32)
    vold_ref[...] = vc_ref[...].astype(F32)
    half = grad_ref.shape[0] // 2
    first_fix = 1.0 - 0.9**STEP
    second_fix = 1.0 - 0.999**STEP
    news = []
    for odd in range(2):
        rows = pl.ds(odd, half, stride=2)
        grad = grad_ref[rows, :]
        m_new = 0.9 * (mold_ref[rows, :] * ms_ref[...]) + 0.1 * grad
        v_new = 0.999 * (vold_ref[rows, :] * vs_ref[...]) + 0.001 * grad * grad
        step_ref[rows, :] = m_new / first_fix / (jnp.sqrt(v_new / second_fix) + 1e-08)
        news.append((m_new, v_new))
    m_top = jnp.maximum(
        jnp.max(jnp.abs(news[0][0]), axis=1, keepdims=True),
        jnp.max(jnp.abs(news[1][0]), axis=1, keepdims=True),
    )
    v_top = jnp.maximum(
        jnp.max(jnp.abs(news[0][1]), axis=1, keepdims=True),
        jnp.max(jnp.abs(news[1][1]), axis=1, keepdims=True),
    )
    ms_out[...] = jnp.broadcast_to(m_top, (half, HD)).T[0:1, :]
    vs_out[...] = jnp.broadcast_to(v_top, (half, HD)).T[0:1, :]
    for odd in range(2):
        rows = pl.ds(odd, half, stride=2)
        mcode_ref[rows, :] = news[odd][0] / (m_top + 1e-06)
        vcode_ref[rows, :] = news[odd][1] / (v_top + 1e-06)
    mc_out[...] = mcode_ref[...].astype(BF16)
    vc_out[...] = vcode_ref[...].astype(BF16)
    master_out[...] = master_ref[...] - 0.01 * step_ref[...]


def adam_call(parts, master, m_code, m_scale, v_code, v_scale):
    shape = master.shape
    return pl.pallas_call(
        adam_kernel,
        out_shape=[
            jax.ShapeDtypeStruct(shape, F32),
            jax.ShapeDtypeStruct(shape, BF16),
            jax.ShapeDtypeStruct(m_scale.shape[::-1], F32),
            jax.ShapeDtypeStruct(shape, BF16),
            jax.ShapeDtypeStruct(v_scale.shape[::-1], F32),
        ],
        scratch_shapes=[pltpu.VMEM(shape, F32) for _ in range(6)],
        cost_estimate=cost(2),
        compiler_params=params(16),
    )(parts, master, m_code, m_scale, v_code, v_scale)


def shards(hidden, query, key, grad_out, doc_lens, master, m_code, m_scale, v_code, v_scale):
    n_far = lax.axis_size("yh") * lax.axis_size("yl") * lax.axis_size("zh")
    low, low_y = lax.axis_index("zl"), lax.axis_index("yl")
    rows = master.shape[0]
    me = lax.axis_index("seq")
    to = jnp.stack([place(me, r // 2, r % 2) for r in range(8)])
    origin = jnp.stack([place(me, (XS - r // 2) % XS, r % 2) for r in range(8)])
    around = jnp.stack([place(me, dx, dc) for dx in (0, 3, 1, 2) for dc in (0, 1)])
    core = lax.rem(me, 2)
    ahead = jnp.where(core == 0, XS - 1, 1)
    own = in_hbm(hidden[0])
    first, second = turn(own, 1), turn(own, -1)
    around = jnp.stack(
        [
            me,
            place(me, 0, 1),
            place(me, ahead, 0),
            place(me, XS - ahead, 1),
            place(me, XS - ahead, 0),
            place(me, ahead, 1),
            place(me, 2, 0),
            place(me, 2, 1),
        ]
    )
    pairs = pack(to, query[0], grad_out[0], key[0])
    pieces = across(along(pairs))
    mine = master.astype(BF16)
    theirs = swap_low(mine, "zl")
    both = jnp.where(low == 0, jnp.stack([mine, theirs]), jnp.stack([theirs, mine]))
    both, _ = lax.optimization_barrier((both, pairs[0]))
    copies = jnp.broadcast_to(both[None], (n_far,) + both.shape)
    weight = lax.all_to_all(copies, ("yh", "yl", "zh"), split_axis=0, concat_axis=0, tiled=True)
    weight = weight.reshape(D, HD)
    far = turn(first, 1)
    near = [own, send(own, 0, 1), first, send(first, 0, 1), second, send(second, 0, 1)]
    pieces = [in_hbm(piece) for piece in pieces[:XS]] + pieces[XS:]
    probs, grad_values = probs_call(doc_lens, origin, pieces)
    far, grad_values, weight, near[1], near[3], near[5] = lax.optimization_barrier(
        (far, grad_values, weight, near[1], near[3], near[5])
    )
    hiddens = near + [far, send(far, 0, 1)]
    keep, give = term_call(around, low[None], hiddens, in_hbm(grad_values), rows, 2)
    other = swap_low(give, "zl")
    values = values_call(hiddens, weight)
    keep, give = split_pair(low_y[None], keep, other, lax.axis_size("yh"))
    values, keep, give = lax.optimization_barrier((values, keep, give))
    other = swap_low(give, "yl")
    probs = in_hbm(probs)
    grads = list(grads_call(origin, to, around, pieces, probs, values))
    other, keep, grads[1] = lax.optimization_barrier((other, keep, grads[1]))
    grads = along(grads)
    parts = add_pair(keep, other).reshape((-1,) + master.shape)
    parts = lax.all_to_all(parts, ("yh", "zh"), split_axis=0, concat_axis=0, tiled=True)
    grad_query, grad_key = unpack(origin, across(grads))
    parts, grad_query, grad_key = lax.optimization_barrier((parts, grad_query, grad_key))
    master, m_code, m_scale, v_code, v_scale = adam_call(
        parts, master, m_code, m_scale, v_code, v_scale
    )
    state = (master, m_code, m_scale.T, v_code, v_scale.T)
    return (grad_query[None], grad_key[None]) + state


DP = ("yh", "yl", "zh", "zl")


def solution(mesh):
    tokens, state = P(DP, "seq", None), P(DP, "seq")
    cut = mesh.devices.reshape(mesh.shape["seq"], mesh.shape["dp"] // 16, 2, 4, 2)
    return jax.shard_map(
        shards,
        mesh=Mesh(cut, ("seq",) + DP),
        in_specs=(tokens,) * 4 + (P(DP, None),) + (state,) * 5,
        out_specs=(tokens,) * 2 + (state,) * 5,
        check_vma=False,
    )
```

```python
import functools
import math

import jax
import jax.numpy as jnp
from jax import lax
from jax.experimental import pallas as pl
from jax.experimental.pallas import tpu as pltpu
from jax.sharding import PartitionSpec as P

D = 4096
HD = 128
DOCS = 8
STEP = 1000
SEQ = 1024
GROUP = 4
QW = GROUP * HD
ROWS = 128
BLOCKS = SEQ // ROWS
MOST = 4
NEG = -1e30
INV_WIDTH = 1.0 / math.sqrt(D)
SCALE = 1.0 / math.sqrt(HD)
F32 = jnp.float32
BF16 = jnp.bfloat16


def dot(a, b):
    return jnp.dot(a, b, preferred_element_type=F32)


def stacked(block):
    return jnp.concatenate([block[:, a * HD : (a + 1) * HD] for a in range(GROUP)], axis=0)


def params(mebibytes=24):
    return pltpu.CompilerParams(vmem_limit_bytes=mebibytes * 1024 * 1024)


def cost(microseconds):
    return pl.CostEstimate(
        flops=int(microseconds * 1e9), bytes_accessed=int(microseconds * 1e6), transcendentals=0
    )


XS = 4


def place(value, dx, dc):
    chip = lax.rem(lax.div(value, 2) + dx, XS)
    return chip * 2 + jnp.bitwise_xor(lax.rem(value, 2), dc)


def send(array, dx, dc):
    pairs = [(s, ((s // 2 + dx) % XS) * 2 + ((s % 2) ^ dc)) for s in range(2 * XS)]
    return lax.ppermute(array, "seq", pairs)


def turn(array, dx):
    pairs = [(s, ((s // 2 + (dx if s % 2 == 0 else -dx)) % XS) * 2 + s % 2) for s in range(2 * XS)]
    return lax.ppermute(array, "seq", pairs)


def in_hbm(array):
    return pltpu.with_memory_space_constraint(array, pltpu.HBM)


ANYWHERE = pl.BlockSpec(memory_space=pl.ANY)
SCALARS = pl.BlockSpec(memory_space=pltpu.SMEM)


def run_copies(copies):
    for copy in copies:
        copy.start()
    for copy in copies:
        copy.wait()


def pack_kernel(to_ref, q_ref, c_ref, k_ref, *refs):
    outs, sems = refs[:-1], refs[-1]
    copies = []
    for r in range(8):
        out = outs[r // 2].at[r % 2]
        j = to_ref[r]
        wide = pl.ds(pl.multiple_of(j * QW, QW), QW)
        thin = pl.ds(pl.multiple_of(j * HD, HD), HD)
        for n, (src, lanes, into) in enumerate(
            [
                (q_ref, wide, pl.ds(0, QW)),
                (c_ref, wide, pl.ds(QW, QW)),
                (k_ref, thin, pl.ds(2 * QW, HD)),
            ]
        ):
            copies.append(
                pltpu.make_async_copy(src.at[:, lanes], out.at[:, into], sems.at[3 * r + n])
            )
    run_copies(copies)


def pack(to, query, cot, key):
    tokens = query.shape[0]
    return pl.pallas_call(
        pack_kernel,
        in_specs=[SCALARS] + [pl.BlockSpec(memory_space=pltpu.VMEM)] * 3,
        out_specs=[ANYWHERE] * XS,
        out_shape=[pltpu.HBM((2, tokens, 2 * QW + HD), BF16)] * XS,
        scratch_shapes=[pltpu.SemaphoreType.DMA((24,))],
        cost_estimate=cost(3),
        compiler_params=params(60),
    )(to, query, cot, key)


def merge_kernel(*refs):
    pairs, out, sems = refs[:XS], refs[XS], refs[XS + 1]
    run_copies(
        [pltpu.make_async_copy(pair.at[1], out.at[r], sems.at[r]) for r, pair in enumerate(pairs)]
    )


def merge(pairs):
    return pl.pallas_call(
        merge_kernel,
        in_specs=[ANYWHERE] * XS,
        out_specs=pl.BlockSpec(memory_space=pltpu.VMEM),
        out_shape=jax.ShapeDtypeStruct((XS,) + pairs[0].shape[1:], BF16),
        scratch_shapes=[pltpu.SemaphoreType.DMA((XS,))],
        cost_estimate=cost(1),
        compiler_params=params(8),
    )(*pairs)


def along(pairs):
    return [pairs[0]] + [send(pairs[dx], dx, 0) for dx in range(1, XS)]


def across(got):
    return got + [send(merge(got), 0, 1)]


def arrived(refs):
    return [refs[r // 2].at[0] if r % 2 == 0 else refs[XS].at[r // 2] for r in range(8)]


def gather_pieces(from_ref, piece_refs, whole_ref, sems):
    run_copies(
        [
            pltpu.make_async_copy(
                piece,
                whole_ref.at[pl.ds(pl.multiple_of(from_ref[r] * ROWS, ROWS), ROWS), :],
                sems.at[r],
            )
            for r, piece in enumerate(arrived(piece_refs))
        ]
    )


def by_step(i, body):
    for v in range(BLOCKS // 2):
        pl.when(i == v)(functools.partial(body, v))


def window(block):
    count = min(block + 1, MOST)
    return count, (block + 1 - count) * ROWS


def block_probs(block, lens_ref, r_ref, pt_ref):
    first = block * ROWS
    count, lower = window(block)
    queries = stacked(r_ref[first : first + ROWS, 0:QW])
    lane = lax.broadcasted_iota(jnp.int32, (1, GROUP * ROWS), 1)
    position = first + jnp.bitwise_and(lane, ROWS - 1)
    start = jnp.zeros_like(position)
    end = jnp.int32(0)
    for k in range(DOCS):
        length = lens_ref[0, k]
        end = end + length
        start = start + jnp.where(position >= end, length, 0)
    row = lax.broadcasted_iota(jnp.int32, (ROWS, GROUP * ROWS), 0)
    first_row = start - lower
    last_row = position - lower
    scores = []
    highest = None
    for b in range(count):
        keys = r_ref[lower + b * ROWS : lower + (b + 1) * ROWS, 2 * QW :]
        tile = lax.dot_general(keys, queries, (((1,), (1,)), ((), ())), preferred_element_type=F32)
        allowed = row >= first_row - b * ROWS
        if b == count - 1:
            allowed = allowed & (row <= last_row - b * ROWS)
        tile = jnp.where(allowed, tile, NEG)
        top = jnp.max(tile, axis=0, keepdims=True)
        highest = top if highest is None else jnp.maximum(highest, top)
        scores.append(tile)
    total = None
    weights = []
    for tile in scores:
        weight = jnp.exp2((tile - highest) * (SCALE * math.log2(math.e)))
        part = jnp.sum(weight, axis=0, keepdims=True)
        total = part if total is None else total + part
        weights.append(weight)
    inverse = 1.0 / total
    for b in range(count):
        pt_ref[b * ROWS : (b + 1) * ROWS, :] = (weights[b] * inverse).astype(BF16)


def probs_kernel(lens_ref, from_ref, *refs):
    pieces, (pt_ref, gv_ref, r_ref, acc_ref, sems) = refs[:5], refs[5:]
    i = pl.program_id(0)

    @pl.when(i == 0)
    def _():
        gather_pieces(from_ref, pieces, r_ref, sems)
        acc_ref[...] = jnp.zeros_like(acc_ref)

    def body(v):
        for n, block in enumerate((v, v + MOST)):
            block_probs(block, lens_ref, r_ref, pt_ref.at[0, n])
        for n, block in enumerate((v, v + MOST)):
            count, lower = window(block)
            cot = stacked(r_ref[block * ROWS : (block + 1) * ROWS, QW : 2 * QW])
            size = count * ROWS
            acc_ref[lower : lower + size, :] += dot(pt_ref[0, n, 0:size, :], cot)

    by_step(i, body)

    @pl.when(i == BLOCKS // 2 - 1)
    def _():
        gv_ref[...] = acc_ref[...].astype(BF16)


PROBS_SHAPE = (BLOCKS // 2, 2, MOST * ROWS, GROUP * ROWS)
PROBS_SPEC = pl.BlockSpec((1,) + PROBS_SHAPE[1:], lambda i: (i, 0, 0, 0))


def probs_call(doc_lens, origin, pieces):
    width = 2 * QW + HD
    return pl.pallas_call(
        probs_kernel,
        grid=(BLOCKS // 2,),
        in_specs=[SCALARS, SCALARS] + [ANYWHERE] * 5,
        out_specs=[PROBS_SPEC, pl.BlockSpec((SEQ, HD), lambda i: (0, 0))],
        out_shape=[
            pltpu.HBM(PROBS_SHAPE, BF16),
            pltpu.HBM((SEQ, HD), BF16),
        ],
        scratch_shapes=[
            pltpu.VMEM((SEQ, width), BF16),
            pltpu.VMEM((SEQ, HD), F32),
            pltpu.SemaphoreType.DMA((8,)),
        ],
        cost_estimate=cost(8),
        compiler_params=params(),
    )(doc_lens, origin, *pieces)


def join(refs):
    return jnp.concatenate([ref[...] for ref in refs], axis=0)


def term_kernel(from_ref, *refs):
    hidden_refs, (gv_ref, term_ref, gvt_ref) = refs[:8], refs[8:]

    @pl.when(pl.program_id(0) == 0)
    def _():
        for r in range(8):
            rows = pl.ds(pl.multiple_of(from_ref[r] * ROWS, ROWS), ROWS)
            gvt_ref[:, r * ROWS : (r + 1) * ROWS] = gv_ref[rows, :].T

    term = dot(gvt_ref[...], join(hidden_refs))
    term_ref[...] = (term.T * INV_WIDTH).astype(BF16)


def values_kernel(*refs):
    hidden_refs, (w_ref, val_ref, acc_ref) = refs[:-3], refs[-3:]
    j = pl.program_id(0)

    @pl.when(j == 0)
    def _():
        acc_ref[...] = jnp.zeros_like(acc_ref)

    acc_ref[...] += dot(join(hidden_refs), w_ref[...])

    @pl.when(j == pl.num_programs(0) - 1)
    def _():
        val_ref[...] = (acc_ref[...] * INV_WIDTH).astype(BF16)


STRIPE = 1024


def hidden_specs(pieces):
    return [pl.BlockSpec((piece.shape[0], STRIPE), lambda j: (0, j)) for piece in pieces]


def term_call(origin, pieces, grad_values):
    return pl.pallas_call(
        term_kernel,
        grid=(D // STRIPE,),
        in_specs=[SCALARS]
        + hidden_specs(pieces)
        + [pl.BlockSpec((SEQ, HD), lambda j: (0, 0))],
        out_specs=pl.BlockSpec((STRIPE, HD), lambda j: (j, 0)),
        out_shape=pltpu.HBM((D, HD), BF16),
        scratch_shapes=[pltpu.VMEM((HD, SEQ), BF16)],
        cost_estimate=cost(5),
        compiler_params=params(),
    )(origin, *pieces, grad_values)


def values_call(pieces, weight):
    rows = sum(piece.shape[0] for piece in pieces)
    return pl.pallas_call(
        values_kernel,
        grid=(D // STRIPE,),
        in_specs=hidden_specs(pieces) + [pl.BlockSpec((STRIPE, HD), lambda j: (j, 0))],
        out_specs=pl.BlockSpec((rows, HD), lambda j: (0, 0)),
        out_shape=jax.ShapeDtypeStruct((rows, HD), BF16),
        scratch_shapes=[pltpu.VMEM((rows, HD), F32)],
        cost_estimate=cost(rows * 6 // SEQ),
        compiler_params=params(),
    )(*pieces, weight)


def block_grads(block, r_ref, pt_ref, val_ref, out_ref, acc_ref, kt_ref, vt_ref):
    first = block * ROWS
    count, lower = window(block)
    size = count * ROWS
    queries = stacked(r_ref[first : first + ROWS, 0:QW])
    cot_t = stacked(r_ref[first : first + ROWS, QW : 2 * QW]).T
    attn_t = dot(vt_ref[:, lower : lower + size], pt_ref[0:size, :]).astype(BF16)
    delta = jnp.sum(attn_t.astype(F32) * cot_t.astype(F32), axis=0, keepdims=True)
    prob_grad = dot(val_ref[lower : lower + size, :], cot_t)
    probs = pt_ref[0:size, :].astype(F32)
    score_grad = (probs * (prob_grad - delta)).astype(BF16)
    acc_ref[lower : lower + size, :] += dot(score_grad, queries)
    grad_t = dot(kt_ref[:, lower : lower + size], score_grad) * SCALE
    grad = grad_t.T.astype(BF16)
    for a in range(GROUP):
        out_ref[first : first + ROWS, a * HD : (a + 1) * HD] = grad[a * ROWS : (a + 1) * ROWS, :]


def grads_kernel(from_ref, to_ref, around_ref, *refs):
    pieces, (pt_ref, held_ref), outs = refs[:5], refs[5:7], refs[7 : 7 + XS]
    r_ref, val_ref, out_ref, acc_ref, kt_ref, vt_ref, sems = refs[7 + XS :]
    i = pl.program_id(0)

    @pl.when(i == 0)
    def _():
        gather_pieces(from_ref, pieces, r_ref, sems)
        acc_ref[...] = jnp.zeros_like(acc_ref)
        kt_ref[...] = r_ref[:, 2 * QW :].T
        for r in range(8):
            rows = pl.ds(pl.multiple_of(around_ref[r] * ROWS, ROWS), ROWS)
            val_ref[rows, :] = held_ref[r * ROWS : (r + 1) * ROWS, :]
        vt_ref[...] = val_ref[...].T

    def body(v):
        for n, block in enumerate((v, v + MOST)):
            block_grads(block, r_ref, pt_ref.at[0, n], val_ref, out_ref, acc_ref, kt_ref, vt_ref)

    by_step(i, body)

    @pl.when(i == BLOCKS // 2 - 1)
    def _():
        out_ref[:, QW:] = (acc_ref[...] * SCALE).astype(BF16)
        run_copies(
            [
                pltpu.make_async_copy(
                    out_ref.at[pl.ds(pl.multiple_of(to_ref[r] * ROWS, ROWS), ROWS), :],
                    outs[r // 2].at[r % 2],
                    sems.at[r],
                )
                for r in range(8)
            ]
        )


def grads_call(origin, to, around, pieces, probs, values):
    width = 2 * QW + HD
    return pl.pallas_call(
        grads_kernel,
        grid=(BLOCKS // 2,),
        in_specs=[SCALARS, SCALARS, SCALARS]
        + [ANYWHERE] * 5
        + [
            PROBS_SPEC,
            pl.BlockSpec((SEQ, HD), lambda i: (0, 0)),
        ],
        out_specs=[ANYWHERE] * XS,
        out_shape=[pltpu.HBM((2, ROWS, QW + HD), BF16)] * XS,
        scratch_shapes=[
            pltpu.VMEM((SEQ, width), BF16),
            pltpu.VMEM((SEQ, HD), BF16),
            pltpu.VMEM((SEQ, QW + HD), BF16),
            pltpu.VMEM((SEQ, HD), F32),
            pltpu.VMEM((HD, SEQ), BF16),
            pltpu.VMEM((HD, SEQ), BF16),
            pltpu.SemaphoreType.DMA((8,)),
        ],
        cost_estimate=cost(9),
        compiler_params=params(),
    )(origin, to, around, *pieces, probs, values)


def unpack_kernel(from_ref, *refs):
    pieces, (q_ref, k_ref, sems) = refs[:5], refs[5:]
    copies = []
    for r, piece in enumerate(arrived(pieces)):
        j = from_ref[r]
        wide = pl.ds(pl.multiple_of(j * QW, QW), QW)
        thin = pl.ds(pl.multiple_of(j * HD, HD), HD)
        copies.append(
            pltpu.make_async_copy(piece.at[:, pl.ds(0, QW)], q_ref.at[:, wide], sems.at[2 * r])
        )
        copies.append(
            pltpu.make_async_copy(piece.at[:, pl.ds(QW, HD)], k_ref.at[:, thin], sems.at[2 * r + 1])
        )
    run_copies(copies)


def unpack(origin, pieces):
    return pl.pallas_call(
        unpack_kernel,
        in_specs=[SCALARS] + [pl.BlockSpec(memory_space=pltpu.VMEM)] * 5,
        out_specs=[ANYWHERE] * 2,
        out_shape=[
            jax.ShapeDtypeStruct((ROWS, 8 * QW), BF16),
            jax.ShapeDtypeStruct((ROWS, 8 * HD), BF16),
        ],
        scratch_shapes=[pltpu.SemaphoreType.DMA((16,))],
        cost_estimate=cost(2),
        compiler_params=params(8),
    )(origin, *pieces)


def adam_kernel(
    parts_ref,
    master_ref,
    mc_ref,
    ms_ref,
    vc_ref,
    vs_ref,
    master_out,
    mc_out,
    ms_out,
    vc_out,
    vs_out,
    grad_ref,
    mold_ref,
    vold_ref,
    step_ref,
    mcode_ref,
    vcode_ref,
):
    total = jnp.zeros(grad_ref.shape, F32)
    for g in range(parts_ref.shape[0]):
        total = total + parts_ref[g].astype(F32)
    grad_ref[...] = total
    mold_ref[...] = mc_ref[...].astype(F32)
    vold_ref[...] = vc_ref[...].astype(F32)
    half = grad_ref.shape[0] // 2
    first_fix = 1.0 - 0.9**STEP
    second_fix = 1.0 - 0.999**STEP
    news = []
    for odd in range(2):
        rows = pl.ds(odd, half, stride=2)
        grad = grad_ref[rows, :]
        m_new = 0.9 * (mold_ref[rows, :] * ms_ref[...]) + 0.1 * grad
        v_new = 0.999 * (vold_ref[rows, :] * vs_ref[...]) + 0.001 * grad * grad
        step_ref[rows, :] = m_new / first_fix / (jnp.sqrt(v_new / second_fix) + 1e-08)
        news.append((m_new, v_new))
    m_top = jnp.maximum(
        jnp.max(jnp.abs(news[0][0]), axis=1, keepdims=True),
        jnp.max(jnp.abs(news[1][0]), axis=1, keepdims=True),
    )
    v_top = jnp.maximum(
        jnp.max(jnp.abs(news[0][1]), axis=1, keepdims=True),
        jnp.max(jnp.abs(news[1][1]), axis=1, keepdims=True),
    )
    ms_out[...] = jnp.broadcast_to(m_top, (half, HD)).T[0:1, :]
    vs_out[...] = jnp.broadcast_to(v_top, (half, HD)).T[0:1, :]
    for odd in range(2):
        rows = pl.ds(odd, half, stride=2)
        mcode_ref[rows, :] = news[odd][0] / (m_top + 1e-06)
        vcode_ref[rows, :] = news[odd][1] / (v_top + 1e-06)
    mc_out[...] = mcode_ref[...].astype(BF16)
    vc_out[...] = vcode_ref[...].astype(BF16)
    master_out[...] = master_ref[...] - 0.01 * step_ref[...]


def adam_call(parts, master, m_code, m_scale, v_code, v_scale):
    shape = master.shape
    return pl.pallas_call(
        adam_kernel,
        out_shape=[
            jax.ShapeDtypeStruct(shape, F32),
            jax.ShapeDtypeStruct(shape, BF16),
            jax.ShapeDtypeStruct(m_scale.shape[::-1], F32),
            jax.ShapeDtypeStruct(shape, BF16),
            jax.ShapeDtypeStruct(v_scale.shape[::-1], F32),
        ],
        scratch_shapes=[pltpu.VMEM(shape, F32) for _ in range(6)],
        cost_estimate=cost(2),
        compiler_params=params(16),
    )(parts, master, m_code, m_scale, v_code, v_scale)


def shards(hidden, query, key, grad_out, doc_lens, master, m_code, m_scale, v_code, v_scale):
    n_dp = lax.axis_size("dp")
    me = lax.axis_index("seq")
    to = jnp.stack([place(me, r // 2, r % 2) for r in range(8)])
    origin = jnp.stack([place(me, (XS - r // 2) % XS, r % 2) for r in range(8)])
    around = jnp.stack([place(me, dx, dc) for dx in (0, 3, 1, 2) for dc in (0, 1)])
    core = lax.rem(me, 2)
    ahead = jnp.where(core == 0, XS - 1, 1)
    own = in_hbm(hidden[0])
    first, second = turn(own, 1), turn(own, -1)
    around = jnp.stack(
        [
            me,
            place(me, 0, 1),
            place(me, ahead, 0),
            place(me, XS - ahead, 1),
            place(me, XS - ahead, 0),
            place(me, ahead, 1),
            place(me, 2, 0),
            place(me, 2, 1),
        ]
    )
    pairs = pack(to, query[0], grad_out[0], key[0])
    pieces = across(along(pairs))
    mine, _ = lax.optimization_barrier((master.astype(BF16), pairs[0]))
    copies = jnp.broadcast_to(mine[None], (n_dp,) + master.shape)
    weight = lax.all_to_all(copies, "dp", split_axis=0, concat_axis=0, tiled=True)
    weight = weight.reshape(D, HD)
    far = turn(first, 1)
    near = [own, send(own, 0, 1), first, send(first, 0, 1), second, send(second, 0, 1)]
    pieces = [in_hbm(piece) for piece in pieces[:XS]] + pieces[XS:]
    probs, grad_values = probs_call(doc_lens, origin, pieces)
    far, grad_values, weight, near[1], near[3], near[5] = lax.optimization_barrier(
        (far, grad_values, weight, near[1], near[3], near[5])
    )
    hiddens = near + [far, send(far, 0, 1)]
    term = term_call(around, hiddens, in_hbm(grad_values))
    parts = lax.all_to_all(
        term.reshape((n_dp,) + master.shape), "dp", split_axis=0, concat_axis=0, tiled=True
    )
    values = values_call(hiddens, weight)
    probs = in_hbm(probs)
    grads = along(grads_call(origin, to, around, pieces, probs, values))
    grad_query, grad_key = unpack(origin, across(grads))
    master, m_code, m_scale, v_code, v_scale = adam_call(
        parts, master, m_code, m_scale, v_code, v_scale
    )
    state = (master, m_code, m_scale.T, v_code, v_scale.T)
    return (grad_query[None], grad_key[None]) + state


def solution(mesh):
    tokens, state = P("dp", "seq", None), P("dp", "seq")
    return jax.shard_map(
        shards,
        mesh=mesh,
        in_specs=(tokens,) * 4 + (P("dp", None),) + (state,) * 5,
        out_specs=(tokens,) * 2 + (state,) * 5,
        check_vma=False,
    )
```
